32 devices in a mesh: grp: 2 (over y), row: 8 (over z, x), col: 2 (over core).
Axes of the slice: x: 2, y: 2, z: 4, core: 2. Of those that a mesh axis runs over, the one named last changes fastest.
Arguments:
- tokens: bfloat16 [128, 256, 180], P(('grp', 'row'), 'col'), parts along dimension 0, may hold values from -6 to 6
- grad_out: bfloat16 [128, 256, 180], P(('grp', 'row'), 'col'), parts along dimension 0, may hold values from -8 to 8
- regions: int32 [128, 256], P(('grp', 'row'), 'col'), parts along dimension 0, may hold values from 0 to 15, as said below
- ln_gain: float32 [180], replicated, may hold values from 0.1 to 1.9
- ln_offset: float32 [180], replicated, may hold values from -1.5 to 1.5
- qkv_weight: bfloat16 [180, 540], replicated, may hold values from -0.4375 to 0.4375
- qkv_bias: float32 [540], replicated, may hold values from -1.5 to 1.5
- proj_weight: bfloat16 [180, 180], replicated, may hold values from -0.4375 to 0.4375
- bias_table: float32 [225, 6], replicated, may hold values from -4 to 320
Outputs:
- d_tokens: bfloat16 [128, 256, 180], P(('grp', 'row'), 'col'), parts along dimension 0
- d_qkv_weight: float32 [360, 540], P('grp'), parts along dimension 0
- d_qkv_bias: float32 [1080], P('grp'), parts along dimension 0
- d_proj_weight: float32 [360, 180], P('grp'), parts along dimension 0
- d_bias_table: float32 [450, 6], P('grp'), parts along dimension 0
- d_ln_gain: float32 [360], P('grp'), parts along dimension 0
- d_ln_offset: float32 [360], P('grp'), parts along dimension 0
The draws below stay inside these ranges and needn't reach their ends.
There are 2 independent parts, one for each index of `grp`. The reference program is written for one: setup_inputs(seed, part) draws one part's arguments, and reference() takes and returns one part's arrays. A program takes and returns all parts, laid end to end along the dimension named above; an argument that names none is the same for every part. Nothing has to cross between parts.
Inputs may be any that keep to these rules, and one draw needn't show every extreme that they name: `regions`: A token attends only to tokens of its window with the same id. The map is a grid: the id is 4 a + b, where a, from 0 to 3, depends only on the token's row and b, from 0 to 3, only on its column.
All inputs are finite; a program needn't handle non-finite values.
Results may differ from the reference program's by a relative error of at most 0.0085.
Values may be sent and summed in bfloat16 or wider, within the bound.
A program may use at most 64 MiB of HBM per device.

```python
import jax
import jax.numpy as jnp
from jax import lax

C = 180
HEADS = 6
WIN = 8
SHIFT = 4
TABLE = 225
H = 64
W = 256


def draw_grad_out(key, part):
    key_one = jax.random.fold_in(key, 0)
    noise = jax.random.normal(key_one, (H, W, C), jnp.float32)
    values = noise
    return jnp.clip(values, -8.0, 8.0).astype(jnp.bfloat16)


def draw_regions(key, part):
    row_key, col_key = jax.random.split(key)
    row_flag = (jax.random.randint(row_key, (H,), 0, 16) == 0).astype(jnp.int32)
    row_flag = row_flag.at[0].set(0).at[1:4].set(1)
    col_flag = (jax.random.randint(col_key, (W,), 0, 16) == 0).astype(jnp.int32)
    col_flag = col_flag.at[0].set(0).at[1:4].set(1)
    row_band = jnp.cumsum(row_flag) % 4
    col_band = jnp.cumsum(col_flag) % 4
    return (row_band[:, None] * 4 + col_band[None, :]).astype(jnp.int32)


def draw_bias_table(key, part):
    values = jnp.clip(jax.random.normal(key, (TABLE, HEADS), jnp.float32), -4.0, 4.0)
    return values


def level_of(rng, dims, shards, smallest, top_value):
    def one(dim, shards_of):
        steps = jax.random.uniform(jax.random.fold_in(jax.random.fold_in(rng, 6), dim), (shards_of,), jnp.float32, smallest / len(shards), top_value / len(shards))
        return jnp.repeat(jnp.exp(steps), dims[dim] // shards_of).reshape((-1,) + (1,) * (len(dims) - dim - 1))

    factor_of = one(*shards[0])
    for cut in shards[1:]:
        factor_of = factor_of * one(*cut)
    return factor_of


def normal_values(own_key, extent, scale, reach, shards=(), kind=jnp.bfloat16):
    gain = level_of(own_key, extent, shards, -0.22, 0.18) if shards else 1.0
    entries = jax.random.normal(own_key, extent, jnp.float32) * scale * gain
    return jnp.minimum(jnp.maximum(entries, -reach), reach).astype(kind)


def setup_inputs(seed: int = 0, part: int = 0) -> dict:
    arg_keys = jax.random.split(jax.random.key(seed), 10)
    own_keys = jax.random.split(jax.random.fold_in(arg_keys[9], part), 10)
    return {
        "tokens": normal_values(own_keys[0], (H, W, C), 1.0, 6.0, ((0, 8), (1, 2))),
        "grad_out": draw_grad_out(jax.random.fold_in(jax.random.fold_in(arg_keys[9], part), 71), part),
        "regions": draw_regions(jax.random.fold_in(jax.random.fold_in(arg_keys[9], part), 71), part),
        "ln_gain": jnp.clip(1.0 + 0.18 * jax.random.normal(arg_keys[3], (C,), jnp.float32), 0.1, 1.9),
        "ln_offset": normal_values(arg_keys[4], (C,), 0.3, 1.5, (), jnp.float32),
        "qkv_weight": normal_values(arg_keys[5], (C, 3 * C), C ** -0.5, 0.4375),
        "qkv_bias": normal_values(arg_keys[6], (3 * C,), 0.3, 1.5, (), jnp.float32),
        "proj_weight": normal_values(arg_keys[7], (C, C), C ** -0.5, 0.4375),
        "bias_table": draw_bias_table(jax.random.fold_in(arg_keys[9], 71), part),
    }


masked_score = -10000.0

def multiply(form, left, right):
    return jnp.einsum(form, left.astype(jnp.float32), right.astype(jnp.float32))

def relative_onehot(table_rows):
    span_size = WIN * WIN
    position = jnp.arange(span_size, dtype=jnp.int32)
    row_pos = position // WIN
    col_pos = position % WIN
    entry_index = (row_pos[:, None] - row_pos[None, :] + WIN - 1) * (2 * WIN - 1) + col_pos[:, None] - col_pos[None, :] + WIN - 1
    return (entry_index.reshape(-1)[:, None] == jnp.arange(table_rows, dtype=jnp.int32)[None, :]).astype(jnp.float32)

def normalize(values, gain_vec, offset_vec):
    as_float = values.astype(jnp.float32)
    center = lax.optimization_barrier(jnp.mean(as_float, -1, keepdims=True))
    variance = lax.optimization_barrier(jnp.mean(jnp.square(as_float - center), -1, keepdims=True))
    inv_std = lax.rsqrt(variance + 1e-05)
    unit_tokens = (as_float - center) * inv_std
    normed = (unit_tokens * gain_vec + offset_vec).astype(jnp.bfloat16)
    return (normed, unit_tokens, inv_std)

def project(normed, weights, offsets):
    channels = normed.shape[-1]
    summed = multiply('rcd,df->rcf', normed, weights) + offsets
    factor = jnp.where(jnp.arange(3 * channels) < channels, (channels // HEADS) ** (-0.5), 1.0)
    return (summed * factor).astype(jnp.bfloat16)

def window_band(qkv, grad_band, label_band, rel_bias, proj_weight):
    channels = grad_band.shape[-1]
    head_count = rel_bias.shape[0]
    head_size = channels // head_count
    tile_cols = grad_band.shape[1]
    win_count = tile_cols // WIN
    span_size = WIN * WIN

    def windows(array):
        array = array.reshape((WIN, win_count, WIN) + array.shape[2:])
        array = jnp.moveaxis(array, 1, 0)
        return array.reshape((win_count, span_size) + array.shape[3:])

    def unwindow(array):
        array = array.reshape((win_count, WIN, WIN) + array.shape[2:])
        array = jnp.moveaxis(array, 0, 1)
        return array.reshape((WIN, tile_cols) + array.shape[3:])
    parted = windows(qkv).reshape(win_count, span_size, 3, head_count, head_size)
    query_part = parted[:, :, 0]
    key_part = parted[:, :, 1]
    value_part = parted[:, :, 2]
    grad_win = windows(grad_band)
    label_win = windows(label_band)
    matched = label_win[:, :, None] == label_win[:, None, :]
    scores = multiply('nihd,njhd->nhij', query_part, key_part) + rel_bias[None]
    scores = jnp.where(matched[:, None], scores, masked_score)
    probability = jax.nn.softmax(scores, axis=-1)
    prob_low = probability.astype(jnp.bfloat16)
    attended = multiply('nhij,njhd->nihd', prob_low, value_part).astype(jnp.bfloat16).reshape(win_count * span_size, channels)
    flat_grad = grad_win.reshape(win_count * span_size, channels)
    d_proj = multiply('tc,td->cd', attended, flat_grad)
    d_attended = multiply('td,cd->tc', flat_grad, proj_weight).astype(jnp.bfloat16).reshape(win_count, span_size, head_count, head_size)
    d_prob = multiply('nihd,njhd->nhij', d_attended, value_part)
    d_scores = probability * (d_prob - lax.optimization_barrier(jnp.sum(probability * d_prob, -1, keepdims=True)))
    score_sum = lax.optimization_barrier(jnp.sum(d_scores, 0))
    d_score_low = d_scores.astype(jnp.bfloat16)
    d_query = multiply('nhij,njhd->nihd', d_score_low, key_part) * head_size ** (-0.5)
    d_key = multiply('nhij,nihd->njhd', d_score_low, query_part)
    d_value = multiply('nhij,nihd->njhd', prob_low, d_attended)
    d_qkv = jnp.stack([d_query, d_key, d_value], 2).astype(jnp.bfloat16).reshape(win_count, span_size, 3 * channels)
    return (unwindow(d_qkv), d_proj, score_sum)

def input_backward(d_qkv, normed, unit_tokens, inv_std, gain_vec, qkv_weight):
    d_weight = multiply('rcd,rcf->df', normed, d_qkv)
    d_offsets = lax.optimization_barrier(jnp.sum(d_qkv.astype(jnp.float32), (0, 1)))
    d_normed = multiply('rcf,df->rcd', d_qkv, qkv_weight)
    d_gain = lax.optimization_barrier(jnp.sum(d_normed * unit_tokens, (0, 1)))
    d_offset = lax.optimization_barrier(jnp.sum(d_normed, (0, 1)))
    scaled_grad = d_normed * gain_vec
    d_input = inv_std * (scaled_grad - lax.optimization_barrier(jnp.mean(scaled_grad, -1, keepdims=True)) - unit_tokens * lax.optimization_barrier(jnp.mean(scaled_grad * unit_tokens, -1, keepdims=True)))
    return (d_input, d_weight, d_offsets, d_gain, d_offset)

def reference(tokens, grad_out, regions, ln_gain, ln_offset, qkv_weight, qkv_bias, proj_weight, bias_table):
    shifted = jnp.roll(tokens, (-SHIFT, -SHIFT), (0, 1))
    grad_shifted = jnp.roll(grad_out, (-SHIFT, -SHIFT), (0, 1))
    labels = jnp.roll(regions, (-SHIFT, -SHIFT), (0, 1))
    entry_table = relative_onehot(bias_table.shape[0])
    rel_bias = jnp.dot(entry_table, bias_table, precision=lax.Precision.HIGHEST).reshape(WIN * WIN, WIN * WIN, HEADS).transpose(2, 0, 1)
    band_count = H // WIN

    def to_bands(array):
        return array.reshape((band_count, WIN) + array.shape[1:])

    def band_step(running, pieces):
        normed, unit_tokens, inv_std = normalize(pieces[0], ln_gain, ln_offset)
        qkv = project(normed, qkv_weight, qkv_bias)
        d_qkv, d_proj, score_sum = window_band(qkv, pieces[1], pieces[2], rel_bias, proj_weight)
        d_input, d_weight, d_offsets, d_gain, d_offset = input_backward(d_qkv, normed, unit_tokens, inv_std, ln_gain, qkv_weight)
        added = (d_proj, score_sum, d_weight, d_offsets, d_gain, d_offset)
        return (tuple((before + extra for before, extra in zip(running, added))), d_input)
    initial = (jnp.zeros((C, C), jnp.float32), jnp.zeros((HEADS, WIN * WIN, WIN * WIN), jnp.float32), jnp.zeros((C, 3 * C), jnp.float32), jnp.zeros((3 * C,), jnp.float32), jnp.zeros((C,), jnp.float32), jnp.zeros((C,), jnp.float32))
    totals, d_shifted = lax.scan(band_step, initial, (to_bands(shifted), to_bands(grad_shifted), to_bands(labels)))
    d_shifted = d_shifted.reshape(H, W, C)
    d_tokens = (grad_out.astype(jnp.float32) + jnp.roll(d_shifted, (SHIFT, SHIFT), (0, 1))).astype(jnp.bfloat16)
    out_scale = (H * W) ** (-0.5)
    d_table = jnp.dot(entry_table.T, jnp.transpose(totals[1], (1, 2, 0)).reshape(-1, HEADS), precision=lax.Precision.HIGHEST)
    return (d_tokens, totals[2] * out_scale, totals[3] * out_scale, totals[0] * out_scale, d_table * out_scale, totals[4] * out_scale, totals[5] * out_scale)
```

```python
import functools

import jax
import jax.numpy as jnp
from jax import lax
from jax.experimental import pallas as pl
from jax.experimental.pallas import tpu as pltpu
from jax.sharding import PartitionSpec as P

HEADS = 6
WIN = 8
SHIFT = 4
SPAN = WIN * WIN
C = 180
HEAD = C // HEADS
LANES = HEADS * SPAN
BLOCK = 192
LANE = 128
WIDE = 2 * LANE
HEADW = 32
EDGE = 16
MASKED = -10000.0
MESH = pl.DeviceIdType.MESH
F32 = jnp.float32
BF16 = jnp.bfloat16

NN = (((1,), (0,)), ((), ()))
NT = (((1,), (1,)), ((), ()))
TN = (((0,), (0,)), ((), ()))


def mul(left, right, form=NN):
    return lax.dot_general(left, right, form, preferred_element_type=F32)


def exact(left, right, form=NN):
    return lax.dot_general(
        left, right, form, preferred_element_type=F32, precision=lax.Precision.HIGHEST
    )


def split_mul(left, picks):
    high = left.astype(BF16)
    low = (left - high.astype(F32)).astype(BF16)
    return mul(high, picks) + mul(low, picks)


def iota(shape, dim):
    return lax.broadcasted_iota(jnp.int32, shape, dim)


def col_spread(cj):
    src = iota((SPAN, 128), 0)
    dst = iota((SPAN, 128), 1)
    return (dst == (src >> 3) * 16 + (src & 7) - cj + 7).astype(F32)


def row_spread(rj):
    src = iota((128, 256), 0)
    dst = iota((128, 256), 1)
    return (dst == src + 16 * (7 - rj)).astype(F32)


def table_spread(entries):
    src = iota((entries, 256), 0)
    dst = iota((entries, 256), 1)
    hit = (src == (dst >> 4) * 15 + (dst & 15)) & ((dst & 15) < 15) & (dst < 240)
    return hit.astype(F32)


def head_spread():
    src = iota((C, WIDE), 0)
    lane = iota((1, WIDE), 1)
    head, place = lane >> 5, lane & (HEADW - 1)
    wanted = jnp.where((place < HEAD) & (head < HEADS), head * HEAD + place, -1)
    return (src == wanted).astype(F32).astype(BF16)


def part_pick():
    lane = iota((1, 3 * C), 1)
    part = (lane >= C).astype(jnp.int32) + (lane >= 2 * C).astype(jnp.int32)
    place = lane - part * C
    head = sum((place >= t * HEAD).astype(jnp.int32) for t in range(1, HEADS))
    place = place - head * HEAD
    near = part * LANE + head * HEADW + place
    far = 3 * LANE + (part >> 1) * LANE + (part & 1) * 64 + (head - 4) * HEADW + place
    wanted = jnp.where(head < 4, near, far)
    return (iota((5 * LANE, 3 * C), 0) == wanted).astype(F32).astype(BF16)


def body(
    rows_n, cols_n, rows_total, out_scale,
    both, reg, gain_ref, offset_ref, qkvw, qkvb, projw, table,
    d_tok, d_qkvw, d_qkvb, d_projw, d_table, d_gain, d_offset,
    both_b, both_r, both_d, reg_b, reg_r,
    unit, inv_std, gradf, nt_s, q_s, k_s, v_s, da_s, gb_s, att, dq_s, dk_s, dv_s,
    w_s, b_s, pw_s, e_s, pick_s, bias_t, span_a, span_b, hmask, lab_col, lab_row, score_acc, sums,
    fold_a, fold_b, frame_low, frame_two, back_u, back_l, back_ul,
    pack, pack_low, pair_in, half_low, part_in, result,
    halo_send, halo_recv, back_send, back_recv, pair_sem,
    part_send, part_recv, all_send, all_recv, fwd_send, fwd_recv,
):
    row = lax.axis_index("row")
    col = lax.axis_index("col")
    up = lax.rem(row + rows_n - 1, rows_n)
    down = lax.rem(row + 1, rows_n)
    other = lax.rem(col + 1, cols_n)
    tile_cols = both.shape[1]
    wins = tile_cols // WIN
    count = wins * SPAN
    half = rows_total // 2
    chunk = half // rows_n

    def remote(src, dst, send, recv, to_row, to_col):
        return pltpu.make_async_remote_copy(
            src_ref=src, dst_ref=dst, send_sem=send, recv_sem=recv,
            device_id={"row": to_row, "col": to_col}, device_id_type=MESH,
        )

    barrier = pltpu.get_barrier_semaphore()

    @pl.loop(1, rows_n)
    def _(k):
        pl.semaphore_signal(
            barrier, inc=1, device_id={"row": lax.rem(row + k, rows_n), "col": col},
            device_id_type=MESH,
        )

    for to_row in (row, up, down):
        pl.semaphore_signal(
            barrier, inc=1, device_id={"row": to_row, "col": other}, device_id_type=MESH
        )
    pl.semaphore_wait(barrier, rows_n + 2)

    step_wins = 4
    step = step_wins * SPAN
    steps = wins // step_wins
    span_cols = step_wins * WIN

    def halo(i, src, dst, to_row, to_col):
        return remote(src, dst, halo_send.at[i], halo_recv.at[i], to_row, to_col)

    labels = [halo(0, reg, reg_b, up, col), halo(1, reg, reg_r, row, other)]
    sides = [
        halo(2, both.at[SHIFT:WIN, 0:EDGE], both_r, row, other),
        halo(3, both.at[0:SHIFT, 0:EDGE], both_d, up, other),
    ]
    chunks = []
    for b in range(steps):
        first = b * span_cols + (EDGE if b else 0)
        last = min((b + 1) * span_cols + EDGE, tile_cols)
        src, dst = both.at[0:SHIFT, first:last], both_b.at[0:SHIFT, first:last]
        chunks.append([halo(4 + b, src, dst, up, col)])
    small = 6 * BLOCK
    for copy in labels + chunks[0] + sides + chunks[1]:
        copy.start()

    flat = exact(table[...], table_spread(table.shape[1]))
    for rj in range(WIN):
        span_b[pl.ds(rj, HEADS, stride=WIN), :] = exact(flat, row_spread(rj), NT)
    for cj in range(WIN):
        span_a[pl.ds(cj, HEADS * WIN, stride=WIN), :] = exact(span_b[...], col_spread(cj), NT)
    for h in range(HEADS):
        bias_t[:, h * SPAN : (h + 1) * SPAN] = span_a[h * SPAN : (h + 1) * SPAN, :]
    mask_row = iota((4 * 16, LANE), 0) >> 4
    hmask[...] = ((iota((4 * 16, LANE), 1) >> 5) == mask_row).astype(F32).astype(BF16)
    e_s[...] = head_spread()
    pick_s[...] = part_pick()
    score_acc[...] = jnp.zeros_like(score_acc)
    sums[...] = jnp.zeros_like(sums)
    pack[small:] = jnp.zeros_like(pack[small:])

    nt_s[...] = jnp.ones_like(nt_s)
    for cj in range(WIN):
        fold_a[cj * SPAN : (cj + 1) * SPAN, :] = col_spread(cj).astype(BF16)
    for rj in range(WIN):
        fold_b[rj * 128 : (rj + 1) * 128, :] = row_spread(rj).astype(BF16)
    weights = qkvw[...]
    offsets = qkvb[...]
    for i in range(3):
        w_s[i] = mul(weights[:, i * C : (i + 1) * C], e_s[...]).astype(BF16)
        b_s[i] = exact(offsets[:, i * C : (i + 1) * C], e_s[...].astype(F32))
    pw_s[...] = mul(e_s[...], projw[...], TN).astype(BF16)

    for copy in labels:
        copy.wait()

    own = reg[...]
    row_part = jnp.concatenate([own[SHIFT:], reg_b[0:SHIFT, :]], 0)[:, 0:1] >> 2
    col_own = pltpu.roll(own, tile_cols - SHIFT, 1)
    col_right = pltpu.roll(reg_r[...], tile_cols - SHIFT, 1)
    col_part = jnp.where(iota((WIN, tile_cols), 1) < tile_cols - SHIFT, col_own, col_right)[0:1] & 3
    label = (row_part * 4 + col_part).astype(F32)
    spread = jnp.broadcast_to(label[:, None, :], (WIN, WIN, tile_cols)).reshape(SPAN, tile_cols)
    spread = jnp.where(
        (iota((SPAN, tile_cols), 0) & 7) == (iota((SPAN, tile_cols), 1) & 7), spread, 0.0
    )
    pick = ((iota((tile_cols, wins), 0) >> 3) == iota((tile_cols, wins), 1)).astype(F32)
    columns = exact(spread, pick)
    tiled = (iota((SPAN, LANE), 0) == (iota((SPAN, LANE), 1) & (SPAN - 1))).astype(F32)
    lab_row[...] = exact(columns, tiled, TN)
    for w in range(wins):
        lab_col[w] = jnp.broadcast_to(columns[:, w : w + 1], (SPAN, 128))

    lane = iota((SPAN, LANE), 1)

    def gather_heads(stacked):
        out = stacked[-SPAN:]
        for h in range(stacked.shape[0] // SPAN - 2, -1, -1):
            out = jnp.where(lane < (h + 1) * HEADW, stacked[h * SPAN : (h + 1) * SPAN], out)
        return out

    def diagonal(x, heads):
        tiles = x.reshape(SPAN // 16, 16, LANE)
        parts = [
            (tiles * hmask[h * 16 : (h + 1) * 16, :][None]).reshape(SPAN, LANE) for h in range(heads)
        ]
        return jnp.concatenate(parts, 0)

    edge = tile_cols - EDGE
    backs = []

    def back(src, dst, to_row, to_col):
        i = len(backs)
        backs.append(remote(src, dst, back_send.at[i], back_recv.at[i], to_row, to_col))
        backs[-1].start()

    for b in range(steps):
        for copy in chunks[b] + (sides if b == steps - 1 else []):
            copy.wait()
        if b + 2 < steps:
            for copy in chunks[b + 2]:
                copy.start()
        at = slice(b * step, (b + 1) * step)
        win_at = slice(b * step_wins, (b + 1) * step_wins)
        cols = slice(b * span_cols, (b + 1) * span_cols)
        near = slice(b * span_cols, min((b + 1) * span_cols + EDGE, tile_cols))

        for r in range(WIN):
            if r < SHIFT:
                part, beyond = both[r + SHIFT, near], both_r[r]
            else:
                part, beyond = both_b[r - SHIFT, near], both_d[r - SHIFT]
            wide = part.astype(F32)
            if b == steps - 1:
                wide = jnp.concatenate([wide, beyond.astype(F32)], 0)
            wide = wide[SHIFT : SHIFT + span_cols]
            unit[win_at, r] = wide[:, 0:C].reshape(step_wins, WIN, C)
            gradf[win_at, r] = wide[:, C : 2 * C].reshape(step_wins, WIN, C)

        x = unit[win_at].reshape(step, C)
        center = jnp.mean(x, -1, keepdims=True)
        x = x - center
        inv = lax.rsqrt(jnp.mean(x * x, -1, keepdims=True) + 1e-05)
        x = x * inv
        unit[win_at] = x.reshape(step_wins, WIN, WIN, C)
        inv_std[at] = inv
        n = (x * gain_ref[...] + offset_ref[...]).astype(BF16)
        nt_s[0:C, at] = n.T
        q_s[at] = ((mul(n, w_s[0]) + b_s[0]) * HEAD ** (-0.5)).astype(BF16)
        k_s[at] = (mul(n, w_s[1]) + b_s[1]).astype(BF16)
        v_s[at] = (mul(n, w_s[2]) + b_s[2]).astype(BF16)
        g = gradf[win_at].reshape(step, C).astype(BF16)
        gb_s[at] = g
        da_s[at] = mul(g, pw_s[...], NT).astype(BF16)

        @pl.loop(0, step_wins // 2)
        def _(pair_at):
            for i in range(2):
                w = b * step_wins + pair_at * 2 + i
                at = pl.ds(pl.multiple_of(w * SPAN, SPAN), SPAN)
                same = lab_col[w] == lab_row[pl.ds(w, 1), :]
                q, k, v, da = q_s[at], k_s[at], v_s[at], da_s[at]
                att_w, dq_w, dk_w, dv_w = [], [], [], []
                for lanes, heads in ((slice(0, LANE), 4), (slice(LANE, WIDE), 2)):
                    kg, vg = k[:, lanes], v[:, lanes]
                    qm, dam = diagonal(q[:, lanes], heads), diagonal(da[:, lanes], heads)
                    scores = mul(kg, qm, NT)
                    dp = mul(vg, dam, NT)
                    lows, ds_lows = [], []
                    for t in range(heads // 2):
                        cut = slice(t * LANE, (t + 1) * LANE)
                        out_at = slice(lanes.start + t * LANE, lanes.start + (t + 1) * LANE)
                        if lanes.start:
                            out_at = slice(WIDE, WIDE + LANE)
                        biased = jnp.where(same, scores[:, cut] + bias_t[:, out_at], MASKED)
                        e = jnp.exp(biased - jnp.max(biased, 0, keepdims=True))
                        p = e * (1.0 / jnp.sum(e, 0, keepdims=True))
                        lows.append(p.astype(BF16))
                        grad = dp[:, cut]
                        ds = p * (grad - jnp.sum(p * grad, 0, keepdims=True))
                        score_acc[:, out_at] += ds
                        ds_lows.append(ds.astype(BF16))
                    p_low = jnp.concatenate(lows, 1)
                    ds_low = jnp.concatenate(ds_lows, 1)
                    att_w.append(gather_heads(mul(p_low, vg, TN)).astype(BF16))
                    dq_w.append((gather_heads(mul(ds_low, kg, TN)) * HEAD ** (-0.5)).astype(BF16))
                    dk_w.append(mul(ds_low, qm).astype(BF16))
                    dv_w.append(mul(p_low, dam).astype(BF16))
                att[at] = jnp.concatenate(att_w, 1)
                dq_s[at] = jnp.concatenate(dq_w, 1)
                dk_s[at] = jnp.concatenate(dk_w, 1)
                dv_s[at] = jnp.concatenate(dv_w, 1)

        x = unit[win_at].reshape(step, C)
        dn = mul(dq_s[at], w_s[0], NT) + mul(dk_s[at], w_s[1], NT) + mul(dv_s[at], w_s[2], NT)
        sums[0:1, 0:C] += jnp.sum(dn * x, 0, keepdims=True)
        sums[1:2, 0:C] += jnp.sum(dn, 0, keepdims=True)
        g = dn * gain_ref[...]
        dx = inv_std[at] * (
            g - jnp.mean(g, -1, keepdims=True) - x * jnp.mean(g * x, -1, keepdims=True)
        )
        out = (gradf[win_at].reshape(step, C) + dx).reshape(step_wins, WIN, WIN, C)
        for r in range(SHIFT):
            frame_low[r, cols] = out[:, r].reshape(span_cols, C).astype(BF16)
        for r in range(0, SHIFT, 2):
            two = [out[:, SHIFT + r + i].reshape(span_cols, C) for i in range(2)]
            frame_two[r // 2, cols] = jnp.concatenate(two, 1).astype(BF16)
        back(frame_two.at[0:2, cols], back_u.at[0:2, cols], down, col)
        if b == steps - 1:
            back(frame_low.at[0:SHIFT, edge:tile_cols], back_l, row, other)
            back(frame_two.at[0:2, edge:tile_cols], back_ul, down, other)

    lows = []
    for i, part in enumerate((dq_s, dk_s, dv_s)):
        product = mul(nt_s[...], part[...])
        pack[i * BLOCK : (i + 1) * BLOCK, :] = product[:, 0:LANE]
        lows.append(product[:, LANE:WIDE])
    product = mul(gb_s[...], att[...], TN)
    pack[3 * BLOCK : 3 * BLOCK + C, :] = product[:, 0:LANE]
    pack[3 * BLOCK + C : 4 * BLOCK, :] = jnp.zeros((BLOCK - C, LANE), F32)
    pack[4 * BLOCK : 5 * BLOCK, :] = lows[0] + pltpu.roll(lows[1], 64, 1)
    pack[5 * BLOCK : 6 * BLOCK, :] = lows[2]
    pack[5 * BLOCK : 5 * BLOCK + C, :] += pltpu.roll(product[:, LANE:WIDE], 64, 1)
    for h in range(HEADS):
        span_a[h * SPAN : (h + 1) * SPAN, :] = score_acc[:, h * SPAN : (h + 1) * SPAN]
    wide = jnp.concatenate(
        [span_a[pl.ds(cj, HEADS * WIN, stride=WIN), :] for cj in range(WIN)], 1
    )
    span_b[...] = split_mul(wide, fold_a[...])
    wide = jnp.concatenate(
        [span_b[pl.ds(rj, HEADS, stride=WIN), :] for rj in range(WIN)], 1
    )
    flat_sum = split_mul(wide, fold_b[...])
    sums[8 : 8 + HEADS, :] = flat_sum
    pack[small : small + 16, :] = sums[:, 0:LANE]
    pack[small + 16 : small + 32, :] = sums[:, LANE:WIDE]
    pack_low[...] = pack[...].astype(BF16)

    pair = remote(
        pack_low.at[pl.ds(pl.multiple_of(other * half, 16), half)], pair_in,
        pair_sem.at[0], pair_sem.at[1], row, other,
    )
    pair.start()
    pair.wait()
    mine = pl.ds(pl.multiple_of(col * half, 16), half)
    half_low[...] = (pack[mine] + pair_in[...].astype(F32)).astype(BF16)

    def part_copy(k):
        peer = lax.rem(row + k, rows_n)
        return remote(
            half_low.at[pl.ds(pl.multiple_of(peer * chunk, 16), chunk)], part_in.at[k],
            part_send.at[k], part_recv.at[k], peer, col,
        )

    @pl.loop(1, rows_n)
    def _(k):
        part_copy(k).start()

    for copy in backs:
        copy.wait()
    for r in range(WIN):
        if r < SHIFT:
            lanes = slice((r % 2) * C, (r % 2 + 1) * C)
            left_part = back_ul[r // 2].astype(F32)[:, lanes]
            main_part = back_u[r // 2].astype(F32)[:, lanes]
        else:
            left_part, main_part = back_l[r - SHIFT], frame_low[r - SHIFT]
        wide = jnp.concatenate([left_part.astype(F32), main_part.astype(F32)], 0)
        d_tok[r] = wide[EDGE - SHIFT : EDGE - SHIFT + tile_cols].astype(BF16)

    def add_part(k, total):
        part_copy(k).wait()
        return total + part_in[k].astype(F32)

    my_chunk = pl.ds(pl.multiple_of(row * chunk, 16), chunk)
    total = lax.fori_loop(1, rows_n, add_part, half_low[my_chunk].astype(F32))
    own_chunk = result.at[col, my_chunk]
    own_chunk[...] = total.astype(BF16)

    def all_copy(k):
        return remote(
            own_chunk, own_chunk, all_send.at[k], all_recv.at[k],
            lax.rem(row + k, rows_n), col,
        )

    def forward(k):
        source = lax.rem(row + rows_n - k, rows_n)
        piece = result.at[col, pl.ds(pl.multiple_of(source * chunk, 16), chunk)]
        return remote(piece, piece, fwd_send.at[k], fwd_recv.at[k], row, other)

    @pl.loop(1, rows_n)
    def _(k):
        all_copy(k).start()

    forward(0).start()

    @pl.loop(1, rows_n)
    def _(k):
        all_copy(k).wait()
        forward(k).start()

    @pl.loop(0, rows_n)
    def _(k):
        forward(k).wait()

    done = jnp.concatenate([result[0], result[1]], 0)
    blocks = [done[i * BLOCK : (i + 1) * BLOCK] for i in range(6)]
    joined = jnp.concatenate([blocks[i] for i in (0, 1, 2, 4, 5)], 1)
    product = mul(joined, pick_s[...]) * out_scale
    d_qkvw[...] = product[0:C]
    d_qkvb[...] = product[C : C + 1]
    spread = e_s[...]
    far = pltpu.roll(spread[:, LANE:WIDE].astype(F32), 64, 1).astype(BF16)
    product = mul(spread[:, 0:LANE], blocks[3], NT) + mul(far, blocks[5], NT)
    d_projw[...] = product[:, 0:C] * out_scale
    tail = done[small : small + 32].astype(F32) * out_scale
    tail = jnp.concatenate([tail[0:16], tail[16:32]], 1)
    d_gain[...] = tail[0:1, 0:C]
    d_offset[...] = tail[1:2, 0:C]
    entries = table_spread(d_table.shape[1])
    d_table[...] = exact(tail[8 : 8 + HEADS, :], entries, NT)


def on_device(
    tokens, grad_out, regions, ln_gain, ln_offset, qkv_weight, qkv_bias, proj_weight, bias_table
):
    rows_n, cols_n = lax.axis_size("row"), lax.axis_size("col")
    tile_cols = tokens.shape[1]
    wins = tile_cols // WIN
    count = wins * SPAN
    steps = wins // 4
    unit_rows = 2 * 16 * rows_n
    needed = 6 * BLOCK + 32
    rows_total = -(-needed // unit_rows) * unit_rows
    half = rows_total // 2
    chunk = half // rows_n
    total_tokens = tokens.shape[0] * tile_cols * rows_n * cols_n
    vmem = pltpu.VMEM
    halo = [
        vmem((SHIFT, tile_cols, 2 * C), BF16),
        vmem((SHIFT, EDGE, 2 * C), BF16),
        vmem((SHIFT, EDGE, 2 * C), BF16),
    ]
    home = [
        vmem((SHIFT, tile_cols, C), BF16),
        vmem((2, tile_cols, 2 * C), BF16),
        vmem((2, tile_cols, 2 * C), BF16),
        vmem((SHIFT, EDGE, C), BF16),
        vmem((2, EDGE, 2 * C), BF16),
    ]
    flat_low = vmem((count, WIDE), BF16)
    whole = pl.BlockSpec(memory_space=pltpu.VMEM)
    dma = pltpu.SemaphoreType.DMA
    outs = pl.pallas_call(
        functools.partial(body, rows_n, cols_n, rows_total, total_tokens ** (-0.5)),
        out_shape=(
            jax.ShapeDtypeStruct(tokens.shape, BF16),
            jax.ShapeDtypeStruct((C, 3 * C), F32),
            jax.ShapeDtypeStruct((1, 3 * C), F32),
            jax.ShapeDtypeStruct((C, C), F32),
            jax.ShapeDtypeStruct((HEADS, bias_table.shape[0]), F32),
            jax.ShapeDtypeStruct((1, C), F32),
            jax.ShapeDtypeStruct((1, C), F32),
        ),
        in_specs=[whole] * 8,
        out_specs=(whole,) * 7,
        scratch_shapes=halo + [
            vmem(regions.shape, jnp.int32),
            vmem(regions.shape, jnp.int32),
            vmem((wins, WIN, WIN, C), F32),
            vmem((count, 1), F32),
            vmem((wins, WIN, WIN, C), F32),
            vmem((192, count), BF16),
        ] + [flat_low] * 4 + [vmem((count, C), BF16)] + [flat_low] * 4 + [
            vmem((3, C, WIDE), BF16),
            vmem((3, 1, WIDE), F32),
            vmem((WIDE, C), BF16),
            vmem((C, WIDE), BF16),
            vmem((5 * LANE, 3 * C), BF16),
            vmem((SPAN, LANES), F32),
            vmem((HEADS * SPAN, SPAN), F32),
            vmem((HEADS * WIN, 128), F32),
            vmem((4 * 16, LANE), BF16),
            vmem((wins, SPAN, 128), F32),
            vmem((wins, LANE), F32),
            vmem((SPAN, LANES), F32),
            vmem((16, WIDE), F32),
            vmem((WIN * SPAN, 128), BF16),
            vmem((WIN * 128, 256), BF16),
        ] + home + [
            vmem((rows_total, LANE), F32),
            vmem((rows_total, LANE), BF16),
            vmem((half, LANE), BF16),
            vmem((half, LANE), BF16),
            vmem((rows_n, chunk, LANE), BF16),
            vmem((2, half, LANE), BF16),
            dma((4 + steps,)), dma((4 + steps,)),
            dma((steps + 2,)), dma((steps + 2,)), dma((2,)),
            dma((rows_n,)), dma((rows_n,)), dma((rows_n,)), dma((rows_n,)),
            dma((rows_n,)), dma((rows_n,)),
        ],
        compiler_params=pltpu.CompilerParams(
            collective_id=0, has_side_effects=True, vmem_limit_bytes=48 * 1024 * 1024
        ),
    )(
        jnp.concatenate([tokens, grad_out], -1), regions, ln_gain.reshape(1, C), ln_offset.reshape(1, C), qkv_weight,
        qkv_bias.reshape(1, 3 * C), proj_weight, bias_table.T,
    )
    d_tokens, d_qkvw, d_qkvb, d_projw, d_table, d_gain, d_offset = outs
    return (
        d_tokens,
        d_qkvw,
        d_qkvb.reshape(3 * C),
        d_projw,
        d_table.T,
        d_gain.reshape(C),
        d_offset.reshape(C),
    )


def solution(mesh):
    placed = (
        P(("grp", "row"), "col", None),
        P(("grp", "row"), "col", None),
        P(("grp", "row"), "col"),
        P(),
        P(),
        P(),
        P(),
        P(),
        P(),
    )
    return jax.shard_map(
        on_device,
        mesh=mesh,
        in_specs=placed,
        out_specs=(
            P(("grp", "row"), "col", None),
            P("grp", None),
            P("grp"),
            P("grp", None),
            P("grp", None),
            P("grp"),
            P("grp"),
        ),
        check_vma=False,
    )
```

```python
import functools

import jax
import jax.numpy as jnp
from jax import lax
from jax.experimental import pallas as pl
from jax.experimental.pallas import tpu as pltpu
from jax.sharding import PartitionSpec as P

HEADS = 6
WIN = 8
SHIFT = 4
SPAN = WIN * WIN
C = 180
HEAD = C // HEADS
LANES = HEADS * SPAN
BLOCK = 192
LANE = 128
WIDE = 2 * LANE
HEADW = 32
EDGE = 16
MASKED = -10000.0
MESH = pl.DeviceIdType.MESH
F32 = jnp.float32
BF16 = jnp.bfloat16

NN = (((1,), (0,)), ((), ()))
NT = (((1,), (1,)), ((), ()))
TN = (((0,), (0,)), ((), ()))


def mul(left, right, form=NN):
    return lax.dot_general(left, right, form, preferred_element_type=F32)


def exact(left, right, form=NN):
    return lax.dot_general(
        left, right, form, preferred_element_type=F32, precision=lax.Precision.HIGHEST
    )


def split_mul(left, picks):
    high = left.astype(BF16)
    low = (left - high.astype(F32)).astype(BF16)
    return mul(high, picks) + mul(low, picks)


def iota(shape, dim):
    return lax.broadcasted_iota(jnp.int32, shape, dim)


def col_spread(cj):
    src = iota((SPAN, 128), 0)
    dst = iota((SPAN, 128), 1)
    return (dst == (src >> 3) * 16 + (src & 7) - cj + 7).astype(F32)


def row_spread(rj):
    src = iota((128, 256), 0)
    dst = iota((128, 256), 1)
    return (dst == src + 16 * (7 - rj)).astype(F32)


def table_spread(entries):
    src = iota((entries, 256), 0)
    dst = iota((entries, 256), 1)
    hit = (src == (dst >> 4) * 15 + (dst & 15)) & ((dst & 15) < 15) & (dst < 240)
    return hit.astype(F32)


def head_spread():
    src = iota((C, WIDE), 0)
    lane = iota((1, WIDE), 1)
    head, place = lane >> 5, lane & (HEADW - 1)
    wanted = jnp.where((place < HEAD) & (head < HEADS), head * HEAD + place, -1)
    return (src == wanted).astype(F32).astype(BF16)


def part_pick():
    lane = iota((1, 3 * C), 1)
    part = (lane >= C).astype(jnp.int32) + (lane >= 2 * C).astype(jnp.int32)
    place = lane - part * C
    head = sum((place >= t * HEAD).astype(jnp.int32) for t in range(1, HEADS))
    place = place - head * HEAD
    near = part * LANE + head * HEADW + place
    far = 3 * LANE + (part >> 1) * LANE + (part & 1) * 64 + (head - 4) * HEADW + place
    wanted = jnp.where(head < 4, near, far)
    return (iota((5 * LANE, 3 * C), 0) == wanted).astype(F32).astype(BF16)


def body(
    rows_n, cols_n, rows_total, out_scale,
    both, reg, gain_ref, offset_ref, qkvw, qkvb, projw, table,
    d_tok, d_qkvw, d_qkvb, d_projw, d_table, d_gain, d_offset,
    both_b, both_r, both_d, reg_b, reg_r,
    unit, inv_std, gradf, nt_s, q_s, k_s, v_s, da_s, gb_s, att, dq_s, dk_s, dv_s,
    w_s, b_s, pw_s, e_s, pick_s, bias_t, span_a, span_b, hmask, lab_col, lab_row, score_acc, sums,
    scores_s, dp_s, p_s, ds_s,
    fold_a, fold_b, frame_low, frame_two, back_u, back_l, back_ul,
    pack, pack_low, pair_in, half_low, part_in, result,
    halo_send, halo_recv, back_send, back_recv, pair_sem,
    part_send, part_recv, all_send, all_recv, fwd_send, fwd_recv,
):
    row = lax.axis_index("row")
    col = lax.axis_index("col")
    up = lax.rem(row + rows_n - 1, rows_n)
    down = lax.rem(row + 1, rows_n)
    other = lax.rem(col + 1, cols_n)
    tile_cols = both.shape[1]
    wins = tile_cols // WIN
    count = wins * SPAN
    half = rows_total // 2
    chunk = half // rows_n

    def remote(src, dst, send, recv, to_row, to_col):
        return pltpu.make_async_remote_copy(
            src_ref=src, dst_ref=dst, send_sem=send, recv_sem=recv,
            device_id={"row": to_row, "col": to_col}, device_id_type=MESH,
        )

    barrier = pltpu.get_barrier_semaphore()

    @pl.loop(1, rows_n)
    def _(k):
        pl.semaphore_signal(
            barrier, inc=1, device_id={"row": lax.rem(row + k, rows_n), "col": col},
            device_id_type=MESH,
        )

    for to_row in (row, up, down):
        pl.semaphore_signal(
            barrier, inc=1, device_id={"row": to_row, "col": other}, device_id_type=MESH
        )
    pl.semaphore_wait(barrier, rows_n + 2)

    step_wins = 4
    step = step_wins * SPAN
    steps = wins // step_wins
    span_cols = step_wins * WIN

    def halo(i, src, dst, to_row, to_col):
        return remote(src, dst, halo_send.at[i], halo_recv.at[i], to_row, to_col)

    labels = [halo(0, reg, reg_b, up, col), halo(1, reg, reg_r, row, other)]
    sides = [
        halo(2, both.at[SHIFT:WIN, 0:EDGE], both_r, row, other),
        halo(3, both.at[0:SHIFT, 0:EDGE], both_d, up, other),
    ]
    chunks = []
    for b in range(steps):
        first = b * span_cols + (EDGE if b else 0)
        last = min((b + 1) * span_cols + EDGE, tile_cols)
        src, dst = both.at[0:SHIFT, first:last], both_b.at[0:SHIFT, first:last]
        chunks.append([halo(4 + b, src, dst, up, col)])
    small = 6 * BLOCK
    for copy in labels + chunks[0] + sides + chunks[1]:
        copy.start()

    flat = exact(table[...], table_spread(table.shape[1]))
    for rj in range(WIN):
        span_b[pl.ds(rj, HEADS, stride=WIN), :] = exact(flat, row_spread(rj), NT)
    for cj in range(WIN):
        span_a[pl.ds(cj, HEADS * WIN, stride=WIN), :] = exact(span_b[...], col_spread(cj), NT)
    for h in range(HEADS):
        bias_t[:, h * SPAN : (h + 1) * SPAN] = span_a[h * SPAN : (h + 1) * SPAN, :]
    mask_row = iota((4 * 16, LANE), 0) >> 4
    hmask[...] = ((iota((4 * 16, LANE), 1) >> 5) == mask_row).astype(F32).astype(BF16)
    e_s[...] = head_spread()
    pick_s[...] = part_pick()
    score_acc[...] = jnp.zeros_like(score_acc)
    sums[...] = jnp.zeros_like(sums)
    pack[small:] = jnp.zeros_like(pack[small:])

    nt_s[...] = jnp.ones_like(nt_s)
    for cj in range(WIN):
        fold_a[cj * SPAN : (cj + 1) * SPAN, :] = col_spread(cj).astype(BF16)
    for rj in range(WIN):
        fold_b[rj * 128 : (rj + 1) * 128, :] = row_spread(rj).astype(BF16)
    weights = qkvw[...]
    offsets = qkvb[...]
    for i in range(3):
        w_s[i] = mul(weights[:, i * C : (i + 1) * C], e_s[...]).astype(BF16)
        b_s[i] = exact(offsets[:, i * C : (i + 1) * C], e_s[...].astype(F32))
    pw_s[...] = mul(e_s[...], projw[...], TN).astype(BF16)

    for copy in labels:
        copy.wait()

    own = reg[...]
    row_part = jnp.concatenate([own[SHIFT:], reg_b[0:SHIFT, :]], 0)[:, 0:1] >> 2
    col_own = pltpu.roll(own, tile_cols - SHIFT, 1)
    col_right = pltpu.roll(reg_r[...], tile_cols - SHIFT, 1)
    col_part = jnp.where(iota((WIN, tile_cols), 1) < tile_cols - SHIFT, col_own, col_right)[0:1] & 3
    label = (row_part * 4 + col_part).astype(F32)
    spread = jnp.broadcast_to(label[:, None, :], (WIN, WIN, tile_cols)).reshape(SPAN, tile_cols)
    spread = jnp.where(
        (iota((SPAN, tile_cols), 0) & 7) == (iota((SPAN, tile_cols), 1) & 7), spread, 0.0
    )
    pick = ((iota((tile_cols, wins), 0) >> 3) == iota((tile_cols, wins), 1)).astype(F32)
    columns = exact(spread, pick)
    tiled = (iota((SPAN, LANE), 0) == (iota((SPAN, LANE), 1) & (SPAN - 1))).astype(F32)
    lab_row[...] = exact(columns, tiled, TN)
    for w in range(wins):
        lab_col[w] = jnp.broadcast_to(columns[:, w : w + 1], (SPAN, 128))

    lane = iota((SPAN, LANE), 1)

    def gather_heads(stacked):
        out = stacked[-SPAN:]
        for h in range(stacked.shape[0] // SPAN - 2, -1, -1):
            out = jnp.where(lane < (h + 1) * HEADW, stacked[h * SPAN : (h + 1) * SPAN], out)
        return out

    def diagonal(x, heads):
        tiles = x.reshape(SPAN // 16, 16, LANE)
        parts = [
            (tiles * hmask[h * 16 : (h + 1) * 16, :][None]).reshape(SPAN, LANE) for h in range(heads)
        ]
        return jnp.concatenate(parts, 0)

    groups = ((slice(0, LANE), slice(0, 4 * SPAN), 4), (slice(LANE, WIDE), slice(4 * SPAN, LANES), 2))

    def score_step(w0, n):
        for w in range(w0, w0 + n):
            at = slice(w * SPAN, (w + 1) * SPAN)
            for lanes, cut, heads in groups:
                scores_s[w, :, cut] = mul(k_s[at, lanes], diagonal(q_s[at, lanes], heads), NT)
                dp_s[w, :, cut] = mul(v_s[at, lanes], diagonal(da_s[at, lanes], heads), NT)

    def softmax_step(w0, n):
        for w in range(w0, w0 + n):
            same = lab_col[w] == lab_row[w : w + 1, :]
            for t in range(HEADS // 2):
                cut = slice(t * LANE, (t + 1) * LANE)
                scores = jnp.where(same, scores_s[w, :, cut] + bias_t[:, cut], MASKED)
                e = jnp.exp(scores - jnp.max(scores, 0, keepdims=True))
                p = e * (1.0 / jnp.sum(e, 0, keepdims=True))
                p_s[w, :, cut] = p.astype(BF16)
                dp = dp_s[w, :, cut]
                ds = p * (dp - jnp.sum(p * dp, 0, keepdims=True))
                score_acc[:, cut] += ds
                ds_s[w, :, cut] = ds.astype(BF16)

    def spread_step(w0, n):
        for w in range(w0, w0 + n):
            at = slice(w * SPAN, (w + 1) * SPAN)
            for lanes, cut, heads in groups:
                p, ds = p_s[w, :, cut], ds_s[w, :, cut]
                att[at, lanes] = gather_heads(mul(p, v_s[at, lanes], TN)).astype(BF16)
                dq = gather_heads(mul(ds, k_s[at, lanes], TN))
                dq_s[at, lanes] = (dq * HEAD ** (-0.5)).astype(BF16)
                dk_s[at, lanes] = mul(ds, diagonal(q_s[at, lanes], heads)).astype(BF16)
                dv_s[at, lanes] = mul(p, diagonal(da_s[at, lanes], heads)).astype(BF16)

    edge = tile_cols - EDGE
    backs = []

    def back(src, dst, to_row, to_col):
        i = len(backs)
        backs.append(remote(src, dst, back_send.at[i], back_recv.at[i], to_row, to_col))
        backs[-1].start()

    for b in range(steps):
        for copy in chunks[b] + (sides if b == steps - 1 else []):
            copy.wait()
        if b + 2 < steps:
            for copy in chunks[b + 2]:
                copy.start()
        at = slice(b * step, (b + 1) * step)
        win_at = slice(b * step_wins, (b + 1) * step_wins)
        cols = slice(b * span_cols, (b + 1) * span_cols)
        near = slice(b * span_cols, min((b + 1) * span_cols + EDGE, tile_cols))

        for r in range(WIN):
            if r < SHIFT:
                part, beyond = both[r + SHIFT, near], both_r[r]
            else:
                part, beyond = both_b[r - SHIFT, near], both_d[r - SHIFT]
            wide = part.astype(F32)
            if b == steps - 1:
                wide = jnp.concatenate([wide, beyond.astype(F32)], 0)
            wide = wide[SHIFT : SHIFT + span_cols]
            unit[win_at, r] = wide[:, 0:C].reshape(step_wins, WIN, C)
            gradf[win_at, r] = wide[:, C : 2 * C].reshape(step_wins, WIN, C)

        x = unit[win_at].reshape(step, C)
        center = jnp.mean(x, -1, keepdims=True)
        x = x - center
        inv = lax.rsqrt(jnp.mean(x * x, -1, keepdims=True) + 1e-05)
        x = x * inv
        unit[win_at] = x.reshape(step_wins, WIN, WIN, C)
        inv_std[at] = inv
        n = (x * gain_ref[...] + offset_ref[...]).astype(BF16)
        nt_s[0:C, at] = n.T
        q_s[at] = ((mul(n, w_s[0]) + b_s[0]) * HEAD ** (-0.5)).astype(BF16)
        k_s[at] = (mul(n, w_s[1]) + b_s[1]).astype(BF16)
        v_s[at] = (mul(n, w_s[2]) + b_s[2]).astype(BF16)
        g = gradf[win_at].reshape(step, C).astype(BF16)
        gb_s[at] = g
        da_s[at] = mul(g, pw_s[...], NT).astype(BF16)

        first = b * step_wins
        score_step(first, 2)
        for w in range(first, first + step_wins, 2):
            softmax_step(w, 2)
            if w + 2 < first + step_wins:
                score_step(w + 2, 2)
            spread_step(w, 2)

        x = unit[win_at].reshape(step, C)
        dn = mul(dq_s[at], w_s[0], NT) + mul(dk_s[at], w_s[1], NT) + mul(dv_s[at], w_s[2], NT)
        sums[0:1, 0:C] += jnp.sum(dn * x, 0, keepdims=True)
        sums[1:2, 0:C] += jnp.sum(dn, 0, keepdims=True)
        g = dn * gain_ref[...]
        dx = inv_std[at] * (
            g - jnp.mean(g, -1, keepdims=True) - x * jnp.mean(g * x, -1, keepdims=True)
        )
        out = (gradf[win_at].reshape(step, C) + dx).reshape(step_wins, WIN, WIN, C)
        for r in range(SHIFT):
            frame_low[r, cols] = out[:, r].reshape(span_cols, C).astype(BF16)
        for r in range(0, SHIFT, 2):
            two = [out[:, SHIFT + r + i].reshape(span_cols, C) for i in range(2)]
            frame_two[r // 2, cols] = jnp.concatenate(two, 1).astype(BF16)
        back(frame_two.at[0:2, cols], back_u.at[0:2, cols], down, col)
        if b == steps - 1:
            back(frame_low.at[0:SHIFT, edge:tile_cols], back_l, row, other)
            back(frame_two.at[0:2, edge:tile_cols], back_ul, down, other)

    lows = []
    for i, part in enumerate((dq_s, dk_s, dv_s)):
        product = mul(nt_s[...], part[...])
        pack[i * BLOCK : (i + 1) * BLOCK, :] = product[:, 0:LANE]
        lows.append(product[:, LANE:WIDE])
    product = mul(gb_s[...], att[...], TN)
    pack[3 * BLOCK : 3 * BLOCK + C, :] = product[:, 0:LANE]
    pack[3 * BLOCK + C : 4 * BLOCK, :] = jnp.zeros((BLOCK - C, LANE), F32)
    pack[4 * BLOCK : 5 * BLOCK, :] = lows[0] + pltpu.roll(lows[1], 64, 1)
    pack[5 * BLOCK : 6 * BLOCK, :] = lows[2]
    pack[5 * BLOCK : 5 * BLOCK + C, :] += pltpu.roll(product[:, LANE:WIDE], 64, 1)
    for h in range(HEADS):
        span_a[h * SPAN : (h + 1) * SPAN, :] = score_acc[:, h * SPAN : (h + 1) * SPAN]
    wide = jnp.concatenate(
        [span_a[pl.ds(cj, HEADS * WIN, stride=WIN), :] for cj in range(WIN)], 1
    )
    span_b[...] = split_mul(wide, fold_a[...])
    wide = jnp.concatenate(
        [span_b[pl.ds(rj, HEADS, stride=WIN), :] for rj in range(WIN)], 1
    )
    flat_sum = split_mul(wide, fold_b[...])
    sums[8 : 8 + HEADS, :] = flat_sum
    pack[small : small + 16, :] = sums[:, 0:LANE]
    pack[small + 16 : small + 32, :] = sums[:, LANE:WIDE]
    pack_low[...] = pack[...].astype(BF16)

    pair = remote(
        pack_low.at[pl.ds(pl.multiple_of(other * half, 16), half)], pair_in,
        pair_sem.at[0], pair_sem.at[1], row, other,
    )
    pair.start()
    pair.wait()
    mine = pl.ds(pl.multiple_of(col * half, 16), half)
    half_low[...] = (pack[mine] + pair_in[...].astype(F32)).astype(BF16)

    def part_copy(k):
        peer = lax.rem(row + k, rows_n)
        return remote(
            half_low.at[pl.ds(pl.multiple_of(peer * chunk, 16), chunk)], part_in.at[k],
            part_send.at[k], part_recv.at[k], peer, col,
        )

    @pl.loop(1, rows_n)
    def _(k):
        part_copy(k).start()

    for copy in backs:
        copy.wait()
    for r in range(WIN):
        if r < SHIFT:
            lanes = slice((r % 2) * C, (r % 2 + 1) * C)
            left_part = back_ul[r // 2].astype(F32)[:, lanes]
            main_part = back_u[r // 2].astype(F32)[:, lanes]
        else:
            left_part, main_part = back_l[r - SHIFT], frame_low[r - SHIFT]
        wide = jnp.concatenate([left_part.astype(F32), main_part.astype(F32)], 0)
        d_tok[r] = wide[EDGE - SHIFT : EDGE - SHIFT + tile_cols].astype(BF16)

    def add_part(k, total):
        part_copy(k).wait()
        return total + part_in[k].astype(F32)

    my_chunk = pl.ds(pl.multiple_of(row * chunk, 16), chunk)
    total = lax.fori_loop(1, rows_n, add_part, half_low[my_chunk].astype(F32))
    own_chunk = result.at[col, my_chunk]
    own_chunk[...] = total.astype(BF16)

    def all_copy(k):
        return remote(
            own_chunk, own_chunk, all_send.at[k], all_recv.at[k],
            lax.rem(row + k, rows_n), col,
        )

    def forward(k):
        source = lax.rem(row + rows_n - k, rows_n)
        piece = result.at[col, pl.ds(pl.multiple_of(source * chunk, 16), chunk)]
        return remote(piece, piece, fwd_send.at[k], fwd_recv.at[k], row, other)

    @pl.loop(1, rows_n)
    def _(k):
        all_copy(k).start()

    forward(0).start()

    @pl.loop(1, rows_n)
    def _(k):
        all_copy(k).wait()
        forward(k).start()

    @pl.loop(0, rows_n)
    def _(k):
        forward(k).wait()

    done = jnp.concatenate([result[0], result[1]], 0)
    blocks = [done[i * BLOCK : (i + 1) * BLOCK] for i in range(6)]
    joined = jnp.concatenate([blocks[i] for i in (0, 1, 2, 4, 5)], 1)
    product = mul(joined, pick_s[...]) * out_scale
    d_qkvw[...] = product[0:C]
    d_qkvb[...] = product[C : C + 1]
    spread = e_s[...]
    far = pltpu.roll(spread[:, LANE:WIDE].astype(F32), 64, 1).astype(BF16)
    product = mul(spread[:, 0:LANE], blocks[3], NT) + mul(far, blocks[5], NT)
    d_projw[...] = product[:, 0:C] * out_scale
    tail = done[small : small + 32].astype(F32) * out_scale
    tail = jnp.concatenate([tail[0:16], tail[16:32]], 1)
    d_gain[...] = tail[0:1, 0:C]
    d_offset[...] = tail[1:2, 0:C]
    entries = table_spread(d_table.shape[1])
    d_table[...] = exact(tail[8 : 8 + HEADS, :], entries, NT)


def on_device(
    tokens, grad_out, regions, ln_gain, ln_offset, qkv_weight, qkv_bias, proj_weight, bias_table
):
    rows_n, cols_n = lax.axis_size("row"), lax.axis_size("col")
    tile_cols = tokens.shape[1]
    wins = tile_cols // WIN
    count = wins * SPAN
    steps = wins // 4
    unit_rows = 2 * 16 * rows_n
    needed = 6 * BLOCK + 32
    rows_total = -(-needed // unit_rows) * unit_rows
    half = rows_total // 2
    chunk = half // rows_n
    total_tokens = tokens.shape[0] * tile_cols * rows_n * cols_n
    vmem = pltpu.VMEM
    halo = [
        vmem((SHIFT, tile_cols, 2 * C), BF16),
        vmem((SHIFT, EDGE, 2 * C), BF16),
        vmem((SHIFT, EDGE, 2 * C), BF16),
    ]
    home = [
        vmem((SHIFT, tile_cols, C), BF16),
        vmem((2, tile_cols, 2 * C), BF16),
        vmem((2, tile_cols, 2 * C), BF16),
        vmem((SHIFT, EDGE, C), BF16),
        vmem((2, EDGE, 2 * C), BF16),
    ]
    flat_low = vmem((count, WIDE), BF16)
    whole = pl.BlockSpec(memory_space=pltpu.VMEM)
    dma = pltpu.SemaphoreType.DMA
    outs = pl.pallas_call(
        functools.partial(body, rows_n, cols_n, rows_total, total_tokens ** (-0.5)),
        out_shape=(
            jax.ShapeDtypeStruct(tokens.shape, BF16),
            jax.ShapeDtypeStruct((C, 3 * C), F32),
            jax.ShapeDtypeStruct((1, 3 * C), F32),
            jax.ShapeDtypeStruct((C, C), F32),
            jax.ShapeDtypeStruct((HEADS, bias_table.shape[0]), F32),
            jax.ShapeDtypeStruct((1, C), F32),
            jax.ShapeDtypeStruct((1, C), F32),
        ),
        in_specs=[whole] * 8,
        out_specs=(whole,) * 7,
        scratch_shapes=halo + [
            vmem(regions.shape, jnp.int32),
            vmem(regions.shape, jnp.int32),
            vmem((wins, WIN, WIN, C), F32),
            vmem((count, 1), F32),
            vmem((wins, WIN, WIN, C), F32),
            vmem((192, count), BF16),
        ] + [flat_low] * 4 + [vmem((count, C), BF16)] + [flat_low] * 4 + [
            vmem((3, C, WIDE), BF16),
            vmem((3, 1, WIDE), F32),
            vmem((WIDE, C), BF16),
            vmem((C, WIDE), BF16),
            vmem((5 * LANE, 3 * C), BF16),
            vmem((SPAN, LANES), F32),
            vmem((HEADS * SPAN, SPAN), F32),
            vmem((HEADS * WIN, 128), F32),
            vmem((4 * 16, LANE), BF16),
            vmem((wins, SPAN, 128), F32),
            vmem((wins, LANE), F32),
            vmem((SPAN, LANES), F32),
            vmem((16, WIDE), F32),
            vmem((wins, SPAN, LANES), F32),
            vmem((wins, SPAN, LANES), F32),
            vmem((wins, SPAN, LANES), BF16),
            vmem((wins, SPAN, LANES), BF16),
            vmem((WIN * SPAN, 128), BF16),
            vmem((WIN * 128, 256), BF16),
        ] + home + [
            vmem((rows_total, LANE), F32),
            vmem((rows_total, LANE), BF16),
            vmem((half, LANE), BF16),
            vmem((half, LANE), BF16),
            vmem((rows_n, chunk, LANE), BF16),
            vmem((2, half, LANE), BF16),
            dma((4 + steps,)), dma((4 + steps,)),
            dma((steps + 2,)), dma((steps + 2,)), dma((2,)),
            dma((rows_n,)), dma((rows_n,)), dma((rows_n,)), dma((rows_n,)),
            dma((rows_n,)), dma((rows_n,)),
        ],
        compiler_params=pltpu.CompilerParams(
            collective_id=0, has_side_effects=True, vmem_limit_bytes=48 * 1024 * 1024
        ),
    )(
        jnp.concatenate([tokens, grad_out], -1), regions, ln_gain.reshape(1, C), ln_offset.reshape(1, C), qkv_weight,
        qkv_bias.reshape(1, 3 * C), proj_weight, bias_table.T,
    )
    d_tokens, d_qkvw, d_qkvb, d_projw, d_table, d_gain, d_offset = outs
    return (
        d_tokens,
        d_qkvw,
        d_qkvb.reshape(3 * C),
        d_projw,
        d_table.T,
        d_gain.reshape(C),
        d_offset.reshape(C),
    )


def solution(mesh):
    placed = (
        P(("grp", "row"), "col", None),
        P(("grp", "row"), "col", None),
        P(("grp", "row"), "col"),
        P(),
        P(),
        P(),
        P(),
        P(),
        P(),
    )
    return jax.shard_map(
        on_device,
        mesh=mesh,
        in_specs=placed,
        out_specs=(
            P(("grp", "row"), "col", None),
            P("grp", None),
            P("grp"),
            P("grp", None),
            P("grp", None),
            P("grp"),
            P("grp"),
        ),
        check_vma=False,
    )
```

```python
import functools

import jax
import jax.numpy as jnp
from jax import lax
from jax.experimental import pallas as pl
from jax.experimental.pallas import tpu as pltpu
from jax.sharding import PartitionSpec as P

HEADS = 6
WIN = 8
SHIFT = 4
SPAN = WIN * WIN
C = 180
HEAD = C // HEADS
LANES = HEADS * SPAN
BLOCK = 192
LANE = 128
WIDE = 2 * LANE
HEADW = 32
EDGE = 16
MASKED = -10000.0
MESH = pl.DeviceIdType.MESH
F32 = jnp.float32
BF16 = jnp.bfloat16

NN = (((1,), (0,)), ((), ()))
NT = (((1,), (1,)), ((), ()))
TN = (((0,), (0,)), ((), ()))


def mul(left, right, form=NN):
    return lax.dot_general(left, right, form, preferred_element_type=F32)


def exact(left, right, form=NN):
    return lax.dot_general(
        left, right, form, preferred_element_type=F32, precision=lax.Precision.HIGHEST
    )


def split_mul(left, picks):
    high = left.astype(BF16)
    low = (left - high.astype(F32)).astype(BF16)
    return mul(high, picks) + mul(low, picks)


def iota(shape, dim):
    return lax.broadcasted_iota(jnp.int32, shape, dim)


def col_spread(cj):
    src = iota((SPAN, 128), 0)
    dst = iota((SPAN, 128), 1)
    return (dst == (src >> 3) * 16 + (src & 7) - cj + 7).astype(F32)


def row_spread(rj):
    src = iota((128, 256), 0)
    dst = iota((128, 256), 1)
    return (dst == src + 16 * (7 - rj)).astype(F32)


def table_spread(entries):
    src = iota((entries, 256), 0)
    dst = iota((entries, 256), 1)
    hit = (src == (dst >> 4) * 15 + (dst & 15)) & ((dst & 15) < 15) & (dst < 240)
    return hit.astype(F32)


def head_spread():
    src = iota((C, WIDE), 0)
    lane = iota((1, WIDE), 1)
    head, place = lane >> 5, lane & (HEADW - 1)
    wanted = jnp.where((place < HEAD) & (head < HEADS), head * HEAD + place, -1)
    return (src == wanted).astype(F32).astype(BF16)


def part_pick():
    lane = iota((1, 3 * C), 1)
    part = (lane >= C).astype(jnp.int32) + (lane >= 2 * C).astype(jnp.int32)
    place = lane - part * C
    head = sum((place >= t * HEAD).astype(jnp.int32) for t in range(1, HEADS))
    place = place - head * HEAD
    near = part * LANE + head * HEADW + place
    far = 3 * LANE + (part >> 1) * LANE + (part & 1) * 64 + (head - 4) * HEADW + place
    wanted = jnp.where(head < 4, near, far)
    return (iota((5 * LANE, 3 * C), 0) == wanted).astype(F32).astype(BF16)


def body(
    rows_n, cols_n, rows_total, out_scale,
    both, reg, gain_in, offset_in, qkvw_in, qkvb_in, projw_in, table_in,
    d_tok, d_qkvw, d_qkvb, d_projw, d_table, d_gain, d_offset,
    both_b, both_r, both_d, reg_b, reg_r,
    unit, inv_std, gradf, nt_s, q_s, k_s, v_s, da_s, gb_s, att, dq_s, dk_s, dv_s,
    w_s, b_s, pw_s, e_s, pick_s, bias_t, span_a, span_b, hmask, lab_col, lab_row, score_acc, sums,
    scores_s, dp_s, p_s, ds_s,
    fold_a, fold_b, frame_low, frame_two, back_u, back_l, back_ul,
    pack, pack_low, pair_in, half_low, part_in, result,
    gain_ref, offset_ref, qkvw, qkvb, projw, table, local_sem,
    halo_send, halo_recv, back_send, back_recv, pair_sem,
    part_send, part_recv, all_send, all_recv, fwd_send, fwd_recv,
):
    row = lax.axis_index("row")
    col = lax.axis_index("col")
    up = lax.rem(row + rows_n - 1, rows_n)
    down = lax.rem(row + 1, rows_n)
    other = lax.rem(col + 1, cols_n)
    tile_cols = both.shape[1]
    wins = tile_cols // WIN
    count = wins * SPAN
    half = rows_total // 2
    chunk = half // rows_n

    def remote(src, dst, send, recv, to_row, to_col):
        return pltpu.make_async_remote_copy(
            src_ref=src, dst_ref=dst, send_sem=send, recv_sem=recv,
            device_id={"row": to_row, "col": to_col}, device_id_type=MESH,
        )

    locals_ = [
        pltpu.make_async_copy(src, dst, local_sem.at[i])
        for i, (src, dst) in enumerate((
            (table_in, table), (gain_in, gain_ref), (offset_in, offset_ref),
            (qkvw_in, qkvw), (qkvb_in, qkvb), (projw_in, projw),
        ))
    ]
    for copy in locals_:
        copy.start()
    barrier = pltpu.get_barrier_semaphore()

    @pl.loop(1, rows_n)
    def _(k):
        pl.semaphore_signal(
            barrier, inc=1, device_id={"row": lax.rem(row + k, rows_n), "col": col},
            device_id_type=MESH,
        )

    for to_row in (row, up, down):
        pl.semaphore_signal(
            barrier, inc=1, device_id={"row": to_row, "col": other}, device_id_type=MESH
        )
    pl.semaphore_wait(barrier, rows_n + 2)

    step_wins = 4
    step = step_wins * SPAN
    steps = wins // step_wins
    span_cols = step_wins * WIN

    def halo(i, src, dst, to_row, to_col):
        return remote(src, dst, halo_send.at[i], halo_recv.at[i], to_row, to_col)

    labels = [halo(0, reg, reg_b, up, col), halo(1, reg, reg_r, row, other)]
    sides = [
        halo(2, both.at[SHIFT:WIN, 0:EDGE], both_r, row, other),
        halo(3, both.at[0:SHIFT, 0:EDGE], both_d, up, other),
    ]
    chunks = []
    for b in range(steps):
        first = b * span_cols + (EDGE if b else 0)
        last = min((b + 1) * span_cols + EDGE, tile_cols)
        src, dst = both.at[0:SHIFT, first:last], both_b.at[0:SHIFT, first:last]
        chunks.append([halo(4 + b, src, dst, up, col)])
    small = 6 * BLOCK
    for copy in labels + chunks[0] + sides + chunks[1]:
        copy.start()

    for copy in locals_:
        copy.wait()
    flat = exact(table[...], table_spread(table.shape[1]))
    for rj in range(WIN):
        span_b[pl.ds(rj, HEADS, stride=WIN), :] = exact(flat, row_spread(rj), NT)
    for cj in range(WIN):
        span_a[pl.ds(cj, HEADS * WIN, stride=WIN), :] = exact(span_b[...], col_spread(cj), NT)
    for h in range(HEADS):
        bias_t[:, h * SPAN : (h + 1) * SPAN] = span_a[h * SPAN : (h + 1) * SPAN, :]
    mask_row = iota((4 * 16, LANE), 0) >> 4
    hmask[...] = ((iota((4 * 16, LANE), 1) >> 5) == mask_row).astype(F32).astype(BF16)
    e_s[...] = head_spread()
    pick_s[...] = part_pick()
    score_acc[...] = jnp.zeros_like(score_acc)
    sums[...] = jnp.zeros_like(sums)
    pack[small:] = jnp.zeros_like(pack[small:])

    nt_s[...] = jnp.ones_like(nt_s)
    for cj in range(WIN):
        fold_a[cj * SPAN : (cj + 1) * SPAN, :] = col_spread(cj).astype(BF16)
    for rj in range(WIN):
        fold_b[rj * 128 : (rj + 1) * 128, :] = row_spread(rj).astype(BF16)
    weights = qkvw[...]
    offsets = qkvb[...].reshape(1, 3 * C)
    for i in range(3):
        w_s[i] = mul(weights[:, i * C : (i + 1) * C], e_s[...]).astype(BF16)
        b_s[i] = exact(offsets[:, i * C : (i + 1) * C], e_s[...].astype(F32))
    pw_s[...] = mul(e_s[...], projw[...], TN).astype(BF16)

    for copy in labels:
        copy.wait()

    own = reg[...]
    row_part = jnp.concatenate([own[SHIFT:], reg_b[0:SHIFT, :]], 0)[:, 0:1] >> 2
    col_own = pltpu.roll(own, tile_cols - SHIFT, 1)
    col_right = pltpu.roll(reg_r[...], tile_cols - SHIFT, 1)
    col_part = jnp.where(iota((WIN, tile_cols), 1) < tile_cols - SHIFT, col_own, col_right)[0:1] & 3
    label = (row_part * 4 + col_part).astype(F32)
    spread = jnp.broadcast_to(label[:, None, :], (WIN, WIN, tile_cols)).reshape(SPAN, tile_cols)
    spread = jnp.where(
        (iota((SPAN, tile_cols), 0) & 7) == (iota((SPAN, tile_cols), 1) & 7), spread, 0.0
    )
    pick = ((iota((tile_cols, wins), 0) >> 3) == iota((tile_cols, wins), 1)).astype(F32)
    columns = exact(spread, pick)
    tiled = (iota((SPAN, LANE), 0) == (iota((SPAN, LANE), 1) & (SPAN - 1))).astype(F32)
    lab_row[...] = exact(columns, tiled, TN)
    for w in range(wins):
        lab_col[w] = jnp.broadcast_to(columns[:, w : w + 1], (SPAN, 128))

    lane = iota((SPAN, LANE), 1)

    def gather_heads(stacked):
        out = stacked[-SPAN:]
        for h in range(stacked.shape[0] // SPAN - 2, -1, -1):
            out = jnp.where(lane < (h + 1) * HEADW, stacked[h * SPAN : (h + 1) * SPAN], out)
        return out

    def diagonal(x, heads):
        tiles = x.reshape(SPAN // 16, 16, LANE)
        parts = [
            (tiles * hmask[h * 16 : (h + 1) * 16, :][None]).reshape(SPAN, LANE) for h in range(heads)
        ]
        return jnp.concatenate(parts, 0)

    groups = ((slice(0, LANE), slice(0, 4 * SPAN), 4), (slice(LANE, WIDE), slice(4 * SPAN, LANES), 2))

    def score_step(w0, n):
        for w in range(w0, w0 + n):
            at = slice(w * SPAN, (w + 1) * SPAN)
            for lanes, cut, heads in groups:
                scores_s[w, :, cut] = mul(k_s[at, lanes], diagonal(q_s[at, lanes], heads), NT)
                dp_s[w, :, cut] = mul(v_s[at, lanes], diagonal(da_s[at, lanes], heads), NT)

    def softmax_step(w0, n):
        for w in range(w0, w0 + n):
            same = lab_col[w] == lab_row[w : w + 1, :]
            for t in range(HEADS // 2):
                cut = slice(t * LANE, (t + 1) * LANE)
                scores = jnp.where(same, scores_s[w, :, cut] + bias_t[:, cut], MASKED)
                e = jnp.exp(scores - jnp.max(scores, 0, keepdims=True))
                p = e * (1.0 / jnp.sum(e, 0, keepdims=True))
                p_s[w, :, cut] = p.astype(BF16)
                dp = dp_s[w, :, cut]
                ds = p * (dp - jnp.sum(p * dp, 0, keepdims=True))
                score_acc[:, cut] += ds
                ds_s[w, :, cut] = ds.astype(BF16)

    def spread_step(w0, n):
        for w in range(w0, w0 + n):
            at = slice(w * SPAN, (w + 1) * SPAN)
            for lanes, cut, heads in groups:
                p, ds = p_s[w, :, cut], ds_s[w, :, cut]
                att[at, lanes] = gather_heads(mul(p, v_s[at, lanes], TN)).astype(BF16)
                dq = gather_heads(mul(ds, k_s[at, lanes], TN))
                dq_s[at, lanes] = (dq * HEAD ** (-0.5)).astype(BF16)
                dk_s[at, lanes] = mul(ds, diagonal(q_s[at, lanes], heads)).astype(BF16)
                dv_s[at, lanes] = mul(p, diagonal(da_s[at, lanes], heads)).astype(BF16)

    edge = tile_cols - EDGE
    backs = []

    def back(src, dst, to_row, to_col):
        i = len(backs)
        backs.append(remote(src, dst, back_send.at[i], back_recv.at[i], to_row, to_col))
        backs[-1].start()

    for b in range(steps):
        for copy in chunks[b] + (sides if b == steps - 1 else []):
            copy.wait()
        if b + 2 < steps:
            for copy in chunks[b + 2]:
                copy.start()
        at = slice(b * step, (b + 1) * step)
        win_at = slice(b * step_wins, (b + 1) * step_wins)
        cols = slice(b * span_cols, (b + 1) * span_cols)
        near = slice(b * span_cols, min((b + 1) * span_cols + EDGE, tile_cols))

        for r in range(WIN):
            if r < SHIFT:
                part, beyond = both[r + SHIFT, near], both_r[r]
            else:
                part, beyond = both_b[r - SHIFT, near], both_d[r - SHIFT]
            wide = part.astype(F32)
            if b == steps - 1:
                wide = jnp.concatenate([wide, beyond.astype(F32)], 0)
            wide = wide[SHIFT : SHIFT + span_cols]
            unit[win_at, r] = wide[:, 0:C].reshape(step_wins, WIN, C)
            gradf[win_at, r] = wide[:, C : 2 * C].reshape(step_wins, WIN, C)

        x = unit[win_at].reshape(step, C)
        center = jnp.mean(x, -1, keepdims=True)
        x = x - center
        inv = lax.rsqrt(jnp.mean(x * x, -1, keepdims=True) + 1e-05)
        x = x * inv
        unit[win_at] = x.reshape(step_wins, WIN, WIN, C)
        inv_std[at] = inv
        n = (x * gain_ref[...] + offset_ref[...]).astype(BF16)
        nt_s[0:C, at] = n.T
        q_s[at] = ((mul(n, w_s[0]) + b_s[0]) * HEAD ** (-0.5)).astype(BF16)
        k_s[at] = (mul(n, w_s[1]) + b_s[1]).astype(BF16)
        v_s[at] = (mul(n, w_s[2]) + b_s[2]).astype(BF16)
        g = gradf[win_at].reshape(step, C).astype(BF16)
        gb_s[at] = g
        da_s[at] = mul(g, pw_s[...], NT).astype(BF16)

        first = b * step_wins
        score_step(first, 2)
        for w in range(first, first + step_wins, 2):
            softmax_step(w, 2)
            if w + 2 < first + step_wins:
                score_step(w + 2, 2)
            spread_step(w, 2)

        x = unit[win_at].reshape(step, C)
        dn = mul(dq_s[at], w_s[0], NT) + mul(dk_s[at], w_s[1], NT) + mul(dv_s[at], w_s[2], NT)
        sums[0:1, 0:C] += jnp.sum(dn * x, 0, keepdims=True)
        sums[1:2, 0:C] += jnp.sum(dn, 0, keepdims=True)
        g = dn * gain_ref[...]
        dx = inv_std[at] * (
            g - jnp.mean(g, -1, keepdims=True) - x * jnp.mean(g * x, -1, keepdims=True)
        )
        out = (gradf[win_at].reshape(step, C) + dx).reshape(step_wins, WIN, WIN, C)
        for r in range(SHIFT):
            frame_low[r, cols] = out[:, r].reshape(span_cols, C).astype(BF16)
        for r in range(0, SHIFT, 2):
            two = [out[:, SHIFT + r + i].reshape(span_cols, C) for i in range(2)]
            frame_two[r // 2, cols] = jnp.concatenate(two, 1).astype(BF16)
        back(frame_two.at[0:2, cols], back_u.at[0:2, cols], down, col)
        if b == steps - 1:
            back(frame_low.at[0:SHIFT, edge:tile_cols], back_l, row, other)
            back(frame_two.at[0:2, edge:tile_cols], back_ul, down, other)

    lows = []
    for i, part in enumerate((dq_s, dk_s, dv_s)):
        product = mul(nt_s[...], part[...])
        pack[i * BLOCK : (i + 1) * BLOCK, :] = product[:, 0:LANE]
        lows.append(product[:, LANE:WIDE])
    product = mul(gb_s[...], att[...], TN)
    pack[3 * BLOCK : 3 * BLOCK + C, :] = product[:, 0:LANE]
    pack[3 * BLOCK + C : 4 * BLOCK, :] = jnp.zeros((BLOCK - C, LANE), F32)
    pack[4 * BLOCK : 5 * BLOCK, :] = lows[0] + pltpu.roll(lows[1], 64, 1)
    pack[5 * BLOCK : 6 * BLOCK, :] = lows[2]
    pack[5 * BLOCK : 5 * BLOCK + C, :] += pltpu.roll(product[:, LANE:WIDE], 64, 1)
    for h in range(HEADS):
        span_a[h * SPAN : (h + 1) * SPAN, :] = score_acc[:, h * SPAN : (h + 1) * SPAN]
    wide = jnp.concatenate(
        [span_a[pl.ds(cj, HEADS * WIN, stride=WIN), :] for cj in range(WIN)], 1
    )
    span_b[...] = split_mul(wide, fold_a[...])
    wide = jnp.concatenate(
        [span_b[pl.ds(rj, HEADS, stride=WIN), :] for rj in range(WIN)], 1
    )
    flat_sum = split_mul(wide, fold_b[...])
    sums[8 : 8 + HEADS, :] = flat_sum
    pack[small : small + 16, :] = sums[:, 0:LANE]
    pack[small + 16 : small + 32, :] = sums[:, LANE:WIDE]
    pack_low[...] = pack[...].astype(BF16)

    pair = remote(
        pack_low.at[pl.ds(pl.multiple_of(other * half, 16), half)], pair_in,
        pair_sem.at[0], pair_sem.at[1], row, other,
    )
    pair.start()
    pair.wait()
    mine = pl.ds(pl.multiple_of(col * half, 16), half)
    half_low[...] = (pack[mine] + pair_in[...].astype(F32)).astype(BF16)

    def part_copy(k):
        peer = lax.rem(row + k, rows_n)
        return remote(
            half_low.at[pl.ds(pl.multiple_of(peer * chunk, 16), chunk)], part_in.at[k],
            part_send.at[k], part_recv.at[k], peer, col,
        )

    @pl.loop(1, rows_n)
    def _(k):
        part_copy(k).start()

    for copy in backs:
        copy.wait()
    for r in range(WIN):
        if r < SHIFT:
            lanes = slice((r % 2) * C, (r % 2 + 1) * C)
            left_part = back_ul[r // 2].astype(F32)[:, lanes]
            main_part = back_u[r // 2].astype(F32)[:, lanes]
        else:
            left_part, main_part = back_l[r - SHIFT], frame_low[r - SHIFT]
        wide = jnp.concatenate([left_part.astype(F32), main_part.astype(F32)], 0)
        d_tok[r] = wide[EDGE - SHIFT : EDGE - SHIFT + tile_cols].astype(BF16)

    def add_part(k, total):
        part_copy(k).wait()
        return total + part_in[k].astype(F32)

    my_chunk = pl.ds(pl.multiple_of(row * chunk, 16), chunk)
    total = lax.fori_loop(1, rows_n, add_part, half_low[my_chunk].astype(F32))
    own_chunk = result.at[col, my_chunk]
    own_chunk[...] = total.astype(BF16)

    def all_copy(k):
        return remote(
            own_chunk, own_chunk, all_send.at[k], all_recv.at[k],
            lax.rem(row + k, rows_n), col,
        )

    def forward(k):
        source = lax.rem(row + rows_n - k, rows_n)
        piece = result.at[col, pl.ds(pl.multiple_of(source * chunk, 16), chunk)]
        return remote(piece, piece, fwd_send.at[k], fwd_recv.at[k], row, other)

    @pl.loop(1, rows_n)
    def _(k):
        all_copy(k).start()

    forward(0).start()

    @pl.loop(1, rows_n)
    def _(k):
        all_copy(k).wait()
        forward(k).start()

    @pl.loop(0, rows_n)
    def _(k):
        forward(k).wait()

    done = jnp.concatenate([result[0], result[1]], 0)
    blocks = [done[i * BLOCK : (i + 1) * BLOCK] for i in range(6)]
    joined = jnp.concatenate([blocks[i] for i in (0, 1, 2, 4, 5)], 1)
    product = mul(joined, pick_s[...]) * out_scale
    d_qkvw[...] = product[0:C]
    d_qkvb[...] = product[C : C + 1]
    spread = e_s[...]
    far = pltpu.roll(spread[:, LANE:WIDE].astype(F32), 64, 1).astype(BF16)
    product = mul(spread[:, 0:LANE], blocks[3], NT) + mul(far, blocks[5], NT)
    d_projw[...] = product[:, 0:C] * out_scale
    tail = done[small : small + 32].astype(F32) * out_scale
    tail = jnp.concatenate([tail[0:16], tail[16:32]], 1)
    d_gain[...] = tail[0:1, 0:C]
    d_offset[...] = tail[1:2, 0:C]
    entries = table_spread(d_table.shape[1])
    d_table[...] = exact(tail[8 : 8 + HEADS, :], entries, NT)


def finish(qkvw, qkvb, projw, table, gain, offset, *rest):
    outs, flat, sems = rest[0:6], rest[6], rest[7]
    flat[...] = qkvb[...].reshape(qkvb.shape[1])
    sources = (qkvw, flat, projw, table, gain, offset)
    copies = [
        pltpu.make_async_copy(src, dst, sems.at[i]) for i, (src, dst) in enumerate(zip(sources, outs))
    ]
    for copy in copies:
        copy.start()
    for copy in copies:
        copy.wait()


def on_device(
    tokens, grad_out, regions, ln_gain, ln_offset, qkv_weight, qkv_bias, proj_weight, bias_table
):
    rows_n, cols_n = lax.axis_size("row"), lax.axis_size("col")
    tile_cols = tokens.shape[1]
    wins = tile_cols // WIN
    count = wins * SPAN
    steps = wins // 4
    unit_rows = 2 * 16 * rows_n
    needed = 6 * BLOCK + 32
    rows_total = -(-needed // unit_rows) * unit_rows
    half = rows_total // 2
    chunk = half // rows_n
    total_tokens = tokens.shape[0] * tile_cols * rows_n * cols_n
    vmem = pltpu.VMEM
    halo = [
        vmem((SHIFT, tile_cols, 2 * C), BF16),
        vmem((SHIFT, EDGE, 2 * C), BF16),
        vmem((SHIFT, EDGE, 2 * C), BF16),
    ]
    home = [
        vmem((SHIFT, tile_cols, C), BF16),
        vmem((2, tile_cols, 2 * C), BF16),
        vmem((2, tile_cols, 2 * C), BF16),
        vmem((SHIFT, EDGE, C), BF16),
        vmem((2, EDGE, 2 * C), BF16),
    ]
    flat_low = vmem((count, WIDE), BF16)
    whole = pl.BlockSpec(memory_space=pltpu.VMEM)
    dma = pltpu.SemaphoreType.DMA
    outs = pl.pallas_call(
        functools.partial(body, rows_n, cols_n, rows_total, total_tokens ** (-0.5)),
        out_shape=(
            jax.ShapeDtypeStruct(tokens.shape, BF16),
            jax.ShapeDtypeStruct((C, 3 * C), F32),
            jax.ShapeDtypeStruct((1, 3 * C), F32),
            jax.ShapeDtypeStruct((C, C), F32),
            jax.ShapeDtypeStruct((HEADS, bias_table.shape[0]), F32),
            jax.ShapeDtypeStruct((1, C), F32),
            jax.ShapeDtypeStruct((1, C), F32),
        ),
        in_specs=[whole] * 2 + [pl.BlockSpec(memory_space=pl.ANY)] * 6,
        out_specs=(whole,) * 7,
        scratch_shapes=halo + [
            vmem(regions.shape, jnp.int32),
            vmem(regions.shape, jnp.int32),
            vmem((wins, WIN, WIN, C), F32),
            vmem((count, 1), F32),
            vmem((wins, WIN, WIN, C), F32),
            vmem((192, count), BF16),
        ] + [flat_low] * 4 + [vmem((count, C), BF16)] + [flat_low] * 4 + [
            vmem((3, C, WIDE), BF16),
            vmem((3, 1, WIDE), F32),
            vmem((WIDE, C), BF16),
            vmem((C, WIDE), BF16),
            vmem((5 * LANE, 3 * C), BF16),
            vmem((SPAN, LANES), F32),
            vmem((HEADS * SPAN, SPAN), F32),
            vmem((HEADS * WIN, 128), F32),
            vmem((4 * 16, LANE), BF16),
            vmem((wins, SPAN, 128), F32),
            vmem((wins, LANE), F32),
            vmem((SPAN, LANES), F32),
            vmem((16, WIDE), F32),
            vmem((wins, SPAN, LANES), F32),
            vmem((wins, SPAN, LANES), F32),
            vmem((wins, SPAN, LANES), BF16),
            vmem((wins, SPAN, LANES), BF16),
            vmem((WIN * SPAN, 128), BF16),
            vmem((WIN * 128, 256), BF16),
        ] + home + [
            vmem((rows_total, LANE), F32),
            vmem((rows_total, LANE), BF16),
            vmem((half, LANE), BF16),
            vmem((half, LANE), BF16),
            vmem((rows_n, chunk, LANE), BF16),
            vmem((2, half, LANE), BF16),
            vmem((1, C), F32), vmem((1, C), F32), vmem(qkv_weight.shape, BF16), vmem((3 * C,), F32),
            vmem(proj_weight.shape, BF16), vmem(bias_table.shape[::-1], F32), dma((6,)),
            dma((4 + steps,)), dma((4 + steps,)),
            dma((steps + 2,)), dma((steps + 2,)), dma((2,)),
            dma((rows_n,)), dma((rows_n,)), dma((rows_n,)), dma((rows_n,)),
            dma((rows_n,)), dma((rows_n,)),
        ],
        compiler_params=pltpu.CompilerParams(
            collective_id=0, has_side_effects=True, vmem_limit_bytes=48 * 1024 * 1024
        ),
    )(
        jnp.concatenate([tokens, grad_out], -1), regions, ln_gain.reshape(1, C), ln_offset.reshape(1, C), qkv_weight,
        qkv_bias, proj_weight, bias_table.T,
    )
    d_tokens = outs[0]
    shapes = [jax.ShapeDtypeStruct(x.shape, F32) for x in outs[1:]]
    shapes[1] = jax.ShapeDtypeStruct((3 * C,), F32)
    anywhere = pl.BlockSpec(memory_space=pl.ANY)
    d_qkvw, d_qkvb, d_projw, d_table, d_gain, d_offset = pl.pallas_call(
        finish,
        out_shape=shapes,
        in_specs=[whole] * 6,
        out_specs=[anywhere] * 6,
        scratch_shapes=[vmem((3 * C,), F32), dma((6,))],
        compiler_params=pltpu.CompilerParams(vmem_limit_bytes=1024 * 1024),
    )(*outs[1:])
    return (
        d_tokens,
        d_qkvw,
        d_qkvb,
        d_projw,
        d_table.T,
        d_gain.reshape(C),
        d_offset.reshape(C),
    )


def solution(mesh):
    placed = (
        P(("grp", "row"), "col", None),
        P(("grp", "row"), "col", None),
        P(("grp", "row"), "col"),
        P(),
        P(),
        P(),
        P(),
        P(),
        P(),
    )
    return jax.shard_map(
        on_device,
        mesh=mesh,
        in_specs=placed,
        out_specs=(
            P(("grp", "row"), "col", None),
            P("grp", None),
            P("grp"),
            P("grp", None),
            P("grp", None),
            P("grp"),
            P("grp"),
        ),
        check_vma=False,
    )
```

```python
import functools

import jax
import jax.numpy as jnp
from jax import lax
from jax.experimental import pallas as pl
from jax.experimental.pallas import tpu as pltpu
from jax.sharding import PartitionSpec as P

HEADS = 6
WIN = 8
SHIFT = 4
SPAN = WIN * WIN
C = 180
HEAD = C // HEADS
LANES = HEADS * SPAN
BLOCK = 192
LANE = 128
WIDE = 2 * LANE
HEADW = 32
EDGE = 16
MASKED = -10000.0
MESH = pl.DeviceIdType.MESH
F32 = jnp.float32
BF16 = jnp.bfloat16

NN = (((1,), (0,)), ((), ()))
NT = (((1,), (1,)), ((), ()))
TN = (((0,), (0,)), ((), ()))


def mul(left, right, form=NN):
    return lax.dot_general(left, right, form, preferred_element_type=F32)


def exact(left, right, form=NN):
    return lax.dot_general(
        left, right, form, preferred_element_type=F32, precision=lax.Precision.HIGHEST
    )


def split_mul(left, picks):
    high = left.astype(BF16)
    low = (left - high.astype(F32)).astype(BF16)
    return mul(high, picks) + mul(low, picks)


def iota(shape, dim):
    return lax.broadcasted_iota(jnp.int32, shape, dim)


def col_spread(cj):
    src = iota((SPAN, 128), 0)
    dst = iota((SPAN, 128), 1)
    return (dst == (src >> 3) * 16 + (src & 7) - cj + 7).astype(F32)


def row_spread(rj):
    src = iota((128, 256), 0)
    dst = iota((128, 256), 1)
    return (dst == src + 16 * (7 - rj)).astype(F32)


def table_spread(entries):
    src = iota((entries, 256), 0)
    dst = iota((entries, 256), 1)
    hit = (src == (dst >> 4) * 15 + (dst & 15)) & ((dst & 15) < 15) & (dst < 240)
    return hit.astype(F32)


def head_spread():
    src = iota((C, WIDE), 0)
    lane = iota((1, WIDE), 1)
    head, place = lane >> 5, lane & (HEADW - 1)
    wanted = jnp.where((place < HEAD) & (head < HEADS), head * HEAD + place, -1)
    return (src == wanted).astype(F32).astype(BF16)


def part_pick():
    lane = iota((1, 3 * C), 1)
    part = (lane >= C).astype(jnp.int32) + (lane >= 2 * C).astype(jnp.int32)
    place = lane - part * C
    head = sum((place >= t * HEAD).astype(jnp.int32) for t in range(1, HEADS))
    place = place - head * HEAD
    near = part * LANE + head * HEADW + place
    far = 3 * LANE + (part >> 1) * LANE + (part & 1) * 64 + (head - 4) * HEADW + place
    wanted = jnp.where(head < 4, near, far)
    return (iota((5 * LANE, 3 * C), 0) == wanted).astype(F32).astype(BF16)


def window_steps(wins):
    return [(w, 4) for w in range(wins - 4, 0, -4)] + [(2, 2), (0, 2)]


def body(
    rows_n, cols_n, rows_total, out_scale,
    both, reg, gain_in, offset_in, qkvw_in, qkvb_in, projw_in, table_in,
    d_tok, d_qkvw, d_qkvb, d_projw, d_table, d_gain, d_offset,
    both_b, both_r, both_d, reg_b, reg_r,
    unit, inv_std, gradf, nt_s, q_s, k_s, v_s, da_s, gb_s, att, dq_s, dk_s, dv_s,
    w_s, b_s, pw_s, e_s, pick_s, bias_t, span_a, span_b, hmask, lab_col, lab_row, score_acc, sums,
    scores_s, dp_s, p_s, ds_s, grads, turned,
    fold_a, fold_b, frame_low, frame_two, back_u, back_l, back_ul,
    pack, pack_low, pair_in, half_low, part_in, result,
    gain_ref, offset_ref, qkvw, qkvb, projw, table, local_sem,
    halo_send, halo_recv, back_send, back_recv, pair_sem,
    part_send, part_recv, all_send, all_recv, fwd_send, fwd_recv,
):
    row = lax.axis_index("row")
    col = lax.axis_index("col")
    up = lax.rem(row + rows_n - 1, rows_n)
    down = lax.rem(row + 1, rows_n)
    other = lax.rem(col + 1, cols_n)
    tile_cols = both.shape[1]
    wins = tile_cols // WIN
    count = wins * SPAN
    half = rows_total // 2
    chunk = half // rows_n

    def remote(src, dst, send, recv, to_row, to_col):
        return pltpu.make_async_remote_copy(
            src_ref=src, dst_ref=dst, send_sem=send, recv_sem=recv,
            device_id={"row": to_row, "col": to_col}, device_id_type=MESH,
        )

    locals_ = [
        pltpu.make_async_copy(src, dst, local_sem.at[i])
        for i, (src, dst) in enumerate((
            (table_in, table), (gain_in, gain_ref), (offset_in, offset_ref),
            (qkvw_in, qkvw), (qkvb_in, qkvb), (projw_in, projw),
        ))
    ]
    for copy in locals_:
        copy.start()
    barrier = pltpu.get_barrier_semaphore()

    @pl.loop(1, rows_n)
    def _(k):
        pl.semaphore_signal(
            barrier, inc=1, device_id={"row": lax.rem(row + k, rows_n), "col": col},
            device_id_type=MESH,
        )

    for to_row in (row, up, down):
        pl.semaphore_signal(
            barrier, inc=1, device_id={"row": to_row, "col": other}, device_id_type=MESH
        )
    pl.semaphore_wait(barrier, rows_n + 2)

    plan = window_steps(wins)
    steps = len(plan)

    def halo(i, src, dst, to_row, to_col):
        return remote(src, dst, halo_send.at[i], halo_recv.at[i], to_row, to_col)

    labels = [halo(0, reg, reg_b, down, col), halo(1, reg, reg_r, row, other)]
    sides = [
        halo(2, both.at[0:SHIFT, 0:EDGE], both_r, row, other),
    ]
    corner = halo(3, both.at[SHIFT:WIN, 0:EDGE], both_b.at[0:SHIFT, 0:EDGE], down, col)
    corner_on = halo(4, both_b.at[0:SHIFT, 0:EDGE], both_d, row, other)
    chunks = []
    for b, (w0, n) in enumerate(plan):
        cols = slice(w0 * WIN, (w0 + n) * WIN)
        chunks.append([halo(5 + b, both.at[SHIFT:WIN, cols], both_b.at[0:SHIFT, cols], down, col)] if w0 else [])
    ahead = 9
    small = 6 * BLOCK
    for copy in labels + [corner] + sides + sum(chunks[:ahead], []):
        copy.start()

    for copy in locals_:
        copy.wait()
    flat = exact(table[...], table_spread(table.shape[1]))
    for rj in range(WIN):
        span_b[pl.ds(rj, HEADS, stride=WIN), :] = exact(flat, row_spread(rj), NT)
    for cj in range(WIN):
        span_a[pl.ds(cj, HEADS * WIN, stride=WIN), :] = exact(span_b[...], col_spread(cj), NT)
    for h in range(HEADS):
        bias_t[:, h * SPAN : (h + 1) * SPAN] = span_a[h * SPAN : (h + 1) * SPAN, :]
    mask_row = iota((4 * 16, LANE), 0) >> 4
    hmask[...] = ((iota((4 * 16, LANE), 1) >> 5) == mask_row).astype(F32).astype(BF16)
    e_s[...] = head_spread()
    pick_s[...] = part_pick()
    score_acc[...] = jnp.zeros_like(score_acc)
    sums[...] = jnp.zeros_like(sums)
    pack[small:] = jnp.zeros_like(pack[small:])

    nt_s[...] = jnp.ones_like(nt_s)
    for cj in range(WIN):
        fold_a[cj * SPAN : (cj + 1) * SPAN, :] = col_spread(cj).astype(BF16)
    for rj in range(WIN):
        fold_b[rj * 128 : (rj + 1) * 128, :] = row_spread(rj).astype(BF16)
    weights = qkvw[...]
    offsets = qkvb[...].reshape(1, 3 * C)
    for i in range(3):
        w_s[i] = mul(weights[:, i * C : (i + 1) * C], e_s[...]).astype(BF16)
        b_s[i] = exact(offsets[:, i * C : (i + 1) * C], e_s[...].astype(F32))
    pw_s[...] = mul(e_s[...], projw[...], TN).astype(BF16)

    for copy in labels:
        copy.wait()

    own = reg[...]
    row_part = jnp.concatenate([reg_b[SHIFT:, :], own[0:SHIFT]], 0)[:, 0:1] >> 2
    col_own = pltpu.roll(own, tile_cols - SHIFT, 1)
    col_right = pltpu.roll(reg_r[...], tile_cols - SHIFT, 1)
    col_part = jnp.where(iota((WIN, tile_cols), 1) < tile_cols - SHIFT, col_own, col_right)[0:1] & 3
    label = (row_part * 4 + col_part).astype(F32)
    spread = jnp.broadcast_to(label[:, None, :], (WIN, WIN, tile_cols)).reshape(SPAN, tile_cols)
    spread = jnp.where(
        (iota((SPAN, tile_cols), 0) & 7) == (iota((SPAN, tile_cols), 1) & 7), spread, 0.0
    )
    pick = ((iota((tile_cols, wins), 0) >> 3) == iota((tile_cols, wins), 1)).astype(F32)
    columns = exact(spread, pick)
    tiled = (iota((SPAN, LANE), 0) == (iota((SPAN, LANE), 1) & (SPAN - 1))).astype(F32)
    lab_row[...] = exact(columns, tiled, TN)
    for w in range(wins):
        lab_col[w] = jnp.broadcast_to(columns[:, w : w + 1], (SPAN, 128))

    lane = iota((SPAN, LANE), 1)

    def gather_heads(stacked):
        out = stacked[-SPAN:]
        for h in range(stacked.shape[0] // SPAN - 2, -1, -1):
            out = jnp.where(lane < (h + 1) * HEADW, stacked[h * SPAN : (h + 1) * SPAN], out)
        return out

    def diagonal(x, heads):
        tiles = x.reshape(SPAN // 16, 16, LANE)
        parts = [
            (tiles * hmask[h * 16 : (h + 1) * 16, :][None]).reshape(SPAN, LANE) for h in range(heads)
        ]
        return jnp.concatenate(parts, 0)

    groups = ((slice(0, LANE), slice(0, 4 * SPAN), 4), (slice(LANE, WIDE), slice(4 * SPAN, LANES), 2))

    def score_step(w0, n):
        for w in range(w0, w0 + n):
            at = slice(w * SPAN, (w + 1) * SPAN)
            for lanes, cut, heads in groups:
                scores_s[w, :, cut] = mul(k_s[at, lanes], diagonal(q_s[at, lanes], heads), NT)
                dp_s[w, :, cut] = mul(v_s[at, lanes], diagonal(da_s[at, lanes], heads), NT)

    def softmax_step(w0, n):
        for w in range(w0, w0 + n):
            same = lab_col[w] == lab_row[w : w + 1, :]
            for t in range(HEADS // 2):
                cut = slice(t * LANE, (t + 1) * LANE)
                scores = jnp.where(same, scores_s[w, :, cut] + bias_t[:, cut], MASKED)
                e = jnp.exp(scores - jnp.max(scores, 0, keepdims=True))
                p = e * (1.0 / jnp.sum(e, 0, keepdims=True))
                p_s[w, :, cut] = p.astype(BF16)
                dp = dp_s[w, :, cut]
                ds = p * (dp - jnp.sum(p * dp, 0, keepdims=True))
                score_acc[:, cut] += ds
                ds_s[w, :, cut] = ds.astype(BF16)

    def spread_step(w0, n):
        for w in range(w0, w0 + n):
            at = slice(w * SPAN, (w + 1) * SPAN)
            for lanes, cut, heads in groups:
                p, ds = p_s[w, :, cut], ds_s[w, :, cut]
                att[at, lanes] = gather_heads(mul(p, v_s[at, lanes], TN)).astype(BF16)
                dq = gather_heads(mul(ds, k_s[at, lanes], TN))
                dq_s[at, lanes] = (dq * HEAD ** (-0.5)).astype(BF16)
                dk_s[at, lanes] = mul(ds, diagonal(q_s[at, lanes], heads)).astype(BF16)
                dv_s[at, lanes] = mul(p, diagonal(da_s[at, lanes], heads)).astype(BF16)

    edge = tile_cols - EDGE
    backs = []

    def back(src, dst, to_row, to_col):
        i = len(backs)
        backs.append(remote(src, dst, back_send.at[i], back_recv.at[i], to_row, to_col))
        backs[-1].start()

    corner.wait()
    corner_on.start()
    waiting = []
    for b, (w0, step_wins) in enumerate(plan):
        for copy in chunks[b] + ([] if b else sides + [corner_on]):
            copy.wait()
        if b + ahead < steps:
            for copy in chunks[b + ahead]:
                copy.start()
        if b >= 2:
            for copy in waiting:
                back(*copy)
            waiting = []
        step, span_cols, end = step_wins * SPAN, step_wins * WIN, w0 + step_wins
        at = slice(w0 * SPAN, end * SPAN)
        win_at = slice(w0, end)
        cols = slice(w0 * WIN, end * WIN)
        near = slice(w0 * WIN, min(end * WIN + EDGE, tile_cols))

        for r in range(WIN):
            if r < SHIFT:
                part, beyond = both_b[r, near], both_d[r]
            else:
                part, beyond = both[r - SHIFT, near], both_r[r - SHIFT]
            wide = part.astype(F32)
            if end == wins:
                wide = jnp.concatenate([wide, beyond.astype(F32)], 0)
            wide = wide[SHIFT : SHIFT + span_cols]
            unit[win_at, r] = wide[:, 0:C].reshape(step_wins, WIN, C)
            gradf[win_at, r] = wide[:, C : 2 * C].reshape(step_wins, WIN, C)

        x = unit[win_at].reshape(step, C)
        center = jnp.mean(x, -1, keepdims=True)
        x = x - center
        inv = lax.rsqrt(jnp.mean(x * x, -1, keepdims=True) + 1e-05)
        x = x * inv
        unit[win_at] = x.reshape(step_wins, WIN, WIN, C)
        inv_std[at] = inv
        n = (x * gain_ref[...] + offset_ref[...]).astype(BF16)
        nt_s[0:C, at] = n.T
        q_s[at] = ((mul(n, w_s[0]) + b_s[0]) * HEAD ** (-0.5)).astype(BF16)
        k_s[at] = (mul(n, w_s[1]) + b_s[1]).astype(BF16)
        v_s[at] = (mul(n, w_s[2]) + b_s[2]).astype(BF16)
        g = gradf[win_at].reshape(step, C).astype(BF16)
        gb_s[at] = g
        da_s[at] = mul(g, pw_s[...], NT).astype(BF16)

        score_step(w0, 2)
        for w in range(w0, end, 2):
            softmax_step(w, 2)
            if w + 2 < end:
                score_step(w + 2, 2)
            spread_step(w, 2)

        x = unit[win_at].reshape(step, C)
        dn = mul(dq_s[at], w_s[0], NT) + mul(dk_s[at], w_s[1], NT) + mul(dv_s[at], w_s[2], NT)
        sums[0:1, 0:C] += jnp.sum(dn * x, 0, keepdims=True)
        sums[1:2, 0:C] += jnp.sum(dn, 0, keepdims=True)
        g = dn * gain_ref[...]
        dx = inv_std[at] * (
            g - jnp.mean(g, -1, keepdims=True) - x * jnp.mean(g * x, -1, keepdims=True)
        )
        out = (gradf[win_at].reshape(step, C) + dx).reshape(step_wins, WIN, WIN, C)
        for r in range(SHIFT):
            frame_low[r, cols] = out[:, SHIFT + r].reshape(span_cols, C).astype(BF16)
        for r in range(0, SHIFT, 2):
            two = [out[:, r + i].reshape(span_cols, C) for i in range(2)]
            frame_two[r // 2, cols] = jnp.concatenate(two, 1).astype(BF16)
        waiting.append((frame_two.at[0:2, cols], back_u.at[0:2, cols], up, col))
        if b == 0:
            waiting.append((frame_low.at[0:SHIFT, edge:tile_cols], back_l, row, other))
            waiting.append((frame_two.at[0:2, edge:tile_cols], back_ul, up, other))
        if w0 != 2:
            over = slice(w0 * SPAN, w0 * SPAN + 4 * SPAN)
            for i, part in enumerate((dq_s, dk_s, dv_s)):
                product = mul(nt_s[:, over], part[over])
                grads[i] = product if b == 0 else grads[i] + product
            product = mul(gb_s[over], att[over], TN)
            grads[3, 0:C] = product if b == 0 else grads[3, 0:C] + product
    for copy in waiting:
        back(*copy)

    for i in range(3):
        pack[i * BLOCK : (i + 1) * BLOCK, :] = grads[i, :, 0:LANE]
    pack[3 * BLOCK : 3 * BLOCK + C, :] = grads[3, 0:C, 0:LANE]
    pack[3 * BLOCK + C : 4 * BLOCK, :] = jnp.zeros((BLOCK - C, LANE), F32)
    pack[4 * BLOCK : 5 * BLOCK, :] = grads[0, :, LANE:WIDE] + pltpu.roll(grads[1, :, LANE:WIDE], 64, 1)
    pack[5 * BLOCK : 6 * BLOCK, :] = grads[2, :, LANE:WIDE]
    pack[5 * BLOCK : 5 * BLOCK + C, :] += pltpu.roll(grads[3, 0:C, LANE:WIDE], 64, 1)
    for h in range(HEADS):
        span_a[h * SPAN : (h + 1) * SPAN, :] = score_acc[:, h * SPAN : (h + 1) * SPAN]
    wide = jnp.concatenate(
        [span_a[pl.ds(cj, HEADS * WIN, stride=WIN), :] for cj in range(WIN)], 1
    )
    span_b[...] = split_mul(wide, fold_a[...])
    wide = jnp.concatenate(
        [span_b[pl.ds(rj, HEADS, stride=WIN), :] for rj in range(WIN)], 1
    )
    flat_sum = split_mul(wide, fold_b[...])
    sums[8 : 8 + HEADS, :] = flat_sum
    pack[small : small + 16, :] = sums[:, 0:LANE]
    pack[small + 16 : small + 32, :] = sums[:, LANE:WIDE]
    pack_low[...] = pack[...].astype(BF16)

    pair = remote(
        pack_low.at[pl.ds(pl.multiple_of(other * half, 16), half)], pair_in,
        pair_sem.at[0], pair_sem.at[1], row, other,
    )
    pair.start()
    pair.wait()
    mine = pl.ds(pl.multiple_of(col * half, 16), half)
    half_low[...] = (pack[mine] + pair_in[...].astype(F32)).astype(BF16)

    def part_copy(k):
        peer = lax.rem(row + k, rows_n)
        return remote(
            half_low.at[pl.ds(pl.multiple_of(peer * chunk, 16), chunk)], part_in.at[k],
            part_send.at[k], part_recv.at[k], peer, col,
        )

    @pl.loop(1, rows_n)
    def _(k):
        part_copy(k).start()

    def add_part(k, total):
        part_copy(k).wait()
        return total + part_in[k].astype(F32)

    my_chunk = pl.ds(pl.multiple_of(row * chunk, 16), chunk)
    total = lax.fori_loop(1, rows_n, add_part, half_low[my_chunk].astype(F32))
    own_chunk = result.at[col, my_chunk]
    own_chunk[...] = total.astype(BF16)

    def all_copy(k):
        return remote(
            own_chunk, own_chunk, all_send.at[k], all_recv.at[k],
            lax.rem(row + k, rows_n), col,
        )

    def forward(k):
        source = lax.rem(row + rows_n - k, rows_n)
        piece = result.at[col, pl.ds(pl.multiple_of(source * chunk, 16), chunk)]
        return remote(piece, piece, fwd_send.at[k], fwd_recv.at[k], row, other)

    @pl.loop(1, rows_n)
    def _(k):
        all_copy(k).start()

    forward(0).start()

    for copy in backs:
        copy.wait()
    for r in range(WIN):
        if r < SHIFT:
            left_part, main_part = back_l[r], frame_low[r]
        else:
            lanes = slice((r % 2) * C, (r % 2 + 1) * C)
            left_part = back_ul[(r - SHIFT) // 2].astype(F32)[:, lanes]
            main_part = back_u[(r - SHIFT) // 2].astype(F32)[:, lanes]
        wide = jnp.concatenate([left_part.astype(F32), main_part.astype(F32)], 0)
        turned[pl.ds(r, C, stride=WIN), :] = wide[EDGE - SHIFT : EDGE - SHIFT + tile_cols].T
    d_tok[...] = turned[...].reshape(C, WIN, tile_cols).astype(BF16)


    @pl.loop(1, rows_n)
    def _(k):
        all_copy(k).wait()
        forward(k).start()

    @pl.loop(0, rows_n)
    def _(k):
        forward(k).wait()

    done = jnp.concatenate([result[0], result[1]], 0)
    blocks = [done[i * BLOCK : (i + 1) * BLOCK] for i in range(6)]
    joined = jnp.concatenate([blocks[i] for i in (0, 1, 2, 4, 5)], 1)
    product = mul(joined, pick_s[...]) * out_scale
    d_qkvw[...] = product[0:C]
    d_qkvb[...] = product[C : C + 1]
    spread = e_s[...]
    far = pltpu.roll(spread[:, LANE:WIDE].astype(F32), 64, 1).astype(BF16)
    product = mul(spread[:, 0:LANE], blocks[3], NT) + mul(far, blocks[5], NT)
    d_projw[...] = product[:, 0:C] * out_scale
    tail = done[small : small + 32].astype(F32) * out_scale
    tail = jnp.concatenate([tail[0:16], tail[16:32]], 1)
    d_gain[...] = tail[0:1, 0:C]
    d_offset[...] = tail[1:2, 0:C]
    entries = table_spread(d_table.shape[1])
    d_table[...] = exact(tail[8 : 8 + HEADS, :], entries, NT)


def finish(tok, qkvw, qkvb, projw, table, gain, offset, *rest):
    outs, flat, sems = rest[0:7], rest[7], rest[8]
    flat[...] = qkvb[...].reshape(qkvb.shape[1])
    sources = (tok, qkvw, flat, projw, table, gain, offset)
    copies = [
        pltpu.make_async_copy(src, dst, sems.at[i]) for i, (src, dst) in enumerate(zip(sources, outs))
    ]
    for copy in copies:
        copy.start()
    for copy in copies:
        copy.wait()


def on_device(
    tokens, grad_out, regions, ln_gain, ln_offset, qkv_weight, qkv_bias, proj_weight, bias_table
):
    rows_n, cols_n = lax.axis_size("row"), lax.axis_size("col")
    tile_cols = tokens.shape[1]
    wins = tile_cols // WIN
    count = wins * SPAN
    steps = len(window_steps(wins))
    unit_rows = 2 * 16 * rows_n
    needed = 6 * BLOCK + 32
    rows_total = -(-needed // unit_rows) * unit_rows
    half = rows_total // 2
    chunk = half // rows_n
    total_tokens = tokens.shape[0] * tile_cols * rows_n * cols_n
    vmem = pltpu.VMEM
    halo = [
        vmem((SHIFT, tile_cols, 2 * C), BF16),
        vmem((SHIFT, EDGE, 2 * C), BF16),
        vmem((SHIFT, EDGE, 2 * C), BF16),
    ]
    home = [
        vmem((SHIFT, tile_cols, C), BF16),
        vmem((2, tile_cols, 2 * C), BF16),
        vmem((2, tile_cols, 2 * C), BF16),
        vmem((SHIFT, EDGE, C), BF16),
        vmem((2, EDGE, 2 * C), BF16),
    ]
    flat_low = vmem((count, WIDE), BF16)
    whole = pl.BlockSpec(memory_space=pltpu.VMEM)
    dma = pltpu.SemaphoreType.DMA
    outs = pl.pallas_call(
        functools.partial(body, rows_n, cols_n, rows_total, total_tokens ** (-0.5)),
        out_shape=(
            jax.ShapeDtypeStruct((C,) + tokens.shape[:2], BF16),
            jax.ShapeDtypeStruct((C, 3 * C), F32),
            jax.ShapeDtypeStruct((1, 3 * C), F32),
            jax.ShapeDtypeStruct((C, C), F32),
            jax.ShapeDtypeStruct((HEADS, bias_table.shape[0]), F32),
            jax.ShapeDtypeStruct((1, C), F32),
            jax.ShapeDtypeStruct((1, C), F32),
        ),
        in_specs=[whole] * 2 + [pl.BlockSpec(memory_space=pl.ANY)] * 6,
        out_specs=(whole,) * 7,
        scratch_shapes=halo + [
            vmem(regions.shape, jnp.int32),
            vmem(regions.shape, jnp.int32),
            vmem((wins, WIN, WIN, C), F32),
            vmem((count, 1), F32),
            vmem((wins, WIN, WIN, C), F32),
            vmem((192, count), BF16),
        ] + [flat_low] * 4 + [vmem((count, C), BF16)] + [flat_low] * 4 + [
            vmem((3, C, WIDE), BF16),
            vmem((3, 1, WIDE), F32),
            vmem((WIDE, C), BF16),
            vmem((C, WIDE), BF16),
            vmem((5 * LANE, 3 * C), BF16),
            vmem((SPAN, LANES), F32),
            vmem((HEADS * SPAN, SPAN), F32),
            vmem((HEADS * WIN, 128), F32),
            vmem((4 * 16, LANE), BF16),
            vmem((wins, SPAN, 128), F32),
            vmem((wins, LANE), F32),
            vmem((SPAN, LANES), F32),
            vmem((16, WIDE), F32),
            vmem((wins, SPAN, LANES), F32),
            vmem((wins, SPAN, LANES), F32),
            vmem((wins, SPAN, LANES), BF16),
            vmem((wins, SPAN, LANES), BF16),
            vmem((4, BLOCK, WIDE), F32),
            vmem((C * WIN, tile_cols), F32),
            vmem((WIN * SPAN, 128), BF16),
            vmem((WIN * 128, 256), BF16),
        ] + home + [
            vmem((rows_total, LANE), F32),
            vmem((rows_total, LANE), BF16),
            vmem((half, LANE), BF16),
            vmem((half, LANE), BF16),
            vmem((rows_n, chunk, LANE), BF16),
            vmem((2, half, LANE), BF16),
            vmem((1, C), F32), vmem((1, C), F32), vmem(qkv_weight.shape, BF16), vmem((3 * C,), F32),
            vmem(proj_weight.shape, BF16), vmem(bias_table.shape[::-1], F32), dma((6,)),
            dma((5 + steps,)), dma((5 + steps,)),
            dma((steps + 2,)), dma((steps + 2,)), dma((2,)),
            dma((rows_n,)), dma((rows_n,)), dma((rows_n,)), dma((rows_n,)),
            dma((rows_n,)), dma((rows_n,)),
        ],
        compiler_params=pltpu.CompilerParams(
            collective_id=0, has_side_effects=True, vmem_limit_bytes=48 * 1024 * 1024
        ),
    )(
        jnp.concatenate([tokens, grad_out], -1), regions, ln_gain.reshape(1, C), ln_offset.reshape(1, C), qkv_weight,
        qkv_bias, proj_weight, bias_table.T,
    )
    shapes = [jax.ShapeDtypeStruct(x.shape, x.dtype) for x in outs]
    shapes[2] = jax.ShapeDtypeStruct((3 * C,), F32)
    anywhere = pl.BlockSpec(memory_space=pl.ANY)
    d_tokens, d_qkvw, d_qkvb, d_projw, d_table, d_gain, d_offset = pl.pallas_call(
        finish,
        out_shape=shapes,
        in_specs=[whole] * 7,
        out_specs=[anywhere] * 7,
        scratch_shapes=[vmem((3 * C,), F32), dma((7,))],
        compiler_params=pltpu.CompilerParams(vmem_limit_bytes=1024 * 1024),
    )(*outs)
    return (
        jnp.transpose(d_tokens, (1, 2, 0)),
        d_qkvw,
        d_qkvb,
        d_projw,
        d_table.T,
        d_gain.reshape(C),
        d_offset.reshape(C),
    )


def solution(mesh):
    placed = (
        P(("grp", "row"), "col", None),
        P(("grp", "row"), "col", None),
        P(("grp", "row"), "col"),
        P(),
        P(),
        P(),
        P(),
        P(),
        P(),
    )
    return jax.shard_map(
        on_device,
        mesh=mesh,
        in_specs=placed,
        out_specs=(
            P(("grp", "row"), "col", None),
            P("grp", None),
            P("grp"),
            P("grp", None),
            P("grp", None),
            P("grp"),
            P("grp"),
        ),
        check_vma=False,
    )
```

```python
import functools

import jax
import jax.numpy as jnp
from jax import lax
from jax.experimental import pallas as pl
from jax.experimental.pallas import tpu as pltpu
from jax.sharding import PartitionSpec as P

HEADS = 6
WIN = 8
SHIFT = 4
SPAN = WIN * WIN
C = 180
HEAD = C // HEADS
LANES = HEADS * SPAN
BLOCK = 192
LANE = 128
WIDE = 2 * LANE
HEADW = 32
EDGE = 16
MASKED = -10000.0
MESH = pl.DeviceIdType.MESH
F32 = jnp.float32
BF16 = jnp.bfloat16

NN = (((1,), (0,)), ((), ()))
NT = (((1,), (1,)), ((), ()))
TN = (((0,), (0,)), ((), ()))


def mul(left, right, form=NN):
    return lax.dot_general(left, right, form, preferred_element_type=F32)


def exact(left, right, form=NN):
    return lax.dot_general(
        left, right, form, preferred_element_type=F32, precision=lax.Precision.HIGHEST
    )


def split_mul(left, picks):
    high = left.astype(BF16)
    low = (left - high.astype(F32)).astype(BF16)
    return mul(high, picks) + mul(low, picks)


def iota(shape, dim):
    return lax.broadcasted_iota(jnp.int32, shape, dim)


def col_spread(cj):
    src = iota((SPAN, 128), 0)
    dst = iota((SPAN, 128), 1)
    return (dst == (src >> 3) * 16 + (src & 7) - cj + 7).astype(F32)


def row_spread(rj):
    src = iota((128, 256), 0)
    dst = iota((128, 256), 1)
    return (dst == src + 16 * (7 - rj)).astype(F32)


def table_spread(entries):
    src = iota((entries, 256), 0)
    dst = iota((entries, 256), 1)
    hit = (src == (dst >> 4) * 15 + (dst & 15)) & ((dst & 15) < 15) & (dst < 240)
    return hit.astype(F32)


def head_spread():
    src = iota((C, WIDE), 0)
    lane = iota((1, WIDE), 1)
    head, place = lane >> 5, lane & (HEADW - 1)
    wanted = jnp.where((place < HEAD) & (head < HEADS), head * HEAD + place, -1)
    return (src == wanted).astype(F32).astype(BF16)


def part_pick():
    lane = iota((1, 3 * C), 1)
    part = (lane >= C).astype(jnp.int32) + (lane >= 2 * C).astype(jnp.int32)
    place = lane - part * C
    head = sum((place >= t * HEAD).astype(jnp.int32) for t in range(1, HEADS))
    place = place - head * HEAD
    near = part * LANE + head * HEADW + place
    far = 3 * LANE + (part >> 1) * LANE + (part & 1) * 64 + (head - 4) * HEADW + place
    wanted = jnp.where(head < 4, near, far)
    return (iota((5 * LANE, 3 * C), 0) == wanted).astype(F32).astype(BF16)


def window_steps(wins):
    return [(w, 4) for w in range(wins - 4, 0, -4)] + [(2, 2), (0, 2)]


def body(
    rows_n, cols_n, rows_total, out_scale,
    tok_in, grad_in, reg_in, gain_in, offset_in, qkvw_in, qkvb_in, projw_in, table_in,
    d_tok, d_qkvw, d_qkvb, d_projw, d_table, d_gain, d_offset,
    both, spread_t, both_b, both_r, both_d, reg_b, reg_r,
    unit, inv_std, gradf, nt_s, q_s, k_s, v_s, da_s, gb_s, att, dq_s, dk_s, dv_s,
    w_s, b_s, pw_s, e_s, pick_s, bias_t, span_a, span_b, hmask, lab_col, lab_row, score_acc, sums,
    scores_s, dp_s, p_s, ds_s, grads, turned,
    fold_a, fold_b, frame_low, frame_two, back_u, back_l, back_ul,
    pack, pack_low, pair_in, half_low, part_in, result,
    tok_t, grad_t, reg, gain_ref, offset_ref, qkvw, qkvb, projw, table, local_sem,
    halo_send, halo_recv, back_send, back_recv, pair_sem,
    part_send, part_recv, all_send, all_recv, fwd_send, fwd_recv,
):
    row = lax.axis_index("row")
    col = lax.axis_index("col")
    up = lax.rem(row + rows_n - 1, rows_n)
    down = lax.rem(row + 1, rows_n)
    other = lax.rem(col + 1, cols_n)
    tile_cols = tok_in.shape[2]
    wins = tile_cols // WIN
    count = wins * SPAN
    half = rows_total // 2
    chunk = half // rows_n

    def remote(src, dst, send, recv, to_row, to_col):
        return pltpu.make_async_remote_copy(
            src_ref=src, dst_ref=dst, send_sem=send, recv_sem=recv,
            device_id={"row": to_row, "col": to_col}, device_id_type=MESH,
        )

    locals_ = [
        pltpu.make_async_copy(src, dst, local_sem.at[i])
        for i, (src, dst) in enumerate((
            (tok_in, tok_t), (grad_in, grad_t), (reg_in, reg),
            (table_in, table), (gain_in, gain_ref), (offset_in, offset_ref),
            (qkvw_in, qkvw), (qkvb_in, qkvb), (projw_in, projw),
        ))
    ]
    for copy in locals_:
        copy.start()
    barrier = pltpu.get_barrier_semaphore()

    @pl.loop(1, rows_n)
    def _(k):
        pl.semaphore_signal(
            barrier, inc=1, device_id={"row": lax.rem(row + k, rows_n), "col": col},
            device_id_type=MESH,
        )

    for to_row in (row, up, down):
        pl.semaphore_signal(
            barrier, inc=1, device_id={"row": to_row, "col": other}, device_id_type=MESH
        )
    def turn(r):
        both[r] = spread_t[pl.ds(r, 2 * C, stride=WIN), :].T.astype(BF16)

    for copy in locals_[0:3]:
        copy.wait()
    spread_t[0 : C * WIN, :] = tok_t[...].astype(F32).reshape(C * WIN, tile_cols)
    spread_t[C * WIN : 2 * C * WIN, :] = grad_t[...].astype(F32).reshape(C * WIN, tile_cols)
    for r in range(SHIFT, WIN):
        turn(r)
    pl.semaphore_wait(barrier, rows_n + 2)

    plan = window_steps(wins)
    steps = len(plan)

    def halo(i, src, dst, to_row, to_col):
        return remote(src, dst, halo_send.at[i], halo_recv.at[i], to_row, to_col)

    labels = [halo(0, reg, reg_b, down, col), halo(1, reg, reg_r, row, other)]
    sides = [
        halo(2, both.at[0:SHIFT, 0:EDGE], both_r, row, other),
    ]
    corner = halo(3, both.at[SHIFT:WIN, 0:EDGE], both_b.at[0:SHIFT, 0:EDGE], down, col)
    corner_on = halo(4, both_b.at[0:SHIFT, 0:EDGE], both_d, row, other)
    chunks = []
    for b, (w0, n) in enumerate(plan):
        cols = slice(w0 * WIN, (w0 + n) * WIN)
        chunks.append([halo(5 + b, both.at[SHIFT:WIN, cols], both_b.at[0:SHIFT, cols], down, col)] if w0 else [])
    ahead = 9
    small = 6 * BLOCK
    for copy in labels + [corner] + sum(chunks[:ahead], []):
        copy.start()
    for r in range(SHIFT):
        turn(r)
    for copy in sides:
        copy.start()

    for copy in locals_[3:]:
        copy.wait()
    flat = exact(table[...], table_spread(table.shape[1]))
    for rj in range(WIN):
        span_b[pl.ds(rj, HEADS, stride=WIN), :] = exact(flat, row_spread(rj), NT)
    for cj in range(WIN):
        span_a[pl.ds(cj, HEADS * WIN, stride=WIN), :] = exact(span_b[...], col_spread(cj), NT)
    for h in range(HEADS):
        bias_t[:, h * SPAN : (h + 1) * SPAN] = span_a[h * SPAN : (h + 1) * SPAN, :]
    mask_row = iota((4 * 16, LANE), 0) >> 4
    hmask[...] = ((iota((4 * 16, LANE), 1) >> 5) == mask_row).astype(F32).astype(BF16)
    e_s[...] = head_spread()
    pick_s[...] = part_pick()
    score_acc[...] = jnp.zeros_like(score_acc)
    sums[...] = jnp.zeros_like(sums)
    pack[small:] = jnp.zeros_like(pack[small:])

    nt_s[...] = jnp.ones_like(nt_s)
    for cj in range(WIN):
        fold_a[cj * SPAN : (cj + 1) * SPAN, :] = col_spread(cj).astype(BF16)
    for rj in range(WIN):
        fold_b[rj * 128 : (rj + 1) * 128, :] = row_spread(rj).astype(BF16)
    weights = qkvw[...]
    offsets = qkvb[...].reshape(1, 3 * C)
    for i in range(3):
        w_s[i] = mul(weights[:, i * C : (i + 1) * C], e_s[...]).astype(BF16)
        b_s[i] = exact(offsets[:, i * C : (i + 1) * C], e_s[...].astype(F32))
    pw_s[...] = mul(e_s[...], projw[...], TN).astype(BF16)

    for copy in labels:
        copy.wait()

    own = reg[...]
    row_part = jnp.concatenate([reg_b[SHIFT:, :], own[0:SHIFT]], 0)[:, 0:1] >> 2
    col_own = pltpu.roll(own, tile_cols - SHIFT, 1)
    col_right = pltpu.roll(reg_r[...], tile_cols - SHIFT, 1)
    col_part = jnp.where(iota((WIN, tile_cols), 1) < tile_cols - SHIFT, col_own, col_right)[0:1] & 3
    label = (row_part * 4 + col_part).astype(F32)
    spread = jnp.broadcast_to(label[:, None, :], (WIN, WIN, tile_cols)).reshape(SPAN, tile_cols)
    spread = jnp.where(
        (iota((SPAN, tile_cols), 0) & 7) == (iota((SPAN, tile_cols), 1) & 7), spread, 0.0
    )
    pick = ((iota((tile_cols, wins), 0) >> 3) == iota((tile_cols, wins), 1)).astype(F32)
    columns = exact(spread, pick)
    tiled = (iota((SPAN, LANE), 0) == (iota((SPAN, LANE), 1) & (SPAN - 1))).astype(F32)
    lab_row[...] = exact(columns, tiled, TN)
    for w in range(wins):
        lab_col[w] = jnp.broadcast_to(columns[:, w : w + 1], (SPAN, 128))

    lane = iota((SPAN, LANE), 1)

    def gather_heads(stacked):
        out = stacked[-SPAN:]
        for h in range(stacked.shape[0] // SPAN - 2, -1, -1):
            out = jnp.where(lane < (h + 1) * HEADW, stacked[h * SPAN : (h + 1) * SPAN], out)
        return out

    def diagonal(x, heads):
        tiles = x.reshape(SPAN // 16, 16, LANE)
        parts = [
            (tiles * hmask[h * 16 : (h + 1) * 16, :][None]).reshape(SPAN, LANE) for h in range(heads)
        ]
        return jnp.concatenate(parts, 0)

    groups = ((slice(0, LANE), slice(0, 4 * SPAN), 4), (slice(LANE, WIDE), slice(4 * SPAN, LANES), 2))

    def score_step(w0, n):
        for w in range(w0, w0 + n):
            at = slice(w * SPAN, (w + 1) * SPAN)
            for lanes, cut, heads in groups:
                scores_s[w, :, cut] = mul(k_s[at, lanes], diagonal(q_s[at, lanes], heads), NT)
                dp_s[w, :, cut] = mul(v_s[at, lanes], diagonal(da_s[at, lanes], heads), NT)

    def softmax_step(w0, n):
        for w in range(w0, w0 + n):
            same = lab_col[w] == lab_row[w : w + 1, :]
            for t in range(HEADS // 2):
                cut = slice(t * LANE, (t + 1) * LANE)
                scores = jnp.where(same, scores_s[w, :, cut] + bias_t[:, cut], MASKED)
                e = jnp.exp(scores - jnp.max(scores, 0, keepdims=True))
                p = e * (1.0 / jnp.sum(e, 0, keepdims=True))
                p_s[w, :, cut] = p.astype(BF16)
                dp = dp_s[w, :, cut]
                ds = p * (dp - jnp.sum(p * dp, 0, keepdims=True))
                score_acc[:, cut] += ds
                ds_s[w, :, cut] = ds.astype(BF16)

    def spread_step(w0, n):
        for w in range(w0, w0 + n):
            at = slice(w * SPAN, (w + 1) * SPAN)
            for lanes, cut, heads in groups:
                p, ds = p_s[w, :, cut], ds_s[w, :, cut]
                att[at, lanes] = gather_heads(mul(p, v_s[at, lanes], TN)).astype(BF16)
                dq = gather_heads(mul(ds, k_s[at, lanes], TN))
                dq_s[at, lanes] = (dq * HEAD ** (-0.5)).astype(BF16)
                dk_s[at, lanes] = mul(ds, diagonal(q_s[at, lanes], heads)).astype(BF16)
                dv_s[at, lanes] = mul(p, diagonal(da_s[at, lanes], heads)).astype(BF16)

    edge = tile_cols - EDGE
    backs = []

    def back(src, dst, to_row, to_col):
        i = len(backs)
        backs.append(remote(src, dst, back_send.at[i], back_recv.at[i], to_row, to_col))
        backs[-1].start()

    corner.wait()
    corner_on.start()
    waiting = []
    for b, (w0, step_wins) in enumerate(plan):
        for copy in chunks[b] + ([] if b else sides + [corner_on]):
            copy.wait()
        if b + ahead < steps:
            for copy in chunks[b + ahead]:
                copy.start()
        if b >= 2:
            for copy in waiting:
                back(*copy)
            waiting = []
        step, span_cols, end = step_wins * SPAN, step_wins * WIN, w0 + step_wins
        at = slice(w0 * SPAN, end * SPAN)
        win_at = slice(w0, end)
        cols = slice(w0 * WIN, end * WIN)
        near = slice(w0 * WIN, min(end * WIN + EDGE, tile_cols))

        for r in range(WIN):
            if r < SHIFT:
                part, beyond = both_b[r, near], both_d[r]
            else:
                part, beyond = both[r - SHIFT, near], both_r[r - SHIFT]
            wide = part.astype(F32)
            if end == wins:
                wide = jnp.concatenate([wide, beyond.astype(F32)], 0)
            wide = wide[SHIFT : SHIFT + span_cols]
            unit[win_at, r] = wide[:, 0:C].reshape(step_wins, WIN, C)
            gradf[win_at, r] = wide[:, C : 2 * C].reshape(step_wins, WIN, C)

        x = unit[win_at].reshape(step, C)
        center = jnp.mean(x, -1, keepdims=True)
        x = x - center
        inv = lax.rsqrt(jnp.mean(x * x, -1, keepdims=True) + 1e-05)
        x = x * inv
        unit[win_at] = x.reshape(step_wins, WIN, WIN, C)
        inv_std[at] = inv
        n = (x * gain_ref[...] + offset_ref[...]).astype(BF16)
        nt_s[0:C, at] = n.T
        q_s[at] = ((mul(n, w_s[0]) + b_s[0]) * HEAD ** (-0.5)).astype(BF16)
        k_s[at] = (mul(n, w_s[1]) + b_s[1]).astype(BF16)
        v_s[at] = (mul(n, w_s[2]) + b_s[2]).astype(BF16)
        g = gradf[win_at].reshape(step, C).astype(BF16)
        gb_s[at] = g
        da_s[at] = mul(g, pw_s[...], NT).astype(BF16)

        score_step(w0, 2)
        for w in range(w0, end, 2):
            softmax_step(w, 2)
            if w + 2 < end:
                score_step(w + 2, 2)
            spread_step(w, 2)

        x = unit[win_at].reshape(step, C)
        dn = mul(dq_s[at], w_s[0], NT) + mul(dk_s[at], w_s[1], NT) + mul(dv_s[at], w_s[2], NT)
        sums[0:1, 0:C] += jnp.sum(dn * x, 0, keepdims=True)
        sums[1:2, 0:C] += jnp.sum(dn, 0, keepdims=True)
        g = dn * gain_ref[...]
        dx = inv_std[at] * (
            g - jnp.mean(g, -1, keepdims=True) - x * jnp.mean(g * x, -1, keepdims=True)
        )
        out = (gradf[win_at].reshape(step, C) + dx).reshape(step_wins, WIN, WIN, C)
        for r in range(SHIFT):
            frame_low[r, cols] = out[:, SHIFT + r].reshape(span_cols, C).astype(BF16)
        for r in range(0, SHIFT, 2):
            two = [out[:, r + i].reshape(span_cols, C) for i in range(2)]
            frame_two[r // 2, cols] = jnp.concatenate(two, 1).astype(BF16)
        waiting.append((frame_two.at[0:2, cols], back_u.at[0:2, cols], up, col))
        if b == 0:
            waiting.append((frame_low.at[0:SHIFT, edge:tile_cols], back_l, row, other))
            waiting.append((frame_two.at[0:2, edge:tile_cols], back_ul, up, other))
        if w0 != 2:
            over = slice(w0 * SPAN, w0 * SPAN + 4 * SPAN)
            for i, part in enumerate((dq_s, dk_s, dv_s)):
                product = mul(nt_s[:, over], part[over])
                grads[i] = product if b == 0 else grads[i] + product
            product = mul(gb_s[over], att[over], TN)
            grads[3, 0:C] = product if b == 0 else grads[3, 0:C] + product
    for copy in waiting:
        back(*copy)

    for i in range(3):
        pack[i * BLOCK : (i + 1) * BLOCK, :] = grads[i, :, 0:LANE]
    pack[3 * BLOCK : 3 * BLOCK + C, :] = grads[3, 0:C, 0:LANE]
    pack[3 * BLOCK + C : 4 * BLOCK, :] = jnp.zeros((BLOCK - C, LANE), F32)
    pack[4 * BLOCK : 5 * BLOCK, :] = grads[0, :, LANE:WIDE] + pltpu.roll(grads[1, :, LANE:WIDE], 64, 1)
    pack[5 * BLOCK : 6 * BLOCK, :] = grads[2, :, LANE:WIDE]
    pack[5 * BLOCK : 5 * BLOCK + C, :] += pltpu.roll(grads[3, 0:C, LANE:WIDE], 64, 1)
    for h in range(HEADS):
        span_a[h * SPAN : (h + 1) * SPAN, :] = score_acc[:, h * SPAN : (h + 1) * SPAN]
    wide = jnp.concatenate(
        [span_a[pl.ds(cj, HEADS * WIN, stride=WIN), :] for cj in range(WIN)], 1
    )
    span_b[...] = split_mul(wide, fold_a[...])
    wide = jnp.concatenate(
        [span_b[pl.ds(rj, HEADS, stride=WIN), :] for rj in range(WIN)], 1
    )
    flat_sum = split_mul(wide, fold_b[...])
    sums[8 : 8 + HEADS, :] = flat_sum
    pack[small : small + 16, :] = sums[:, 0:LANE]
    pack[small + 16 : small + 32, :] = sums[:, LANE:WIDE]
    pack_low[...] = pack[...].astype(BF16)

    pair = remote(
        pack_low.at[pl.ds(pl.multiple_of(other * half, 16), half)], pair_in,
        pair_sem.at[0], pair_sem.at[1], row, other,
    )
    pair.start()
    pair.wait()
    mine = pl.ds(pl.multiple_of(col * half, 16), half)
    half_low[...] = (pack[mine] + pair_in[...].astype(F32)).astype(BF16)

    def part_copy(k):
        peer = lax.rem(row + k, rows_n)
        return remote(
            half_low.at[pl.ds(pl.multiple_of(peer * chunk, 16), chunk)], part_in.at[k],
            part_send.at[k], part_recv.at[k], peer, col,
        )

    @pl.loop(1, rows_n)
    def _(k):
        part_copy(k).start()

    def add_part(k, total):
        part_copy(k).wait()
        return total + part_in[k].astype(F32)

    my_chunk = pl.ds(pl.multiple_of(row * chunk, 16), chunk)
    total = lax.fori_loop(1, rows_n, add_part, half_low[my_chunk].astype(F32))
    own_chunk = result.at[col, my_chunk]
    own_chunk[...] = total.astype(BF16)

    def all_copy(k):
        return remote(
            own_chunk, own_chunk, all_send.at[k], all_recv.at[k],
            lax.rem(row + k, rows_n), col,
        )

    def forward(k):
        source = lax.rem(row + rows_n - k, rows_n)
        piece = result.at[col, pl.ds(pl.multiple_of(source * chunk, 16), chunk)]
        return remote(piece, piece, fwd_send.at[k], fwd_recv.at[k], row, other)

    @pl.loop(1, rows_n)
    def _(k):
        all_copy(k).start()

    forward(0).start()

    for copy in backs:
        copy.wait()
    for r in range(WIN):
        if r < SHIFT:
            left_part, main_part = back_l[r], frame_low[r]
        else:
            lanes = slice((r % 2) * C, (r % 2 + 1) * C)
            left_part = back_ul[(r - SHIFT) // 2].astype(F32)[:, lanes]
            main_part = back_u[(r - SHIFT) // 2].astype(F32)[:, lanes]
        wide = jnp.concatenate([left_part.astype(F32), main_part.astype(F32)], 0)
        turned[pl.ds(r, C, stride=WIN), :] = wide[EDGE - SHIFT : EDGE - SHIFT + tile_cols].T
    d_tok[...] = turned[...].reshape(C, WIN, tile_cols).astype(BF16)


    @pl.loop(1, rows_n)
    def _(k):
        all_copy(k).wait()
        forward(k).start()

    @pl.loop(0, rows_n)
    def _(k):
        forward(k).wait()

    done = jnp.concatenate([result[0], result[1]], 0)
    blocks = [done[i * BLOCK : (i + 1) * BLOCK] for i in range(6)]
    joined = jnp.concatenate([blocks[i] for i in (0, 1, 2, 4, 5)], 1)
    product = mul(joined, pick_s[...]) * out_scale
    d_qkvw[...] = product[0:C]
    d_qkvb[...] = product[C : C + 1].reshape(3 * C)
    spread = e_s[...]
    far = pltpu.roll(spread[:, LANE:WIDE].astype(F32), 64, 1).astype(BF16)
    product = mul(spread[:, 0:LANE], blocks[3], NT) + mul(far, blocks[5], NT)
    d_projw[...] = product[:, 0:C] * out_scale
    tail = done[small : small + 32].astype(F32) * out_scale
    tail = jnp.concatenate([tail[0:16], tail[16:32]], 1)
    d_gain[...] = tail[0:1, 0:C]
    d_offset[...] = tail[1:2, 0:C]
    entries = table_spread(d_table.shape[1])
    d_table[...] = exact(tail[8 : 8 + HEADS, :], entries, NT)


def finish(*refs):
    sources, outs, held, sems = refs[0:7], refs[7:14], refs[14:21], refs[21]
    into = [pltpu.make_async_copy(sources[i], held[i], sems.at[0, i]) for i in range(7)]
    away = [pltpu.make_async_copy(held[i], outs[i], sems.at[1, i]) for i in range(7)]
    for copy in into:
        copy.start()
    for first, second in zip(into, away):
        first.wait()
        second.start()
    for copy in away:
        copy.wait()


def on_device(
    tokens, grad_out, regions, ln_gain, ln_offset, qkv_weight, qkv_bias, proj_weight, bias_table
):
    rows_n, cols_n = lax.axis_size("row"), lax.axis_size("col")
    tile_cols = tokens.shape[1]
    wins = tile_cols // WIN
    count = wins * SPAN
    steps = len(window_steps(wins))
    unit_rows = 2 * 16 * rows_n
    needed = 6 * BLOCK + 32
    rows_total = -(-needed // unit_rows) * unit_rows
    half = rows_total // 2
    chunk = half // rows_n
    total_tokens = tokens.shape[0] * tile_cols * rows_n * cols_n
    vmem = pltpu.VMEM
    halo = [
        vmem((SHIFT, tile_cols, 2 * C), BF16),
        vmem((SHIFT, EDGE, 2 * C), BF16),
        vmem((SHIFT, EDGE, 2 * C), BF16),
    ]
    home = [
        vmem((SHIFT, tile_cols, C), BF16),
        vmem((2, tile_cols, 2 * C), BF16),
        vmem((2, tile_cols, 2 * C), BF16),
        vmem((SHIFT, EDGE, C), BF16),
        vmem((2, EDGE, 2 * C), BF16),
    ]
    flat_low = vmem((count, WIDE), BF16)
    whole = pl.BlockSpec(memory_space=pltpu.VMEM)
    dma = pltpu.SemaphoreType.DMA
    outs = pl.pallas_call(
        functools.partial(body, rows_n, cols_n, rows_total, total_tokens ** (-0.5)),
        out_shape=(
            jax.ShapeDtypeStruct((C,) + tokens.shape[:2], BF16),
            jax.ShapeDtypeStruct((C, 3 * C), F32),
            jax.ShapeDtypeStruct((3 * C,), F32),
            jax.ShapeDtypeStruct((C, C), F32),
            jax.ShapeDtypeStruct((HEADS, bias_table.shape[0]), F32),
            jax.ShapeDtypeStruct((1, C), F32),
            jax.ShapeDtypeStruct((1, C), F32),
        ),
        in_specs=[pl.BlockSpec(memory_space=pl.ANY)] * 9,
        out_specs=(whole,) * 7,
        scratch_shapes=[
            vmem((WIN, tile_cols, 2 * C), BF16),
            vmem((2 * C * WIN, tile_cols), F32),
        ] + halo + [
            vmem(regions.shape, jnp.int32),
            vmem(regions.shape, jnp.int32),
            vmem((wins, WIN, WIN, C), F32),
            vmem((count, 1), F32),
            vmem((wins, WIN, WIN, C), F32),
            vmem((192, count), BF16),
        ] + [flat_low] * 4 + [vmem((count, C), BF16)] + [flat_low] * 4 + [
            vmem((3, C, WIDE), BF16),
            vmem((3, 1, WIDE), F32),
            vmem((WIDE, C), BF16),
            vmem((C, WIDE), BF16),
            vmem((5 * LANE, 3 * C), BF16),
            vmem((SPAN, LANES), F32),
            vmem((HEADS * SPAN, SPAN), F32),
            vmem((HEADS * WIN, 128), F32),
            vmem((4 * 16, LANE), BF16),
            vmem((wins, SPAN, 128), F32),
            vmem((wins, LANE), F32),
            vmem((SPAN, LANES), F32),
            vmem((16, WIDE), F32),
            vmem((wins, SPAN, LANES), F32),
            vmem((wins, SPAN, LANES), F32),
            vmem((wins, SPAN, LANES), BF16),
            vmem((wins, SPAN, LANES), BF16),
            vmem((4, BLOCK, WIDE), F32),
            vmem((C * WIN, tile_cols), F32),
            vmem((WIN * SPAN, 128), BF16),
            vmem((WIN * 128, 256), BF16),
        ] + home + [
            vmem((rows_total, LANE), F32),
            vmem((rows_total, LANE), BF16),
            vmem((half, LANE), BF16),
            vmem((half, LANE), BF16),
            vmem((rows_n, chunk, LANE), BF16),
            vmem((2, half, LANE), BF16),
            vmem((C,) + tokens.shape[:2], BF16), vmem((C,) + tokens.shape[:2], BF16),
            vmem(regions.shape, jnp.int32),
            vmem((1, C), F32), vmem((1, C), F32), vmem(qkv_weight.shape, BF16), vmem((3 * C,), F32),
            vmem(proj_weight.shape, BF16), vmem(bias_table.shape[::-1], F32), dma((9,)),
            dma((5 + steps,)), dma((5 + steps,)),
            dma((steps + 2,)), dma((steps + 2,)), dma((2,)),
            dma((rows_n,)), dma((rows_n,)), dma((rows_n,)), dma((rows_n,)),
            dma((rows_n,)), dma((rows_n,)),
        ],
        compiler_params=pltpu.CompilerParams(
            collective_id=0, has_side_effects=True, vmem_limit_bytes=61 * 1024 * 1024
        ),
    )(
        jnp.transpose(tokens, (2, 0, 1)), jnp.transpose(grad_out, (2, 0, 1)), regions, ln_gain.reshape(1, C), ln_offset.reshape(1, C), qkv_weight,
        qkv_bias, proj_weight, bias_table.T,
    )
    anywhere = pl.BlockSpec(memory_space=pl.ANY)
    d_tokens, d_qkvw, d_qkvb, d_projw, d_table, d_gain, d_offset = pl.pallas_call(
        finish,
        out_shape=[jax.ShapeDtypeStruct(x.shape, x.dtype) for x in outs],
        in_specs=[anywhere] * 7,
        out_specs=[anywhere] * 7,
        scratch_shapes=[vmem(x.shape, x.dtype) for x in outs] + [dma((2, 7))],
        compiler_params=pltpu.CompilerParams(vmem_limit_bytes=61 * 1024 * 1024),
    )(*outs)
    return (
        jnp.transpose(d_tokens, (1, 2, 0)),
        d_qkvw,
        d_qkvb,
        d_projw,
        d_table.T,
        d_gain.reshape(C),
        d_offset.reshape(C),
    )


def solution(mesh):
    placed = (
        P(("grp", "row"), "col", None),
        P(("grp", "row"), "col", None),
        P(("grp", "row"), "col"),
        P(),
        P(),
        P(),
        P(),
        P(),
        P(),
    )
    return jax.shard_map(
        on_device,
        mesh=mesh,
        in_specs=placed,
        out_specs=(
            P(("grp", "row"), "col", None),
            P("grp", None),
            P("grp"),
            P("grp", None),
            P("grp", None),
            P("grp"),
            P("grp"),
        ),
        check_vma=False,
    )
```

```python
import functools

import jax
import jax.numpy as jnp
from jax import lax
from jax.experimental import pallas as pl
from jax.experimental.pallas import tpu as pltpu
from jax.sharding import PartitionSpec as P

HEADS = 6
WIN = 8
SHIFT = 4
SPAN = WIN * WIN
C = 180
HEAD = C // HEADS
LANES = HEADS * SPAN
BLOCK = 192
LANE = 128
WIDE = 2 * LANE
HEADW = 32
EDGE = 16
MASKED = -10000.0
MESH = pl.DeviceIdType.MESH
F32 = jnp.float32
BF16 = jnp.bfloat16

NN = (((1,), (0,)), ((), ()))
NT = (((1,), (1,)), ((), ()))
TN = (((0,), (0,)), ((), ()))


def mul(left, right, form=NN):
    return lax.dot_general(left, right, form, preferred_element_type=F32)


def exact(left, right, form=NN):
    return lax.dot_general(
        left, right, form, preferred_element_type=F32, precision=lax.Precision.HIGHEST
    )


def split_mul(left, picks):
    high = left.astype(BF16)
    low = (left - high.astype(F32)).astype(BF16)
    return mul(high, picks) + mul(low, picks)


def iota(shape, dim):
    return lax.broadcasted_iota(jnp.int32, shape, dim)


def col_spread(cj):
    src = iota((SPAN, 128), 0)
    dst = iota((SPAN, 128), 1)
    return (dst == (src >> 3) * 16 + (src & 7) - cj + 7).astype(F32)


def row_spread(rj):
    src = iota((128, 256), 0)
    dst = iota((128, 256), 1)
    return (dst == src + 16 * (7 - rj)).astype(F32)


def table_spread(entries):
    src = iota((entries, 256), 0)
    dst = iota((entries, 256), 1)
    hit = (src == (dst >> 4) * 15 + (dst & 15)) & ((dst & 15) < 15) & (dst < 240)
    return hit.astype(F32)


def head_spread():
    src = iota((C, WIDE), 0)
    lane = iota((1, WIDE), 1)
    head, place = lane >> 5, lane & (HEADW - 1)
    wanted = jnp.where((place < HEAD) & (head < HEADS), head * HEAD + place, -1)
    return (src == wanted).astype(F32).astype(BF16)


def part_pick():
    lane = iota((1, 3 * C), 1)
    part = (lane >= C).astype(jnp.int32) + (lane >= 2 * C).astype(jnp.int32)
    place = lane - part * C
    head = sum((place >= t * HEAD).astype(jnp.int32) for t in range(1, HEADS))
    place = place - head * HEAD
    near = part * LANE + head * HEADW + place
    far = 3 * LANE + (part >> 1) * LANE + (part & 1) * 64 + (head - 4) * HEADW + place
    wanted = jnp.where(head < 4, near, far)
    return (iota((5 * LANE, 3 * C), 0) == wanted).astype(F32).astype(BF16)


def window_steps(wins):
    return [(w, 4) for w in range(wins - 4, -1, -4)]


def body(
    rows_n, cols_n, rows_total, out_scale,
    tok_in, grad_in, reg_in, gain_in, offset_in, qkvw_in, qkvb_in, projw_in, table_in,
    d_tok, d_qkvw, d_qkvb, d_projw, d_table, d_gain, d_offset,
    both, spread_t, both_b, both_r, both_d, reg_b, reg_r,
    unit, inv_std, gradf, nt_s, q_s, k_s, v_s, da_s, gb_s, att, dq_s, dk_s, dv_s,
    w_s, b_s, pw_s, e_s, pick_s, bias_t, span_a, span_b, hmask, lab_col, lab_row, score_acc, sums,
    scores_s, dp_s, p_s, ds_s, grads, turned,
    fold_a, fold_b, frame_low, frame_two, back_u, back_l, back_ul,
    pack, pack_low, pair_in, half_low, part_in, result,
    tok_t, grad_t, reg, gain_ref, offset_ref, qkvw, qkvb, projw, table, local_sem,
    halo_send, halo_recv, back_send, back_recv, pair_sem,
    part_send, part_recv, all_send, all_recv, fwd_send, fwd_recv,
):
    row = lax.axis_index("row")
    col = lax.axis_index("col")
    up = lax.rem(row + rows_n - 1, rows_n)
    down = lax.rem(row + 1, rows_n)
    other = lax.rem(col + 1, cols_n)
    tile_cols = tok_in.shape[2]
    wins = tile_cols // WIN
    count = wins * SPAN
    half = rows_total // 2
    chunk = half // rows_n

    def remote(src, dst, send, recv, to_row, to_col):
        return pltpu.make_async_remote_copy(
            src_ref=src, dst_ref=dst, send_sem=send, recv_sem=recv,
            device_id={"row": to_row, "col": to_col}, device_id_type=MESH,
        )

    locals_ = [
        pltpu.make_async_copy(src, dst, local_sem.at[i])
        for i, (src, dst) in enumerate((
            (tok_in, tok_t), (grad_in, grad_t), (reg_in, reg),
            (table_in, table), (gain_in, gain_ref), (offset_in, offset_ref),
            (qkvw_in, qkvw), (qkvb_in, qkvb), (projw_in, projw),
        ))
    ]
    for copy in locals_:
        copy.start()
    barrier = pltpu.get_barrier_semaphore()

    @pl.loop(1, rows_n)
    def _(k):
        pl.semaphore_signal(
            barrier, inc=1, device_id={"row": lax.rem(row + k, rows_n), "col": col},
            device_id_type=MESH,
        )

    for to_row in (row, up, down):
        pl.semaphore_signal(
            barrier, inc=1, device_id={"row": to_row, "col": other}, device_id_type=MESH
        )
    def turn(r):
        both[r] = spread_t[pl.ds(r, 2 * C, stride=WIN), :].T.astype(BF16)

    for copy in locals_[0:3]:
        copy.wait()
    spread_t[0 : C * WIN, :] = tok_t[...].astype(F32).reshape(C * WIN, tile_cols)
    spread_t[C * WIN : 2 * C * WIN, :] = grad_t[...].astype(F32).reshape(C * WIN, tile_cols)
    for r in range(SHIFT, WIN):
        turn(r)
    pl.semaphore_wait(barrier, rows_n + 2)

    plan = window_steps(wins)
    steps = len(plan)

    def halo(i, src, dst, to_row, to_col):
        return remote(src, dst, halo_send.at[i], halo_recv.at[i], to_row, to_col)

    labels = [halo(0, reg, reg_b, down, col), halo(1, reg, reg_r, row, other)]
    sides = [
        halo(2, both.at[0:SHIFT, 0:EDGE], both_r, row, other),
    ]
    corner = halo(3, both.at[SHIFT:WIN, 0:EDGE], both_b.at[0:SHIFT, 0:EDGE], down, col)
    corner_on = halo(4, both_b.at[0:SHIFT, 0:EDGE], both_d, row, other)
    chunks = []
    for b, (w0, n) in enumerate(plan):
        cols = slice(max(w0 * WIN, EDGE), (w0 + n) * WIN)
        chunks.append([halo(5 + b, both.at[SHIFT:WIN, cols], both_b.at[0:SHIFT, cols], down, col)])
    ahead = 9
    small = 6 * BLOCK
    for copy in labels + [corner] + sum(chunks[:ahead], []):
        copy.start()
    for r in range(SHIFT):
        turn(r)
    for copy in sides:
        copy.start()

    for copy in locals_[3:]:
        copy.wait()
    flat = exact(table[...], table_spread(table.shape[1]))
    for rj in range(WIN):
        span_b[pl.ds(rj, HEADS, stride=WIN), :] = exact(flat, row_spread(rj), NT)
    for cj in range(WIN):
        span_a[pl.ds(cj, HEADS * WIN, stride=WIN), :] = exact(span_b[...], col_spread(cj), NT)
    for h in range(HEADS):
        bias_t[:, h * SPAN : (h + 1) * SPAN] = span_a[h * SPAN : (h + 1) * SPAN, :]
    mask_row = iota((4 * 16, LANE), 0) >> 4
    hmask[...] = ((iota((4 * 16, LANE), 1) >> 5) == mask_row).astype(F32).astype(BF16)
    e_s[...] = head_spread()
    pick_s[...] = part_pick()
    score_acc[...] = jnp.zeros_like(score_acc)
    sums[...] = jnp.zeros_like(sums)
    pack[small:] = jnp.zeros_like(pack[small:])

    nt_s[...] = jnp.ones_like(nt_s)
    for cj in range(WIN):
        fold_a[cj * SPAN : (cj + 1) * SPAN, :] = col_spread(cj).astype(BF16)
    for rj in range(WIN):
        fold_b[rj * 128 : (rj + 1) * 128, :] = row_spread(rj).astype(BF16)
    weights = qkvw[...]
    offsets = qkvb[...].reshape(1, 3 * C)
    for i in range(3):
        w_s[i] = mul(weights[:, i * C : (i + 1) * C], e_s[...]).astype(BF16)
        b_s[i] = exact(offsets[:, i * C : (i + 1) * C], e_s[...].astype(F32))
    pw_s[...] = mul(e_s[...], projw[...], TN).astype(BF16)

    for copy in labels:
        copy.wait()

    own = reg[...]
    row_part = jnp.concatenate([reg_b[SHIFT:, :], own[0:SHIFT]], 0)[:, 0:1] >> 2
    col_own = pltpu.roll(own, tile_cols - SHIFT, 1)
    col_right = pltpu.roll(reg_r[...], tile_cols - SHIFT, 1)
    col_part = jnp.where(iota((WIN, tile_cols), 1) < tile_cols - SHIFT, col_own, col_right)[0:1] & 3
    label = (row_part * 4 + col_part).astype(F32)
    spread = jnp.broadcast_to(label[:, None, :], (WIN, WIN, tile_cols)).reshape(SPAN, tile_cols)
    spread = jnp.where(
        (iota((SPAN, tile_cols), 0) & 7) == (iota((SPAN, tile_cols), 1) & 7), spread, 0.0
    )
    pick = ((iota((tile_cols, wins), 0) >> 3) == iota((tile_cols, wins), 1)).astype(F32)
    columns = exact(spread, pick)
    tiled = (iota((SPAN, LANE), 0) == (iota((SPAN, LANE), 1) & (SPAN - 1))).astype(F32)
    lab_row[...] = exact(columns, tiled, TN)
    for w in range(wins):
        lab_col[w] = jnp.broadcast_to(columns[:, w : w + 1], (SPAN, 128))

    lane = iota((SPAN, LANE), 1)

    def gather_heads(stacked):
        out = stacked[-SPAN:]
        for h in range(stacked.shape[0] // SPAN - 2, -1, -1):
            out = jnp.where(lane < (h + 1) * HEADW, stacked[h * SPAN : (h + 1) * SPAN], out)
        return out

    def diagonal(x, heads):
        tiles = x.reshape(SPAN // 16, 16, LANE)
        parts = [
            (tiles * hmask[h * 16 : (h + 1) * 16, :][None]).reshape(SPAN, LANE) for h in range(heads)
        ]
        return jnp.concatenate(parts, 0)

    groups = ((slice(0, LANE), slice(0, 4 * SPAN), 4), (slice(LANE, WIDE), slice(4 * SPAN, LANES), 2))

    def score_step(w0, n):
        for w in range(w0, w0 + n):
            at = slice(w * SPAN, (w + 1) * SPAN)
            for lanes, cut, heads in groups:
                scores_s[w, :, cut] = mul(k_s[at, lanes], diagonal(q_s[at, lanes], heads), NT)
                dp_s[w, :, cut] = mul(v_s[at, lanes], diagonal(da_s[at, lanes], heads), NT)

    def softmax_step(w0, n):
        for w in range(w0, w0 + n):
            same = lab_col[w] == lab_row[w : w + 1, :]
            for t in range(HEADS // 2):
                cut = slice(t * LANE, (t + 1) * LANE)
                scores = jnp.where(same, scores_s[w, :, cut] + bias_t[:, cut], MASKED)
                e = jnp.exp(scores - jnp.max(scores, 0, keepdims=True))
                p = e * (1.0 / jnp.sum(e, 0, keepdims=True))
                p_s[w, :, cut] = p.astype(BF16)
                dp = dp_s[w, :, cut]
                ds = p * (dp - jnp.sum(p * dp, 0, keepdims=True))
                score_acc[:, cut] += ds
                ds_s[w, :, cut] = ds.astype(BF16)

    def spread_step(w0, n):
        for w in range(w0, w0 + n):
            at = slice(w * SPAN, (w + 1) * SPAN)
            for lanes, cut, heads in groups:
                p, ds = p_s[w, :, cut], ds_s[w, :, cut]
                att[at, lanes] = gather_heads(mul(p, v_s[at, lanes], TN)).astype(BF16)
                dq = gather_heads(mul(ds, k_s[at, lanes], TN))
                dq_s[at, lanes] = (dq * HEAD ** (-0.5)).astype(BF16)
                dk_s[at, lanes] = mul(ds, diagonal(q_s[at, lanes], heads)).astype(BF16)
                dv_s[at, lanes] = mul(p, diagonal(da_s[at, lanes], heads)).astype(BF16)

    edge = tile_cols - EDGE
    backs = []

    def back(src, dst, to_row, to_col):
        i = len(backs)
        backs.append(remote(src, dst, back_send.at[i], back_recv.at[i], to_row, to_col))
        backs[-1].start()

    corner.wait()
    corner_on.start()
    waiting = []
    for b, (w0, step_wins) in enumerate(plan):
        for copy in chunks[b] + ([] if b else sides + [corner_on]):
            copy.wait()
        if b + ahead < steps:
            for copy in chunks[b + ahead]:
                copy.start()
        if b >= 2:
            for copy in waiting:
                back(*copy)
            waiting = []
        step, span_cols, end = step_wins * SPAN, step_wins * WIN, w0 + step_wins
        at = slice(w0 * SPAN, end * SPAN)
        win_at = slice(w0, end)
        cols = slice(w0 * WIN, end * WIN)
        near = slice(w0 * WIN, min(end * WIN + EDGE, tile_cols))

        for r in range(WIN):
            if r < SHIFT:
                part, beyond = both_b[r, near], both_d[r]
            else:
                part, beyond = both[r - SHIFT, near], both_r[r - SHIFT]
            wide = part.astype(F32)
            if end == wins:
                wide = jnp.concatenate([wide, beyond.astype(F32)], 0)
            wide = wide[SHIFT : SHIFT + span_cols]
            unit[win_at, r] = wide[:, 0:C].reshape(step_wins, WIN, C)
            gradf[win_at, r] = wide[:, C : 2 * C].reshape(step_wins, WIN, C)

        x = unit[win_at].reshape(step, C)
        center = jnp.mean(x, -1, keepdims=True)
        x = x - center
        inv = lax.rsqrt(jnp.mean(x * x, -1, keepdims=True) + 1e-05)
        x = x * inv
        unit[win_at] = x.reshape(step_wins, WIN, WIN, C)
        inv_std[at] = inv
        n = (x * gain_ref[...] + offset_ref[...]).astype(BF16)
        nt_s[0:C, at] = n.T
        q_s[at] = ((mul(n, w_s[0]) + b_s[0]) * HEAD ** (-0.5)).astype(BF16)
        k_s[at] = (mul(n, w_s[1]) + b_s[1]).astype(BF16)
        v_s[at] = (mul(n, w_s[2]) + b_s[2]).astype(BF16)
        g = gradf[win_at].reshape(step, C).astype(BF16)
        gb_s[at] = g
        da_s[at] = mul(g, pw_s[...], NT).astype(BF16)

        score_step(w0, 2)
        for w in range(w0, end, 2):
            softmax_step(w, 2)
            if w + 2 < end:
                score_step(w + 2, 2)
            spread_step(w, 2)

        x = unit[win_at].reshape(step, C)
        dn = mul(dq_s[at], w_s[0], NT) + mul(dk_s[at], w_s[1], NT) + mul(dv_s[at], w_s[2], NT)
        sums[0:1, 0:C] += jnp.sum(dn * x, 0, keepdims=True)
        sums[1:2, 0:C] += jnp.sum(dn, 0, keepdims=True)
        g = dn * gain_ref[...]
        dx = inv_std[at] * (
            g - jnp.mean(g, -1, keepdims=True) - x * jnp.mean(g * x, -1, keepdims=True)
        )
        out = (gradf[win_at].reshape(step, C) + dx).reshape(step_wins, WIN, WIN, C)
        for r in range(SHIFT):
            frame_low[r, cols] = out[:, SHIFT + r].reshape(span_cols, C).astype(BF16)
        for r in range(0, SHIFT, 2):
            two = [out[:, r + i].reshape(span_cols, C) for i in range(2)]
            frame_two[r // 2, cols] = jnp.concatenate(two, 1).astype(BF16)
        waiting.append((frame_two.at[0:2, cols], back_u.at[0:2, cols], up, col))
        if b == 0:
            waiting.append((frame_low.at[0:SHIFT, edge:tile_cols], back_l, row, other))
            waiting.append((frame_two.at[0:2, edge:tile_cols], back_ul, up, other))
        if w0 != 2:
            over = slice(w0 * SPAN, w0 * SPAN + 4 * SPAN)
            for i, part in enumerate((dq_s, dk_s, dv_s)):
                product = mul(nt_s[:, over], part[over])
                grads[i] = product if b == 0 else grads[i] + product
            product = mul(gb_s[over], att[over], TN)
            grads[3, 0:C] = product if b == 0 else grads[3, 0:C] + product
    for copy in waiting:
        back(*copy)

    for i in range(3):
        pack[i * BLOCK : (i + 1) * BLOCK, :] = grads[i, :, 0:LANE]
    pack[3 * BLOCK : 3 * BLOCK + C, :] = grads[3, 0:C, 0:LANE]
    pack[3 * BLOCK + C : 4 * BLOCK, :] = jnp.zeros((BLOCK - C, LANE), F32)
    pack[4 * BLOCK : 5 * BLOCK, :] = grads[0, :, LANE:WIDE] + pltpu.roll(grads[1, :, LANE:WIDE], 64, 1)
    pack[5 * BLOCK : 6 * BLOCK, :] = grads[2, :, LANE:WIDE]
    pack[5 * BLOCK : 5 * BLOCK + C, :] += pltpu.roll(grads[3, 0:C, LANE:WIDE], 64, 1)
    for h in range(HEADS):
        span_a[h * SPAN : (h + 1) * SPAN, :] = score_acc[:, h * SPAN : (h + 1) * SPAN]
    wide = jnp.concatenate(
        [span_a[pl.ds(cj, HEADS * WIN, stride=WIN), :] for cj in range(WIN)], 1
    )
    span_b[...] = split_mul(wide, fold_a[...])
    wide = jnp.concatenate(
        [span_b[pl.ds(rj, HEADS, stride=WIN), :] for rj in range(WIN)], 1
    )
    flat_sum = split_mul(wide, fold_b[...])
    sums[8 : 8 + HEADS, :] = flat_sum
    pack[small : small + 16, :] = sums[:, 0:LANE]
    pack[small + 16 : small + 32, :] = sums[:, LANE:WIDE]
    pack_low[...] = pack[...].astype(BF16)

    pair = remote(
        pack_low.at[pl.ds(pl.multiple_of(other * half, 16), half)], pair_in,
        pair_sem.at[0], pair_sem.at[1], row, other,
    )
    pair.start()
    pair.wait()
    mine = pl.ds(pl.multiple_of(col * half, 16), half)
    half_low[...] = (pack[mine] + pair_in[...].astype(F32)).astype(BF16)

    def part_copy(k):
        peer = lax.rem(row + k, rows_n)
        return remote(
            half_low.at[pl.ds(pl.multiple_of(peer * chunk, 16), chunk)], part_in.at[k],
            part_send.at[k], part_recv.at[k], peer, col,
        )

    @pl.loop(1, rows_n)
    def _(k):
        part_copy(k).start()

    def add_part(k, total):
        part_copy(k).wait()
        return total + part_in[k].astype(F32)

    my_chunk = pl.ds(pl.multiple_of(row * chunk, 16), chunk)
    total = lax.fori_loop(1, rows_n, add_part, half_low[my_chunk].astype(F32))
    own_chunk = result.at[col, my_chunk]
    own_chunk[...] = total.astype(BF16)

    def all_copy(k):
        return remote(
            own_chunk, own_chunk, all_send.at[k], all_recv.at[k],
            lax.rem(row + k, rows_n), col,
        )

    def forward(k):
        source = lax.rem(row + rows_n - k, rows_n)
        piece = result.at[col, pl.ds(pl.multiple_of(source * chunk, 16), chunk)]
        return remote(piece, piece, fwd_send.at[k], fwd_recv.at[k], row, other)

    @pl.loop(1, rows_n)
    def _(k):
        all_copy(k).start()

    forward(0).start()

    for copy in backs:
        copy.wait()
    for r in range(WIN):
        if r < SHIFT:
            left_part, main_part = back_l[r], frame_low[r]
        else:
            lanes = slice((r % 2) * C, (r % 2 + 1) * C)
            left_part = back_ul[(r - SHIFT) // 2].astype(F32)[:, lanes]
            main_part = back_u[(r - SHIFT) // 2].astype(F32)[:, lanes]
        wide = jnp.concatenate([left_part.astype(F32), main_part.astype(F32)], 0)
        turned[pl.ds(r, C, stride=WIN), :] = wide[EDGE - SHIFT : EDGE - SHIFT + tile_cols].T
    d_tok[...] = turned[...].reshape(C, WIN, tile_cols).astype(BF16)


    @pl.loop(1, rows_n)
    def _(k):
        all_copy(k).wait()
        forward(k).start()

    @pl.loop(0, rows_n)
    def _(k):
        forward(k).wait()

    done = jnp.concatenate([result[0], result[1]], 0)
    blocks = [done[i * BLOCK : (i + 1) * BLOCK] for i in range(6)]
    joined = jnp.concatenate([blocks[i] for i in (0, 1, 2, 4, 5)], 1)
    product = mul(joined, pick_s[...]) * out_scale
    d_qkvw[...] = product[0:C]
    d_qkvb[...] = product[C : C + 1].reshape(3 * C)
    spread = e_s[...]
    far = pltpu.roll(spread[:, LANE:WIDE].astype(F32), 64, 1).astype(BF16)
    product = mul(spread[:, 0:LANE], blocks[3], NT) + mul(far, blocks[5], NT)
    d_projw[...] = product[:, 0:C] * out_scale
    tail = done[small : small + 32].astype(F32) * out_scale
    tail = jnp.concatenate([tail[0:16], tail[16:32]], 1)
    d_gain[...] = tail[0:1, 0:C]
    d_offset[...] = tail[1:2, 0:C]
    entries = table_spread(d_table.shape[1])
    d_table[...] = exact(tail[8 : 8 + HEADS, :], entries, NT)


def finish(*refs):
    sources, outs, held, sems = refs[0:7], refs[7:14], refs[14:21], refs[21]
    into = [pltpu.make_async_copy(sources[i], held[i], sems.at[0, i]) for i in range(7)]
    away = [pltpu.make_async_copy(held[i], outs[i], sems.at[1, i]) for i in range(7)]
    for copy in into:
        copy.start()
    for first, second in zip(into, away):
        first.wait()
        second.start()
    for copy in away:
        copy.wait()


def on_device(
    tokens, grad_out, regions, ln_gain, ln_offset, qkv_weight, qkv_bias, proj_weight, bias_table
):
    rows_n, cols_n = lax.axis_size("row"), lax.axis_size("col")
    tile_cols = tokens.shape[1]
    wins = tile_cols // WIN
    count = wins * SPAN
    steps = len(window_steps(wins))
    unit_rows = 2 * 16 * rows_n
    needed = 6 * BLOCK + 32
    rows_total = -(-needed // unit_rows) * unit_rows
    half = rows_total // 2
    chunk = half // rows_n
    total_tokens = tokens.shape[0] * tile_cols * rows_n * cols_n
    vmem = pltpu.VMEM
    halo = [
        vmem((SHIFT, tile_cols, 2 * C), BF16),
        vmem((SHIFT, EDGE, 2 * C), BF16),
        vmem((SHIFT, EDGE, 2 * C), BF16),
    ]
    home = [
        vmem((SHIFT, tile_cols, C), BF16),
        vmem((2, tile_cols, 2 * C), BF16),
        vmem((2, tile_cols, 2 * C), BF16),
        vmem((SHIFT, EDGE, C), BF16),
        vmem((2, EDGE, 2 * C), BF16),
    ]
    flat_low = vmem((count, WIDE), BF16)
    whole = pl.BlockSpec(memory_space=pltpu.VMEM)
    dma = pltpu.SemaphoreType.DMA
    outs = pl.pallas_call(
        functools.partial(body, rows_n, cols_n, rows_total, total_tokens ** (-0.5)),
        out_shape=(
            jax.ShapeDtypeStruct((C,) + tokens.shape[:2], BF16),
            jax.ShapeDtypeStruct((C, 3 * C), F32),
            jax.ShapeDtypeStruct((3 * C,), F32),
            jax.ShapeDtypeStruct((C, C), F32),
            jax.ShapeDtypeStruct((HEADS, bias_table.shape[0]), F32),
            jax.ShapeDtypeStruct((1, C), F32),
            jax.ShapeDtypeStruct((1, C), F32),
        ),
        in_specs=[pl.BlockSpec(memory_space=pl.ANY)] * 9,
        out_specs=(whole,) * 7,
        scratch_shapes=[
            vmem((WIN, tile_cols, 2 * C), BF16),
            vmem((2 * C * WIN, tile_cols), F32),
        ] + halo + [
            vmem(regions.shape, jnp.int32),
            vmem(regions.shape, jnp.int32),
            vmem((wins, WIN, WIN, C), F32),
            vmem((count, 1), F32),
            vmem((wins, WIN, WIN, C), F32),
            vmem((192, count), BF16),
        ] + [flat_low] * 4 + [vmem((count, C), BF16)] + [flat_low] * 4 + [
            vmem((3, C, WIDE), BF16),
            vmem((3, 1, WIDE), F32),
            vmem((WIDE, C), BF16),
            vmem((C, WIDE), BF16),
            vmem((5 * LANE, 3 * C), BF16),
            vmem((SPAN, LANES), F32),
            vmem((HEADS * SPAN, SPAN), F32),
            vmem((HEADS * WIN, 128), F32),
            vmem((4 * 16, LANE), BF16),
            vmem((wins, SPAN, 128), F32),
            vmem((wins, LANE), F32),
            vmem((SPAN, LANES), F32),
            vmem((16, WIDE), F32),
            vmem((wins, SPAN, LANES), F32),
            vmem((wins, SPAN, LANES), F32),
            vmem((wins, SPAN, LANES), BF16),
            vmem((wins, SPAN, LANES), BF16),
            vmem((4, BLOCK, WIDE), F32),
            vmem((C * WIN, tile_cols), F32),
            vmem((WIN * SPAN, 128), BF16),
            vmem((WIN * 128, 256), BF16),
        ] + home + [
            vmem((rows_total, LANE), F32),
            vmem((rows_total, LANE), BF16),
            vmem((half, LANE), BF16),
            vmem((half, LANE), BF16),
            vmem((rows_n, chunk, LANE), BF16),
            vmem((2, half, LANE), BF16),
            vmem((C,) + tokens.shape[:2], BF16), vmem((C,) + tokens.shape[:2], BF16),
            vmem(regions.shape, jnp.int32),
            vmem((1, C), F32), vmem((1, C), F32), vmem(qkv_weight.shape, BF16), vmem((3 * C,), F32),
            vmem(proj_weight.shape, BF16), vmem(bias_table.shape[::-1], F32), dma((9,)),
            dma((5 + steps,)), dma((5 + steps,)),
            dma((steps + 2,)), dma((steps + 2,)), dma((2,)),
            dma((rows_n,)), dma((rows_n,)), dma((rows_n,)), dma((rows_n,)),
            dma((rows_n,)), dma((rows_n,)),
        ],
        compiler_params=pltpu.CompilerParams(
            collective_id=0, has_side_effects=True, vmem_limit_bytes=61 * 1024 * 1024
        ),
    )(
        jnp.transpose(tokens, (2, 0, 1)), jnp.transpose(grad_out, (2, 0, 1)), regions, ln_gain.reshape(1, C), ln_offset.reshape(1, C), qkv_weight,
        qkv_bias, proj_weight, bias_table.T,
    )
    anywhere = pl.BlockSpec(memory_space=pl.ANY)
    d_tokens, d_qkvw, d_qkvb, d_projw, d_table, d_gain, d_offset = pl.pallas_call(
        finish,
        out_shape=[jax.ShapeDtypeStruct(x.shape, x.dtype) for x in outs],
        in_specs=[anywhere] * 7,
        out_specs=[anywhere] * 7,
        scratch_shapes=[vmem(x.shape, x.dtype) for x in outs] + [dma((2, 7))],
        compiler_params=pltpu.CompilerParams(vmem_limit_bytes=61 * 1024 * 1024),
    )(*outs)
    return (
        jnp.transpose(d_tokens, (1, 2, 0)),
        d_qkvw,
        d_qkvb,
        d_projw,
        d_table.T,
        d_gain.reshape(C),
        d_offset.reshape(C),
    )


def solution(mesh):
    placed = (
        P(("grp", "row"), "col", None),
        P(("grp", "row"), "col", None),
        P(("grp", "row"), "col"),
        P(),
        P(),
        P(),
        P(),
        P(),
        P(),
    )
    return jax.shard_map(
        on_device,
        mesh=mesh,
        in_specs=placed,
        out_specs=(
            P(("grp", "row"), "col", None),
            P("grp", None),
            P("grp"),
            P("grp", None),
            P("grp", None),
            P("grp"),
            P("grp"),
        ),
        check_vma=False,
    )
```

```python
import functools

import jax
import jax.numpy as jnp
from jax import lax
from jax.experimental import pallas as pl
from jax.experimental.pallas import tpu as pltpu
from jax.sharding import PartitionSpec as P

HEADS = 6
WIN = 8
SHIFT = 4
SPAN = WIN * WIN
C = 180
HEAD = C // HEADS
LANES = HEADS * SPAN
BLOCK = 192
LANE = 128
WIDE = 2 * LANE
HEADW = 32
EDGE = 16
MASKED = -10000.0
MESH = pl.DeviceIdType.MESH
F32 = jnp.float32
BF16 = jnp.bfloat16

NN = (((1,), (0,)), ((), ()))
NT = (((1,), (1,)), ((), ()))
TN = (((0,), (0,)), ((), ()))


def mul(left, right, form=NN):
    return lax.dot_general(left, right, form, preferred_element_type=F32)


def exact(left, right, form=NN):
    return lax.dot_general(
        left, right, form, preferred_element_type=F32, precision=lax.Precision.HIGHEST
    )


def split_mul(left, picks):
    high = left.astype(BF16)
    low = (left - high.astype(F32)).astype(BF16)
    return mul(high, picks) + mul(low, picks)


def iota(shape, dim):
    return lax.broadcasted_iota(jnp.int32, shape, dim)


def col_spread(cj):
    src = iota((SPAN, 128), 0)
    dst = iota((SPAN, 128), 1)
    return (dst == (src >> 3) * 16 + (src & 7) - cj + 7).astype(F32)


def row_spread(rj):
    src = iota((128, 256), 0)
    dst = iota((128, 256), 1)
    return (dst == src + 16 * (7 - rj)).astype(F32)


def table_spread(entries):
    src = iota((entries, 256), 0)
    dst = iota((entries, 256), 1)
    hit = (src == (dst >> 4) * 15 + (dst & 15)) & ((dst & 15) < 15) & (dst < 240)
    return hit.astype(F32)


def head_spread():
    src = iota((C, WIDE), 0)
    lane = iota((1, WIDE), 1)
    head, place = lane >> 5, lane & (HEADW - 1)
    wanted = jnp.where((place < HEAD) & (head < HEADS), head * HEAD + place, -1)
    return (src == wanted).astype(F32).astype(BF16)


def part_pick():
    lane = iota((1, 3 * C), 1)
    part = (lane >= C).astype(jnp.int32) + (lane >= 2 * C).astype(jnp.int32)
    place = lane - part * C
    head = sum((place >= t * HEAD).astype(jnp.int32) for t in range(1, HEADS))
    place = place - head * HEAD
    near = part * LANE + head * HEADW + place
    far = 3 * LANE + (part >> 1) * LANE + (part & 1) * 64 + (head - 4) * HEADW + place
    wanted = jnp.where(head < 4, near, far)
    return (iota((5 * LANE, 3 * C), 0) == wanted).astype(F32).astype(BF16)


def window_steps(wins):
    return [(w, 4) for w in range(wins - 4, -1, -4)]


def body(
    rows_n, cols_n, rows_total, out_scale,
    tok_in, grad_in, reg_in, gain_in, offset_in, qkvw_in, qkvb_in, projw_in, table_in,
    d_tok, d_qkvw, d_qkvb, d_projw, d_table, d_gain, d_offset,
    both, spread_t, both_b, both_r, both_d, reg_b, reg_r,
    unit, inv_std, gradf, nt_s, q_s, k_s, v_s, da_s, gb_s, att, dq_s, dk_s, dv_s,
    w_s, b_s, pw_s, e_s, pick_s, bias_t, span_a, span_b, hmask, lab_col, lab_row, score_acc, sums,
    scores_s, dp_s, p_s, ds_s, grads, turned,
    fold_a, fold_b, frame_low, frame_two, back_u, back_l, back_ul,
    pack, pack_low, pair_in, half_low, part_in, result,
    tok_t, grad_t, reg, gain_ref, offset_ref, qkvw, qkvb, projw, table, local_sem,
    halo_send, halo_recv, back_send, back_recv, pair_sem,
    part_send, part_recv, all_send, all_recv, fwd_send, fwd_recv,
):
    row = lax.axis_index("row")
    col = lax.axis_index("col")
    up = lax.rem(row + rows_n - 1, rows_n)
    down = lax.rem(row + 1, rows_n)
    other = lax.rem(col + 1, cols_n)
    tile_cols = tok_in.shape[2]
    wins = tile_cols // WIN
    count = wins * SPAN
    half = rows_total // 2
    chunk = half // rows_n

    def remote(src, dst, send, recv, to_row, to_col):
        return pltpu.make_async_remote_copy(
            src_ref=src, dst_ref=dst, send_sem=send, recv_sem=recv,
            device_id={"row": to_row, "col": to_col}, device_id_type=MESH,
        )

    locals_ = [
        pltpu.make_async_copy(src, dst, local_sem.at[i])
        for i, (src, dst) in enumerate((
            (tok_in, tok_t), (grad_in, grad_t), (reg_in, reg),
            (table_in, table), (gain_in, gain_ref), (offset_in, offset_ref),
            (qkvw_in, qkvw), (qkvb_in, qkvb), (projw_in, projw),
        ))
    ]
    for copy in locals_:
        copy.start()
    barrier = pltpu.get_barrier_semaphore()

    @pl.loop(1, rows_n)
    def _(k):
        pl.semaphore_signal(
            barrier, inc=1, device_id={"row": lax.rem(row + k, rows_n), "col": col},
            device_id_type=MESH,
        )

    for to_row in (row, up, down):
        pl.semaphore_signal(
            barrier, inc=1, device_id={"row": to_row, "col": other}, device_id_type=MESH
        )
    def turn(r):
        both[r] = spread_t[pl.ds(r, 2 * C, stride=WIN), :].T.astype(BF16)

    for copy in locals_[0:3]:
        copy.wait()
    spread_t[0 : C * WIN, :] = tok_t[...].astype(F32).reshape(C * WIN, tile_cols)
    spread_t[C * WIN : 2 * C * WIN, :] = grad_t[...].astype(F32).reshape(C * WIN, tile_cols)
    for r in range(SHIFT, WIN):
        turn(r)
    pl.semaphore_wait(barrier, rows_n + 2)

    plan = window_steps(wins)
    steps = len(plan)

    def halo(i, src, dst, to_row, to_col):
        return remote(src, dst, halo_send.at[i], halo_recv.at[i], to_row, to_col)

    labels = [halo(0, reg, reg_b, down, col), halo(1, reg, reg_r, row, other)]
    sides = [
        halo(2, both.at[0:SHIFT, 0:EDGE], both_r, row, other),
    ]
    corner = halo(3, both.at[SHIFT:WIN, 0:EDGE], both_b.at[0:SHIFT, 0:EDGE], down, col)
    corner_on = halo(4, both_b.at[0:SHIFT, 0:EDGE], both_d, row, other)
    chunks = []
    for b, (w0, n) in enumerate(plan):
        cols = slice(max(w0 * WIN, EDGE), (w0 + n) * WIN)
        chunks.append([halo(5 + b, both.at[SHIFT:WIN, cols], both_b.at[0:SHIFT, cols], down, col)])
    ahead = 3
    small = 6 * BLOCK
    for copy in labels + [corner] + sum(chunks[:ahead], []):
        copy.start()
    for r in range(SHIFT):
        turn(r)
    for copy in sides:
        copy.start()

    for copy in locals_[3:]:
        copy.wait()
    flat = exact(table[...], table_spread(table.shape[1]))
    for rj in range(WIN):
        span_b[pl.ds(rj, HEADS, stride=WIN), :] = exact(flat, row_spread(rj), NT)
    for cj in range(WIN):
        span_a[pl.ds(cj, HEADS * WIN, stride=WIN), :] = exact(span_b[...], col_spread(cj), NT)
    for h in range(HEADS):
        bias_t[:, h * SPAN : (h + 1) * SPAN] = span_a[h * SPAN : (h + 1) * SPAN, :]
    mask_row = iota((4 * 16, LANE), 0) >> 4
    hmask[...] = ((iota((4 * 16, LANE), 1) >> 5) == mask_row).astype(F32).astype(BF16)
    e_s[...] = head_spread()
    pick_s[...] = part_pick()
    score_acc[...] = jnp.zeros_like(score_acc)
    sums[...] = jnp.zeros_like(sums)
    pack[small:] = jnp.zeros_like(pack[small:])

    nt_s[...] = jnp.ones_like(nt_s)
    for cj in range(WIN):
        fold_a[cj * SPAN : (cj + 1) * SPAN, :] = col_spread(cj).astype(BF16)
    for rj in range(WIN):
        fold_b[rj * 128 : (rj + 1) * 128, :] = row_spread(rj).astype(BF16)
    weights = qkvw[...]
    offsets = qkvb[...].reshape(1, 3 * C)
    for i in range(3):
        w_s[i] = mul(weights[:, i * C : (i + 1) * C], e_s[...]).astype(BF16)
        b_s[i] = exact(offsets[:, i * C : (i + 1) * C], e_s[...].astype(F32))
    pw_s[...] = mul(e_s[...], projw[...], TN).astype(BF16)

    for copy in labels:
        copy.wait()

    own = reg[...]
    row_part = jnp.concatenate([reg_b[SHIFT:, :], own[0:SHIFT]], 0)[:, 0:1] >> 2
    col_own = pltpu.roll(own, tile_cols - SHIFT, 1)
    col_right = pltpu.roll(reg_r[...], tile_cols - SHIFT, 1)
    col_part = jnp.where(iota((WIN, tile_cols), 1) < tile_cols - SHIFT, col_own, col_right)[0:1] & 3
    label = (row_part * 4 + col_part).astype(F32)
    spread = jnp.broadcast_to(label[:, None, :], (WIN, WIN, tile_cols)).reshape(SPAN, tile_cols)
    spread = jnp.where(
        (iota((SPAN, tile_cols), 0) & 7) == (iota((SPAN, tile_cols), 1) & 7), spread, 0.0
    )
    pick = ((iota((tile_cols, wins), 0) >> 3) == iota((tile_cols, wins), 1)).astype(F32)
    columns = exact(spread, pick)
    tiled = (iota((SPAN, LANE), 0) == (iota((SPAN, LANE), 1) & (SPAN - 1))).astype(F32)
    lab_row[...] = exact(columns, tiled, TN)
    for w in range(wins):
        lab_col[w] = jnp.broadcast_to(columns[:, w : w + 1], (SPAN, 128))

    lane = iota((SPAN, LANE), 1)

    def gather_heads(stacked):
        out = stacked[-SPAN:]
        for h in range(stacked.shape[0] // SPAN - 2, -1, -1):
            out = jnp.where(lane < (h + 1) * HEADW, stacked[h * SPAN : (h + 1) * SPAN], out)
        return out

    def diagonal(x, heads):
        tiles = x.reshape(SPAN // 16, 16, LANE)
        parts = [
            (tiles * hmask[h * 16 : (h + 1) * 16, :][None]).reshape(SPAN, LANE) for h in range(heads)
        ]
        return jnp.concatenate(parts, 0)

    groups = ((slice(0, LANE), slice(0, 4 * SPAN), 4), (slice(LANE, WIDE), slice(4 * SPAN, LANES), 2))

    def score_step(w0, n):
        for w in range(w0, w0 + n):
            at = slice(w * SPAN, (w + 1) * SPAN)
            for lanes, cut, heads in groups:
                scores_s[w, :, cut] = mul(k_s[at, lanes], diagonal(q_s[at, lanes], heads), NT)
                dp_s[w, :, cut] = mul(v_s[at, lanes], diagonal(da_s[at, lanes], heads), NT)

    def softmax_step(w0, n):
        for w in range(w0, w0 + n):
            same = lab_col[w] == lab_row[w : w + 1, :]
            for t in range(HEADS // 2):
                cut = slice(t * LANE, (t + 1) * LANE)
                scores = jnp.where(same, scores_s[w, :, cut] + bias_t[:, cut], MASKED)
                e = jnp.exp(scores - jnp.max(scores, 0, keepdims=True))
                p = e * (1.0 / jnp.sum(e, 0, keepdims=True))
                p_s[w, :, cut] = p.astype(BF16)
                dp = dp_s[w, :, cut]
                ds = p * (dp - jnp.sum(p * dp, 0, keepdims=True))
                score_acc[:, cut] += ds
                ds_s[w, :, cut] = ds.astype(BF16)

    def spread_step(w0, n):
        for w in range(w0, w0 + n):
            at = slice(w * SPAN, (w + 1) * SPAN)
            for lanes, cut, heads in groups:
                p, ds = p_s[w, :, cut], ds_s[w, :, cut]
                att[at, lanes] = gather_heads(mul(p, v_s[at, lanes], TN)).astype(BF16)
                dq = gather_heads(mul(ds, k_s[at, lanes], TN))
                dq_s[at, lanes] = (dq * HEAD ** (-0.5)).astype(BF16)
                dk_s[at, lanes] = mul(ds, diagonal(q_s[at, lanes], heads)).astype(BF16)
                dv_s[at, lanes] = mul(p, diagonal(da_s[at, lanes], heads)).astype(BF16)

    edge = tile_cols - EDGE
    backs = []

    def back(src, dst, to_row, to_col):
        i = len(backs)
        backs.append(remote(src, dst, back_send.at[i], back_recv.at[i], to_row, to_col))
        backs[-1].start()

    corner.wait()
    corner_on.start()
    waiting = []
    for b, (w0, step_wins) in enumerate(plan):
        for copy in chunks[b] + ([] if b else sides + [corner_on]):
            copy.wait()
        if b + ahead < steps:
            for copy in chunks[b + ahead]:
                copy.start()
        if b >= 2:
            for copy in waiting:
                back(*copy)
            waiting = []
        step, span_cols, end = step_wins * SPAN, step_wins * WIN, w0 + step_wins
        at = slice(w0 * SPAN, end * SPAN)
        win_at = slice(w0, end)
        cols = slice(w0 * WIN, end * WIN)
        near = slice(w0 * WIN, min(end * WIN + EDGE, tile_cols))

        for r in range(WIN):
            if r < SHIFT:
                part, beyond = both_b[r, near], both_d[r]
            else:
                part, beyond = both[r - SHIFT, near], both_r[r - SHIFT]
            wide = part.astype(F32)
            if end == wins:
                wide = jnp.concatenate([wide, beyond.astype(F32)], 0)
            wide = wide[SHIFT : SHIFT + span_cols]
            unit[win_at, r] = wide[:, 0:C].reshape(step_wins, WIN, C)
            gradf[win_at, r] = wide[:, C : 2 * C].reshape(step_wins, WIN, C)

        x = unit[win_at].reshape(step, C)
        center = jnp.mean(x, -1, keepdims=True)
        x = x - center
        inv = lax.rsqrt(jnp.mean(x * x, -1, keepdims=True) + 1e-05)
        x = x * inv
        unit[win_at] = x.reshape(step_wins, WIN, WIN, C)
        inv_std[at] = inv
        n = (x * gain_ref[...] + offset_ref[...]).astype(BF16)
        nt_s[0:C, at] = n.T
        q_s[at] = ((mul(n, w_s[0]) + b_s[0]) * HEAD ** (-0.5)).astype(BF16)
        k_s[at] = (mul(n, w_s[1]) + b_s[1]).astype(BF16)
        v_s[at] = (mul(n, w_s[2]) + b_s[2]).astype(BF16)
        g = gradf[win_at].reshape(step, C).astype(BF16)
        gb_s[at] = g
        da_s[at] = mul(g, pw_s[...], NT).astype(BF16)

        score_step(w0, 2)
        for w in range(w0, end, 2):
            softmax_step(w, 2)
            if w + 2 < end:
                score_step(w + 2, 2)
            spread_step(w, 2)

        x = unit[win_at].reshape(step, C)
        dn = mul(dq_s[at], w_s[0], NT) + mul(dk_s[at], w_s[1], NT) + mul(dv_s[at], w_s[2], NT)
        sums[0:1, 0:C] += jnp.sum(dn * x, 0, keepdims=True)
        sums[1:2, 0:C] += jnp.sum(dn, 0, keepdims=True)
        g = dn * gain_ref[...]
        dx = inv_std[at] * (
            g - jnp.mean(g, -1, keepdims=True) - x * jnp.mean(g * x, -1, keepdims=True)
        )
        out = (gradf[win_at].reshape(step, C) + dx).reshape(step_wins, WIN, WIN, C)
        for r in range(SHIFT):
            frame_low[r, cols] = out[:, SHIFT + r].reshape(span_cols, C).astype(BF16)
        for r in range(0, SHIFT, 2):
            two = [out[:, r + i].reshape(span_cols, C) for i in range(2)]
            frame_two[r // 2, cols] = jnp.concatenate(two, 1).astype(BF16)
        waiting.append((frame_two.at[0:2, cols], back_u.at[0:2, cols], up, col))
        if b == 0:
            waiting.append((frame_low.at[0:SHIFT, edge:tile_cols], back_l, row, other))
            waiting.append((frame_two.at[0:2, edge:tile_cols], back_ul, up, other))
        if w0 != 2:
            over = slice(w0 * SPAN, w0 * SPAN + 4 * SPAN)
            for i, part in enumerate((dq_s, dk_s, dv_s)):
                product = mul(nt_s[:, over], part[over])
                grads[i] = product if b == 0 else grads[i] + product
            product = mul(gb_s[over], att[over], TN)
            grads[3, 0:C] = product if b == 0 else grads[3, 0:C] + product
    for copy in waiting:
        back(*copy)

    for i in range(3):
        pack[i * BLOCK : (i + 1) * BLOCK, :] = grads[i, :, 0:LANE]
    pack[3 * BLOCK : 3 * BLOCK + C, :] = grads[3, 0:C, 0:LANE]
    pack[3 * BLOCK + C : 4 * BLOCK, :] = jnp.zeros((BLOCK - C, LANE), F32)
    pack[4 * BLOCK : 5 * BLOCK, :] = grads[0, :, LANE:WIDE] + pltpu.roll(grads[1, :, LANE:WIDE], 64, 1)
    pack[5 * BLOCK : 6 * BLOCK, :] = grads[2, :, LANE:WIDE]
    pack[5 * BLOCK : 5 * BLOCK + C, :] += pltpu.roll(grads[3, 0:C, LANE:WIDE], 64, 1)
    for h in range(HEADS):
        span_a[h * SPAN : (h + 1) * SPAN, :] = score_acc[:, h * SPAN : (h + 1) * SPAN]
    wide = jnp.concatenate(
        [span_a[pl.ds(cj, HEADS * WIN, stride=WIN), :] for cj in range(WIN)], 1
    )
    span_b[...] = split_mul(wide, fold_a[...])
    wide = jnp.concatenate(
        [span_b[pl.ds(rj, HEADS, stride=WIN), :] for rj in range(WIN)], 1
    )
    flat_sum = split_mul(wide, fold_b[...])
    sums[8 : 8 + HEADS, :] = flat_sum
    pack[small : small + 16, :] = sums[:, 0:LANE]
    pack[small + 16 : small + 32, :] = sums[:, LANE:WIDE]
    pack_low[...] = pack[...].astype(BF16)

    pair = remote(
        pack_low.at[pl.ds(pl.multiple_of(other * half, 16), half)], pair_in,
        pair_sem.at[0], pair_sem.at[1], row, other,
    )
    pair.start()
    pair.wait()
    mine = pl.ds(pl.multiple_of(col * half, 16), half)
    half_low[...] = (pack[mine] + pair_in[...].astype(F32)).astype(BF16)

    def part_copy(k):
        peer = lax.rem(row + k, rows_n)
        return remote(
            half_low.at[pl.ds(pl.multiple_of(peer * chunk, 16), chunk)], part_in.at[k],
            part_send.at[k], part_recv.at[k], peer, col,
        )

    @pl.loop(1, rows_n)
    def _(k):
        part_copy(k).start()

    def add_part(k, total):
        part_copy(k).wait()
        return total + part_in[k].astype(F32)

    my_chunk = pl.ds(pl.multiple_of(row * chunk, 16), chunk)
    total = lax.fori_loop(1, rows_n, add_part, half_low[my_chunk].astype(F32))
    own_chunk = result.at[col, my_chunk]
    own_chunk[...] = total.astype(BF16)

    def all_copy(k):
        return remote(
            own_chunk, own_chunk, all_send.at[k], all_recv.at[k],
            lax.rem(row + k, rows_n), col,
        )

    def forward(k):
        source = lax.rem(row + rows_n - k, rows_n)
        piece = result.at[col, pl.ds(pl.multiple_of(source * chunk, 16), chunk)]
        return remote(piece, piece, fwd_send.at[k], fwd_recv.at[k], row, other)

    @pl.loop(1, rows_n)
    def _(k):
        all_copy(k).start()

    forward(0).start()

    for copy in backs:
        copy.wait()
    for r in range(WIN):
        if r < SHIFT:
            left_part, main_part = back_l[r], frame_low[r]
        else:
            lanes = slice((r % 2) * C, (r % 2 + 1) * C)
            left_part = back_ul[(r - SHIFT) // 2].astype(F32)[:, lanes]
            main_part = back_u[(r - SHIFT) // 2].astype(F32)[:, lanes]
        wide = jnp.concatenate([left_part.astype(F32), main_part.astype(F32)], 0)
        turned[pl.ds(r, C, stride=WIN), :] = wide[EDGE - SHIFT : EDGE - SHIFT + tile_cols].T
    d_tok[...] = turned[...].reshape(C, WIN, tile_cols).astype(BF16)


    @pl.loop(1, rows_n)
    def _(k):
        all_copy(k).wait()
        forward(k).start()

    @pl.loop(0, rows_n)
    def _(k):
        forward(k).wait()

    done = jnp.concatenate([result[0], result[1]], 0)
    blocks = [done[i * BLOCK : (i + 1) * BLOCK] for i in range(6)]
    joined = jnp.concatenate([blocks[i] for i in (0, 1, 2, 4, 5)], 1)
    product = mul(joined, pick_s[...]) * out_scale
    d_qkvw[...] = product[0:C]
    d_qkvb[...] = product[C : C + 1].reshape(3 * C)
    spread = e_s[...]
    far = pltpu.roll(spread[:, LANE:WIDE].astype(F32), 64, 1).astype(BF16)
    product = mul(spread[:, 0:LANE], blocks[3], NT) + mul(far, blocks[5], NT)
    d_projw[...] = product[:, 0:C] * out_scale
    tail = done[small : small + 32].astype(F32) * out_scale
    tail = jnp.concatenate([tail[0:16], tail[16:32]], 1)
    d_gain[...] = tail[0:1, 0:C]
    d_offset[...] = tail[1:2, 0:C]
    entries = table_spread(d_table.shape[1])
    d_table[...] = exact(tail[8 : 8 + HEADS, :], entries, NT)


def finish(*refs):
    sources, outs, held, sems = refs[0:7], refs[7:14], refs[14:21], refs[21]
    into = [pltpu.make_async_copy(sources[i], held[i], sems.at[0, i]) for i in range(7)]
    away = [pltpu.make_async_copy(held[i], outs[i], sems.at[1, i]) for i in range(7)]
    for copy in into:
        copy.start()
    for first, second in zip(into, away):
        first.wait()
        second.start()
    for copy in away:
        copy.wait()


def on_device(
    tokens, grad_out, regions, ln_gain, ln_offset, qkv_weight, qkv_bias, proj_weight, bias_table
):
    rows_n, cols_n = lax.axis_size("row"), lax.axis_size("col")
    tile_cols = tokens.shape[1]
    wins = tile_cols // WIN
    count = wins * SPAN
    steps = len(window_steps(wins))
    unit_rows = 2 * 16 * rows_n
    needed = 6 * BLOCK + 32
    rows_total = -(-needed // unit_rows) * unit_rows
    half = rows_total // 2
    chunk = half // rows_n
    total_tokens = tokens.shape[0] * tile_cols * rows_n * cols_n
    vmem = pltpu.VMEM
    halo = [
        vmem((SHIFT, tile_cols, 2 * C), BF16),
        vmem((SHIFT, EDGE, 2 * C), BF16),
        vmem((SHIFT, EDGE, 2 * C), BF16),
    ]
    home = [
        vmem((SHIFT, tile_cols, C), BF16),
        vmem((2, tile_cols, 2 * C), BF16),
        vmem((2, tile_cols, 2 * C), BF16),
        vmem((SHIFT, EDGE, C), BF16),
        vmem((2, EDGE, 2 * C), BF16),
    ]
    flat_low = vmem((count, WIDE), BF16)
    whole = pl.BlockSpec(memory_space=pltpu.VMEM)
    dma = pltpu.SemaphoreType.DMA
    outs = pl.pallas_call(
        functools.partial(body, rows_n, cols_n, rows_total, total_tokens ** (-0.5)),
        out_shape=(
            jax.ShapeDtypeStruct((C,) + tokens.shape[:2], BF16),
            jax.ShapeDtypeStruct((C, 3 * C), F32),
            jax.ShapeDtypeStruct((3 * C,), F32),
            jax.ShapeDtypeStruct((C, C), F32),
            jax.ShapeDtypeStruct((HEADS, bias_table.shape[0]), F32),
            jax.ShapeDtypeStruct((1, C), F32),
            jax.ShapeDtypeStruct((1, C), F32),
        ),
        in_specs=[pl.BlockSpec(memory_space=pl.ANY)] * 9,
        out_specs=(whole,) * 7,
        scratch_shapes=[
            vmem((WIN, tile_cols, 2 * C), BF16),
            vmem((2 * C * WIN, tile_cols), F32),
        ] + halo + [
            vmem(regions.shape, jnp.int32),
            vmem(regions.shape, jnp.int32),
            vmem((wins, WIN, WIN, C), F32),
            vmem((count, 1), F32),
            vmem((wins, WIN, WIN, C), F32),
            vmem((192, count), BF16),
        ] + [flat_low] * 4 + [vmem((count, C), BF16)] + [flat_low] * 4 + [
            vmem((3, C, WIDE), BF16),
            vmem((3, 1, WIDE), F32),
            vmem((WIDE, C), BF16),
            vmem((C, WIDE), BF16),
            vmem((5 * LANE, 3 * C), BF16),
            vmem((SPAN, LANES), F32),
            vmem((HEADS * SPAN, SPAN), F32),
            vmem((HEADS * WIN, 128), F32),
            vmem((4 * 16, LANE), BF16),
            vmem((wins, SPAN, 128), F32),
            vmem((wins, LANE), F32),
            vmem((SPAN, LANES), F32),
            vmem((16, WIDE), F32),
            vmem((wins, SPAN, LANES), F32),
            vmem((wins, SPAN, LANES), F32),
            vmem((wins, SPAN, LANES), BF16),
            vmem((wins, SPAN, LANES), BF16),
            vmem((4, BLOCK, WIDE), F32),
            vmem((C * WIN, tile_cols), F32),
            vmem((WIN * SPAN, 128), BF16),
            vmem((WIN * 128, 256), BF16),
        ] + home + [
            vmem((rows_total, LANE), F32),
            vmem((rows_total, LANE), BF16),
            vmem((half, LANE), BF16),
            vmem((half, LANE), BF16),
            vmem((rows_n, chunk, LANE), BF16),
            vmem((2, half, LANE), BF16),
            vmem((C,) + tokens.shape[:2], BF16), vmem((C,) + tokens.shape[:2], BF16),
            vmem(regions.shape, jnp.int32),
            vmem((1, C), F32), vmem((1, C), F32), vmem(qkv_weight.shape, BF16), vmem((3 * C,), F32),
            vmem(proj_weight.shape, BF16), vmem(bias_table.shape[::-1], F32), dma((9,)),
            dma((5 + steps,)), dma((5 + steps,)),
            dma((steps + 2,)), dma((steps + 2,)), dma((2,)),
            dma((rows_n,)), dma((rows_n,)), dma((rows_n,)), dma((rows_n,)),
            dma((rows_n,)), dma((rows_n,)),
        ],
        compiler_params=pltpu.CompilerParams(
            collective_id=0, has_side_effects=True, vmem_limit_bytes=61 * 1024 * 1024
        ),
    )(
        jnp.transpose(tokens, (2, 0, 1)), jnp.transpose(grad_out, (2, 0, 1)), regions, ln_gain.reshape(1, C), ln_offset.reshape(1, C), qkv_weight,
        qkv_bias, proj_weight, bias_table.T,
    )
    anywhere = pl.BlockSpec(memory_space=pl.ANY)
    d_tokens, d_qkvw, d_qkvb, d_projw, d_table, d_gain, d_offset = pl.pallas_call(
        finish,
        out_shape=[jax.ShapeDtypeStruct(x.shape, x.dtype) for x in outs],
        in_specs=[anywhere] * 7,
        out_specs=[anywhere] * 7,
        scratch_shapes=[vmem(x.shape, x.dtype) for x in outs] + [dma((2, 7))],
        compiler_params=pltpu.CompilerParams(vmem_limit_bytes=61 * 1024 * 1024),
    )(*outs)
    return (
        jnp.transpose(d_tokens, (1, 2, 0)),
        d_qkvw,
        d_qkvb,
        d_projw,
        d_table.T,
        d_gain.reshape(C),
        d_offset.reshape(C),
    )


def solution(mesh):
    placed = (
        P(("grp", "row"), "col", None),
        P(("grp", "row"), "col", None),
        P(("grp", "row"), "col"),
        P(),
        P(),
        P(),
        P(),
        P(),
        P(),
    )
    return jax.shard_map(
        on_device,
        mesh=mesh,
        in_specs=placed,
        out_specs=(
            P(("grp", "row"), "col", None),
            P("grp", None),
            P("grp"),
            P("grp", None),
            P("grp", None),
            P("grp"),
            P("grp"),
        ),
        check_vma=False,
    )
```
